32 devices in a mesh: dp: 8 (over z, x), head: 4 (over y, core).
Axes of the slice: x: 2, y: 2, z: 4, core: 2. Of those that a mesh axis runs over, the one named last changes fastest.
Arguments:
- tokens: bfloat16 [32768, 512], P(('dp', 'head')), may hold values from -6 to 6
- doc_ids: int32 [16, 2048], P('dp'), may hold values from 0 to 15, never falling along the last dimension, each value on 1 to 1024 neighbouring positions
- pad_mask: int32 [16, 2048], P('dp'), may hold values 0 or 1
- norm1_gain: bfloat16 [512], replicated, may hold values from 0.5 to 1.5
- norm1_shift: bfloat16 [512], replicated, may hold values from -4 to 4
- w_qkv: bfloat16 [3, 512, 512], P(None, None, 'head'), may hold values from -0.25 to 0.25
- w_out: bfloat16 [512, 512], P('head'), may hold values from -2 to 2
- norm2_gain: bfloat16 [512], replicated, may hold values from 0.5 to 1.5
- norm2_shift: bfloat16 [512], replicated, may hold values from -4 to 4
- w_hidden: bfloat16 [512, 2048], P(None, 'head'), may hold values from -0.25 to 0.25
- hidden_bias: bfloat16 [2048], P('head'), may hold values from -4 to 4
- w_return: bfloat16 [2048, 512], P('head'), may hold values from -0.25 to 0.25
- return_bias: bfloat16 [512], replicated, may hold values from -4 to 4
- out_grad: bfloat16 [32768, 512], P(('dp', 'head')), may hold values from -6 to 6
Outputs:
- output: bfloat16 [32768, 512], P(('dp', 'head'))
- tokens_grad: float32 [32768, 512], P(('dp', 'head'))
- norm1_gain_grad: float32 [512], replicated
- norm1_shift_grad: float32 [512], replicated
- w_qkv_grad: float32 [3, 512, 512], P(None, None, 'head')
- w_out_grad: float32 [512, 512], P('head')
- norm2_gain_grad: float32 [512], replicated
- norm2_shift_grad: float32 [512], replicated
- w_hidden_grad: float32 [512, 2048], P(None, 'head')
- hidden_bias_grad: float32 [2048], P('head')
- w_return_grad: float32 [2048, 512], P('head')
- return_bias_grad: float32 [512], replicated
The draws below stay inside these ranges and needn't reach their ends.
Inputs may be any that keep to these rules, and one draw needn't show every extreme that they name: `doc_ids`: along each row the document numbers never fall; each number from 0 up covers 1 to 1024 consecutive positions of the row.
All inputs are finite; a program needn't handle non-finite values. No bound on the sum of `pad_mask` on one device may be relied on, other than what follows from the above.
Results may differ from the reference program's by a relative error of at most 0.012.
Values may be sent and summed in bfloat16 or wider, within the bound.
No kernel may reach another device: no remote copies, remote signals or barrier semaphores. Data moves between devices by JAX's collectives and lax.ppermute only.
A program may use at most 192 MiB of HBM per device.

```python
import math
import jax
import jax.numpy as jnp
import numpy as np
from jax import lax

D = 512
HEADS = 8
HEAD_DIM = 64
FF = 2048
LEN = 2048
SPAN = 512
ROWS = 16
TOKENS = 32768


def with_ends(entries, rng, least, largest):
    longest = entries.shape.index(max(entries.shape))
    spots = []
    for shift in (0, 1):
        where = [jax.random.randint(jax.random.fold_in(rng, axis), (), 0, length) for axis, length in enumerate(entries.shape)]
        where[longest] = (where[longest] + shift) % entries.shape[longest]
        spots.append(tuple(where))
    return entries.at[spots[0]].set(least).at[spots[1]].set(largest)


def levels(stream_key, dims, cuts, smallest, largest):
    level = 1.0
    for dim, blocks in cuts:
        draws = jax.random.uniform(jax.random.fold_in(jax.random.fold_in(stream_key, 6), dim), (blocks,), jnp.float32, smallest / len(cuts), largest / len(cuts))
        level = level * jnp.repeat(jnp.exp(draws), dims[dim] // blocks).reshape((-1,) + (1,) * (len(dims) - 1 - dim))
    return level


def split_up(count, total, bound, skew):
    portions = [(1 << 20) // math.isqrt(rank ** skew) + 1 for rank in range(2, count + 1)]
    surplus, given = total - bound - (count - 1), [1] * (count - 1)
    while surplus > 0:
        candidates = [i for i in range(count - 1) if given[i] < bound]
        pool, remaining = sum([portions[i] for i in candidates]), surplus
        for i in candidates:
            extra = min(bound - given[i], max(1, remaining * portions[i] // pool), surplus)
            given[i] = given[i] + extra
            surplus = surplus - extra
    return np.array([bound] + given)


def uneven(stream_key, number_of, total, most, lean):
    if number_of == 2:
        one = jax.random.randint(stream_key, (), max(1, total - most), min(most, total - 1) + 1)
        return jnp.stack([one, total - one])
    tallies = jnp.asarray(split_up(number_of, total, most, lean), jnp.int32)
    pairs = (number_of - 1) // 2
    giver, receiver = tallies[1:1 + 2 * pairs:2], tallies[2:2 + 2 * pairs:2]
    slack = jnp.minimum(giver - 1, most - receiver)
    passed = jax.random.randint(jax.random.fold_in(stream_key, 1), (pairs,), 0, 1 << 20) % (slack + 1)
    tallies = tallies.at[1:1 + 2 * pairs:2].set(giver - passed).at[2:2 + 2 * pairs:2].set(receiver + passed)
    return tallies[jax.random.permutation(jax.random.fold_in(stream_key, 2), number_of)]


def scatter_about(stream_key, shape, scale, reach, cuts=(), held_as=jnp.bfloat16):
    loudness = levels(stream_key, shape, cuts, -0.22, 0.18) if cuts else 1.0
    entries = jax.random.normal(stream_key, shape, jnp.float32) * scale * loudness
    return jnp.minimum(jnp.maximum(entries, -reach), reach).astype(held_as)


def setup_inputs(seed: int = 0) -> dict:
    splits = jax.random.split(jax.random.key(seed), 15)
    tokens = scatter_about(splits[0], (TOKENS, D), 1.0, 6.0, ((0, 32),))
    doc_ids = jax.vmap(lambda own: jnp.searchsorted(jnp.cumsum(uneven(own, max(4, LEN // 128), LEN, LEN // 2, 2)), jnp.arange(LEN), side="right"))(jax.random.split(splits[1], ROWS)).reshape((ROWS, LEN)).astype(jnp.int32)
    pad_mask = with_ends((jax.random.randint(splits[2], (ROWS, LEN), 0, 8) < 7).astype(jnp.int32), jax.random.fold_in(splits[2], 1), 0, 1)
    norm1_gain = jnp.clip(1.0 + 0.1 * jax.random.normal(splits[3], (D,), jnp.float32), 0.5, 1.5).astype(jnp.bfloat16)
    norm1_shift = scatter_about(splits[4], (D,), 0.3, 4.0)
    w_qkv = scatter_about(splits[5], (3, D, D), D ** -0.5, 0.25, ((2, 4),))
    w_out = scatter_about(splits[6], (D, D), (D // 64) ** -0.5, 2.0, ((0, 4),))
    norm2_gain = jnp.clip(1.0 + 0.1 * jax.random.normal(splits[7], (D,), jnp.float32), 0.5, 1.5).astype(jnp.bfloat16)
    norm2_shift = scatter_about(splits[8], (D,), 0.3, 4.0)
    w_hidden = scatter_about(splits[9], (D, FF), D ** -0.5, 0.25, ((1, 4),))
    hidden_bias = scatter_about(splits[10], (FF,), 0.3, 4.0, ((0, 4),))
    w_return = scatter_about(splits[11], (FF, D), (FF // 4) ** -0.5, 0.25, ((0, 4),))
    return_bias = scatter_about(splits[12], (D,), 0.3, 4.0)
    out_grad = scatter_about(splits[13], (TOKENS, D), 1.0, 6.0, ((0, 32),))
    return dict(tokens=tokens, doc_ids=doc_ids, pad_mask=pad_mask, norm1_gain=norm1_gain, norm1_shift=norm1_shift, w_qkv=w_qkv, w_out=w_out, norm2_gain=norm2_gain, norm2_shift=norm2_shift, w_hidden=w_hidden, hidden_bias=hidden_bias, w_return=w_return, return_bias=return_bias, out_grad=out_grad)


highest = lax.Precision.HIGHEST
epsilon = 1e-05

@jax.custom_vjp
def low(v):
    return lax.optimization_barrier(v.astype(jnp.bfloat16)).astype(jnp.float32)

@jax.custom_vjp
def low_back(v):
    return v

def low_keep(v):
    return (low(v), None)

def low_pass(kept, grad):
    return (grad,)

def back_keep(v):
    return (v, None)

def back_low(kept, grad):
    return (low(grad),)
low.defvjp(low_keep, low_pass)
low_back.defvjp(back_keep, back_low)

def layer_norm(values, norm_gain, norm_shift):
    centre = values - lax.optimization_barrier(jnp.mean(values, axis=-1, keepdims=True))
    spread = lax.optimization_barrier(jnp.mean(centre * centre, axis=-1, keepdims=True))
    return centre * lax.rsqrt(spread + epsilon) * norm_gain + norm_shift

def feature(values):
    return jax.nn.elu(values) + 1.0

def span_step(running, pieces):
    memory, key_total = running
    queries, keys_feat, values, segment, previous = pieces
    length = segment.shape[0]
    causal = lax.broadcasted_iota(jnp.int32, (length, length), 0) >= lax.broadcasted_iota(jnp.int32, (length, length), 1)
    allowed = ((segment[:, None] == segment[None, :]) & causal).astype(jnp.float32)
    reads_state = (segment == previous).astype(jnp.float32)
    in_last = (segment == segment[-1]).astype(jnp.float32)
    carried = (segment[-1] == previous).astype(jnp.float32)
    scores = low_back(jnp.einsum('the,she->hts', queries, keys_feat, precision=highest) * allowed[None])
    totals = lax.optimization_barrier(jnp.sum(scores, axis=-1)).T + reads_state[:, None] * lax.optimization_barrier(jnp.sum(queries * key_total[None], axis=-1))
    weighted = jnp.einsum('hts,shf->thf', low(scores), values, precision=highest)
    weighted = weighted + reads_state[:, None, None] * jnp.einsum('the,hef->thf', queries, low(memory), precision=highest)
    chosen = keys_feat * in_last[:, None, None]
    increment = low_back(jnp.einsum('she,shf->hef', chosen, values, precision=highest))
    new_memory = carried * memory + increment
    new_total = carried * key_total + lax.optimization_barrier(jnp.sum(chosen, axis=0))
    return ((new_memory, new_total), (low_back(weighted), totals))

def row_layer(params, row_tokens, row_docs, row_live):
    norm1_gain, norm1_shift, w_qkv, w_out, norm2_gain, norm2_shift, w_hidden, hidden_bias, w_return, return_bias = params
    normed1 = low(layer_norm(row_tokens, norm1_gain, norm1_shift))
    projected = jnp.einsum('td,pde->pte', normed1, w_qkv, precision=highest)
    queries = low(feature(low_back(projected[0])))
    keys_feat = low(feature(low_back(projected[1])) * row_live[:, None])
    values = low(low_back(projected[2]))
    spans = LEN // SPAN
    shape = (spans, SPAN, HEADS, HEAD_DIM)
    doc_blocks = row_docs.reshape(spans, SPAN).astype(jnp.int32)
    previous = jnp.concatenate([jnp.full((1,), -1, jnp.int32), doc_blocks[:-1, -1].astype(jnp.int32)])
    start = (jnp.zeros((HEADS, HEAD_DIM, HEAD_DIM), jnp.float32), jnp.zeros((HEADS, HEAD_DIM), jnp.float32))
    ignored, (weighted, totals) = lax.scan(jax.checkpoint(span_step), start, (queries.reshape(shape), keys_feat.reshape(shape), values.reshape(shape), doc_blocks, previous))
    live_blocks = row_live.reshape(spans, SPAN, 1, 1)
    mixed = low((weighted / jnp.maximum(totals, 1.0)[..., None] * live_blocks).reshape(LEN, D))
    attended = low_back(jnp.dot(mixed, w_out, precision=highest))
    residual = row_tokens + attended
    normed2 = low(layer_norm(residual, norm2_gain, norm2_shift))
    hidden_pre = low_back(jnp.dot(normed2, w_hidden, precision=highest) + hidden_bias)
    activated = low(jax.nn.gelu(hidden_pre, approximate=False))
    branch = low_back(jnp.dot(activated, w_return, precision=highest) + return_bias)
    return residual + branch

def reference(tokens, doc_ids, pad_mask, norm1_gain, norm1_shift, w_qkv, w_out, norm2_gain, norm2_shift, w_hidden, hidden_bias, w_return, return_bias, out_grad):
    params = tuple((item.astype(jnp.float32) for item in (norm1_gain, norm1_shift, w_qkv, w_out, norm2_gain, norm2_shift, w_hidden, hidden_bias, w_return, return_bias)))
    inputs = tokens.astype(jnp.float32).reshape(ROWS, LEN, D)
    live = pad_mask.astype(jnp.float32)

    def forward(inputs, params):

        def one_row(row_data):
            return jax.checkpoint(row_layer)(params, row_data[0], row_data[1], row_data[2])
        return lax.map(one_row, (inputs, doc_ids, live))
    result, pullback = jax.vjp(forward, inputs, params)
    inputs_grad, grads = pullback(out_grad.astype(jnp.float32).reshape(ROWS, LEN, D))
    return (result.reshape(TOKENS, D).astype(jnp.bfloat16), inputs_grad.reshape(TOKENS, D), grads[0], grads[1], grads[2], grads[3], grads[4], grads[5], grads[6], grads[7], grads[8], grads[9])
```

```python
import functools

import jax
import jax.numpy as jnp
from jax import lax
from jax.experimental import pallas as pl
from jax.experimental.pallas import tpu as pltpu
from jax.sharding import PartitionSpec as P

HEAD_DIM = 64
PAIR = 2 * HEAD_DIM
CHUNK = 256
EPSILON = 1e-05
F32 = jnp.float32
BF16 = jnp.bfloat16
VMEM_BYTES = 60 * 1024 * 1024

DOC, LIVE, READ_HALF, READ_CHUNK, IN_LAST, CARRIED, FIRST_HALF = range(7)


def nn(a, b):
    return lax.dot_general(a, b, (((1,), (0,)), ((), ())), preferred_element_type=F32)


def nt(a, b):
    return lax.dot_general(a, b, (((1,), (1,)), ((), ())), preferred_element_type=F32)


def tn(a, b):
    return lax.dot_general(a, b, (((0,), (0,)), ((), ())), preferred_element_type=F32)


def normalise(x):
    centre = x - jnp.mean(x, axis=-1, keepdims=True)
    rstd = lax.rsqrt(jnp.mean(centre * centre, axis=-1, keepdims=True) + EPSILON)
    return centre * rstd, rstd


def head_lanes(shape):
    return lax.broadcasted_iota(jnp.int32, shape, len(shape) - 1) % PAIR < HEAD_DIM


def pair_mask(width):
    rows = lax.broadcasted_iota(jnp.int32, (PAIR, width), 0) < HEAD_DIM
    return rows == head_lanes((PAIR, width))


def allowed_mask(doc_col, doc_row):
    t = lax.broadcasted_iota(jnp.int32, (CHUNK, CHUNK), 0)
    s = lax.broadcasted_iota(jnp.int32, (CHUNK, CHUNK), 1)
    return (doc_col == doc_row) & (s <= t)


def feature(x):
    return jnp.where(x > 0, x + 1.0, jnp.exp(jnp.minimum(x, 0.0)))


def attend_kernel(blocks, first, *refs):
    refs = list(refs)
    take = refs.pop
    src = take(0)
    if first:
        gain, shift = take(0), take(0)
    w = [take(0) for _ in range(blocks)]
    cols, doc_row = take(0), take(0)
    if first:
        n1_out = take(0)
    q_out, k_out, v_out, num_out, tot_out, state_out, last_out, w_all, state = refs
    step = pl.program_id(0)

    @pl.when(step == 0)
    def _():
        for p in range(3):
            for b in range(blocks):
                w_all[p, :, b * PAIR : (b + 1) * PAIR] = w[b][p]
        state[...] = jnp.zeros_like(state)

    if first:
        xhat, _ = normalise(src[...].astype(F32))
        n1 = (xhat * gain[...].astype(F32) + shift[...].astype(F32)).astype(BF16)
        n1_out[...] = n1
    else:
        n1 = src[...]
    live = cols[:, LIVE : LIVE + 1]
    reads = cols[:, READ_CHUNK : READ_CHUNK + 1]
    in_last = cols[:, IN_LAST : IN_LAST + 1].astype(BF16)
    carried = cols[0:1, CARRIED : CARRIED + 1]
    mask = allowed_mask(cols[:, DOC : DOC + 1], doc_row[...])
    q_all = feature(nn(n1, w_all[0])).astype(BF16)
    k_all = (feature(nn(n1, w_all[1])) * live).astype(BF16)
    v_all = nn(n1, w_all[2]).astype(BF16)
    here = head_lanes((CHUNK, PAIR))
    block_diagonal = pair_mask(2 * PAIR)
    ones = jnp.ones((CHUNK, PAIR), BF16)
    zeros = jnp.zeros((CHUNK, PAIR), BF16)
    for b in range(blocks):
        lanes = slice(b * PAIR, (b + 1) * PAIR)
        q, k, v = q_all[:, lanes], k_all[:, lanes], v_all[:, lanes]
        q_out[b], k_out[b], v_out[b] = q, k, v
        total = jnp.zeros((CHUNK, 2 * PAIR), F32)
        for own in (here, jnp.logical_not(here)):
            scores = nt(jnp.where(own, q, zeros), k)
            scores = jnp.where(mask, scores, 0.0).astype(BF16)
            wide = jnp.concatenate([jnp.where(own, v, zeros), jnp.where(own, ones, zeros)], axis=1)
            total = total + nn(scores, wide)
        low = state[b].astype(BF16)
        state_out[0, b] = low
        total = total + reads * nn(q, low)
        num_out[b] = total[:, :PAIR]
        tot_out[b] = total[:, PAIR:]
        grown = tn(k * in_last, jnp.concatenate([v, ones], axis=1))
        state[b] = carried * state[b] + jnp.where(block_diagonal, grown, 0.0)
        last_out[b ^ 1] = state[b].astype(BF16)


def attend(src, norm, w, cols, doc_row):
    tokens, width = src.shape
    blocks, chunks = len(w), tokens // CHUNK
    first = norm is not None
    whole = lambda shape: pl.BlockSpec(shape, lambda i: (0,) * len(shape))
    rows = lambda n: pl.BlockSpec((CHUNK, n), lambda i: (i, 0))
    part = lambda: pl.BlockSpec((blocks, CHUNK, PAIR), lambda i: (0, i, 0))
    in_specs = [rows(width)] + ([whole((1, width))] * 2 if first else [])
    in_specs += [whole((3, width, PAIR))] * blocks
    in_specs += [rows(8), pl.BlockSpec((1, CHUNK), lambda i: (0, i))]
    arrays = [src] + (list(norm) if first else []) + list(w) + [cols, doc_row]
    out_shape = [jax.ShapeDtypeStruct((tokens, width), BF16)] if first else []
    out_specs = [rows(width)] if first else []
    out_shape += [jax.ShapeDtypeStruct((blocks, tokens, PAIR), BF16)] * 3
    out_shape += [jax.ShapeDtypeStruct((blocks, tokens, PAIR), F32)] * 2
    out_shape += [jax.ShapeDtypeStruct((chunks, blocks, PAIR, 2 * PAIR), BF16)]
    out_shape += [jax.ShapeDtypeStruct((blocks, PAIR, 2 * PAIR), BF16)]
    out_specs += [part()] * 5
    out_specs += [pl.BlockSpec((1, blocks, PAIR, 2 * PAIR), lambda i: (i, 0, 0, 0))]
    out_specs += [whole((blocks, PAIR, 2 * PAIR))]
    return pl.pallas_call(
        functools.partial(attend_kernel, blocks, first),
        grid=(chunks,),
        in_specs=in_specs,
        out_specs=out_specs,
        out_shape=out_shape,
        scratch_shapes=[
            pltpu.VMEM((3, width, blocks * PAIR), BF16),
            pltpu.VMEM((blocks, PAIR, 2 * PAIR), F32),
        ],
        compiler_params=pltpu.CompilerParams(
            dimension_semantics=("arbitrary",), vmem_limit_bytes=VMEM_BYTES
        ),
        cost_estimate=pl.CostEstimate(
            flops=2 * tokens * blocks * PAIR * (3 * width + 4 * CHUNK),
            bytes_accessed=8 << 20,
            transcendentals=0,
        ),
        name="attend",
    )(*arrays)


def mix_kernel(groups, tok, *refs):
    refs = list(refs)
    q = [refs.pop(0) for _ in range(groups)]
    num = [refs.pop(0) for _ in range(groups)]
    tot = [refs.pop(0) for _ in range(groups)]
    come = [refs.pop(0) for _ in range(groups)]
    wo = [refs.pop(0) for _ in range(2 * groups)]
    cols, gain, shift, mixed_out, inv_out, residual_out, n2_out, w_all = refs

    @pl.when(pl.program_id(0) == 0)
    def _():
        for b in range(2 * groups):
            w_all[b * PAIR : (b + 1) * PAIR, :] = wo[b][:PAIR, :]

    live = cols[:, LIVE : LIVE + 1]
    reads = cols[:, READ_HALF : READ_HALF + 1]
    for b in range(2 * groups):
        g, i = divmod(b, 2)
        lanes = slice(b * PAIR, (b + 1) * PAIR)
        far = reads * nn(q[g][i], come[g][i])
        inv = 1.0 / jnp.maximum(tot[g][i] + far[:, PAIR:], 1.0)
        inv_out[:, lanes] = inv
        mixed_out[:, lanes] = ((num[g][i] + far[:, :PAIR]) * inv * live).astype(BF16)
    residual = tok[...].astype(F32) + nn(mixed_out[...], w_all[...])
    residual_out[...] = residual
    xhat, _ = normalise(residual)
    n2_out[...] = (xhat * gain[...].astype(F32) + shift[...].astype(F32)).astype(BF16)


def mix(tok, q, num, tot, come, wo, cols, gain, shift):
    tokens, width = tok.shape
    groups = len(q)
    whole = lambda shape: pl.BlockSpec(shape, lambda i: (0,) * len(shape))
    rows = lambda n: pl.BlockSpec((CHUNK, n), lambda i: (i, 0))
    part = pl.BlockSpec((2, CHUNK, PAIR), lambda i: (0, i, 0))
    return pl.pallas_call(
        functools.partial(mix_kernel, groups),
        grid=(tokens // CHUNK,),
        in_specs=[rows(width)]
        + [part] * (3 * groups)
        + [whole((2, PAIR, 2 * PAIR))] * groups
        + [whole(wo[0].shape)] * (2 * groups)
        + [rows(8), whole((1, width)), whole((1, width))],
        out_specs=[rows(width)] * 4,
        out_shape=[
            jax.ShapeDtypeStruct((tokens, width), BF16),
            jax.ShapeDtypeStruct((tokens, width), F32),
            jax.ShapeDtypeStruct((tokens, width), F32),
            jax.ShapeDtypeStruct((tokens, width), BF16),
        ],
        scratch_shapes=[pltpu.VMEM((width, width), BF16)],
        compiler_params=pltpu.CompilerParams(
            dimension_semantics=("arbitrary",), vmem_limit_bytes=VMEM_BYTES
        ),
        cost_estimate=pl.CostEstimate(
            flops=4 * tokens * width * width, bytes_accessed=12 << 20, transcendentals=0
        ),
        name="mix",
    )(tok, *q, *num, *tot, *come, *wo, cols, gain, shift)


def gelu_pair(x):
    cdf = 0.5 + 0.5 * lax.erf(x * 0.7071067811865476)
    density = 0.3989422804014327 * jnp.exp(-0.5 * x * x)
    return x * cdf, cdf + x * density


def feed_kernel(blocks, resume, n2, dy, *refs):
    refs = list(refs)
    wh = [refs.pop(0) for _ in range(blocks)]
    wr = [refs.pop(0) for _ in range(blocks)]
    wo = [refs.pop(0) for _ in range(blocks)]
    if resume:
        branch_in, dn2_in = refs.pop(0), refs.pop(0)
    branch, dn2 = refs.pop(0), refs.pop(0)
    gwh = [refs.pop(0) for _ in range(blocks)]
    gwr = [refs.pop(0) for _ in range(blocks)]
    ghb = [refs.pop(0) for _ in range(blocks)]
    act, hg = refs
    tokens, width = n2.shape
    for b in range(blocks):
        hidden = wh[b].shape[1]
        bias = wo[b][PAIR : PAIR + 1, :].astype(F32)
        bias_grad = jnp.zeros((8, hidden), F32)
        for i in range(tokens // CHUNK):
            rows = slice(i * CHUNK, (i + 1) * CHUNK)
            pre = nn(n2[rows, :], wh[b][...]) + bias
            value, slope = gelu_pair(pre)
            act[rows, :] = value.astype(BF16)
            grad = nt(dy[rows, :], wr[b][...]) * slope
            low = grad.astype(BF16)
            hg[rows, :] = low
            bias_grad = bias_grad + jnp.sum(grad.reshape(CHUNK // 8, 8, hidden), axis=0)
            out = nn(act[rows, :], wr[b][...])
            back = nt(low, wh[b][...])
            if b > 0:
                out = out + branch[rows, :]
                back = back + dn2[rows, :]
            elif resume:
                out = out + branch_in[rows, :]
                back = back + dn2_in[rows, :]
            branch[rows, :] = out
            dn2[rows, :] = back
        gwr[b][...] = tn(act[...], dy[...]).astype(BF16)
        gwh[b][...] = tn(n2[...], hg[...]).astype(BF16)
        ghb[b][...] = bias_grad


def feed(n2, dy, wh, wr, wo, partial):
    tokens, width = n2.shape
    blocks, hidden = len(wh), wh[0].shape[1]
    resume = partial is not None
    arrays = [n2, dy, *wh, *wr, *wo] + (list(partial) if resume else [])
    out_shape = [jax.ShapeDtypeStruct((tokens, width), F32)] * 2
    out_shape += [jax.ShapeDtypeStruct((width, hidden), BF16)] * blocks
    out_shape += [jax.ShapeDtypeStruct((hidden, width), BF16)] * blocks
    out_shape += [jax.ShapeDtypeStruct((8, hidden), F32)] * blocks
    vmem = pl.BlockSpec(memory_space=pltpu.VMEM)
    out = pl.pallas_call(
        functools.partial(feed_kernel, blocks, resume),
        in_specs=[vmem] * len(arrays),
        out_specs=[vmem] * len(out_shape),
        out_shape=out_shape,
        scratch_shapes=[pltpu.VMEM((tokens, hidden), BF16)] * 2,
        compiler_params=pltpu.CompilerParams(vmem_limit_bytes=VMEM_BYTES),
        cost_estimate=pl.CostEstimate(
            flops=12 * tokens * width * hidden * blocks, bytes_accessed=16 << 20, transcendentals=0
        ),
        name="feed",
    )(*arrays)
    return out[:2], out[2 : 2 + blocks], out[2 + blocks : 2 + 2 * blocks], out[2 + 2 * blocks :]


def unmix_kernel(blocks, dn2, residual, dy, mixed, inv, *refs):
    refs = list(refs)
    wo = [refs.pop(0) for _ in range(blocks)]
    q = [refs.pop(0) for _ in range(blocks // 2)]
    cols, gain, rgrad_out, low_out, dw_out, tg_out, back_out, small_out, w_all, back, small = refs
    step, last = pl.program_id(0), pl.num_programs(0) - 1

    @pl.when(step == 0)
    def _():
        for b in range(blocks):
            w_all[b * PAIR : (b + 1) * PAIR, :] = wo[b][:PAIR, :]
        back[...] = jnp.zeros_like(back)
        small[...] = jnp.zeros_like(small)

    live = cols[:, LIVE : LIVE + 1]
    reads = cols[:, READ_HALF : READ_HALF + 1].astype(BF16)
    xhat, rstd = normalise(residual[...])
    grad = dn2[...]
    scaled = grad * gain[...].astype(F32)
    mean_one = jnp.mean(scaled, axis=-1, keepdims=True)
    mean_two = jnp.mean(scaled * xhat, axis=-1, keepdims=True)
    wide = dy[...].astype(F32)
    rgrad = wide + rstd * (scaled - mean_one - xhat * mean_two)
    rgrad_out[...] = rgrad
    eight = lambda x: jnp.sum(x.reshape(CHUNK // 8, 8, x.shape[1]), axis=0)
    small[0] += eight(grad * xhat)
    small[1] += eight(grad)
    small[2] += eight(wide)
    low = rgrad.astype(BF16)
    low_out[...] = low
    mgrad = nt(low, w_all[...]) * live
    sums = pair_mask(PAIR).astype(BF16)
    sums = jnp.concatenate([sums, sums], axis=0)
    block_diagonal = pair_mask(2 * PAIR)
    for b in range(blocks):
        lanes = slice(b * PAIR, (b + 1) * PAIR)
        one = mgrad[:, lanes]
        scale = inv[:, lanes]
        dw = (one * scale).astype(BF16)
        terms = one * mixed[:, lanes].astype(F32)
        high = terms.astype(BF16)
        rest = (terms - high.astype(F32)).astype(BF16)
        total = nn(jnp.concatenate([high, rest], axis=1), sums)
        tg = jnp.where(scale < 1.0, -total * scale, 0.0).astype(BF16)
        dw_out[:, lanes] = dw
        tg_out[:, lanes] = tg
        back[b] += tn(q[b // 2][b % 2] * reads, jnp.concatenate([dw, tg], axis=1))

    @pl.when(step == last)
    def _():
        for b in range(blocks):
            back_out[b ^ 1] = jnp.where(block_diagonal, back[b], 0.0).astype(BF16)
        small_out[...] = small[...]


def unmix(dn2, residual, dy, mixed, inv, wo, q, cols, gain):
    tokens, width = dy.shape
    blocks = len(wo)
    whole = lambda shape: pl.BlockSpec(shape, lambda i: (0,) * len(shape))
    rows = lambda n: pl.BlockSpec((CHUNK, n), lambda i: (i, 0))
    part = pl.BlockSpec((2, CHUNK, PAIR), lambda i: (0, i, 0))
    return pl.pallas_call(
        functools.partial(unmix_kernel, blocks),
        grid=(tokens // CHUNK,),
        in_specs=[rows(width)] * 5
        + [whole(wo[0].shape)] * blocks
        + [part] * (blocks // 2)
        + [rows(8), whole((1, width))],
        out_specs=[rows(width)] * 4 + [whole((blocks, PAIR, 2 * PAIR)), whole((3, 8, width))],
        out_shape=[
            jax.ShapeDtypeStruct((tokens, width), F32),
            jax.ShapeDtypeStruct((tokens, width), BF16),
            jax.ShapeDtypeStruct((tokens, width), BF16),
            jax.ShapeDtypeStruct((tokens, width), BF16),
            jax.ShapeDtypeStruct((blocks, PAIR, 2 * PAIR), BF16),
            jax.ShapeDtypeStruct((3, 8, width), F32),
        ],
        scratch_shapes=[
            pltpu.VMEM((width, width), BF16),
            pltpu.VMEM((blocks, PAIR, 2 * PAIR), F32),
            pltpu.VMEM((3, 8, width), F32),
        ],
        compiler_params=pltpu.CompilerParams(
            dimension_semantics=("arbitrary",), vmem_limit_bytes=VMEM_BYTES
        ),
        cost_estimate=pl.CostEstimate(
            flops=4 * tokens * width * width, bytes_accessed=14 << 20, transcendentals=0
        ),
        name="unmix",
    )(dn2, residual, dy, mixed, inv, *wo, *q, cols, gain)


def finish_kernel(blocks, residual, branch, bias, mixed, low, *refs):
    out, gwo = refs[0], refs[1:]
    out[...] = (residual[...] + branch[...] + bias[...].astype(F32)).astype(BF16)
    grad = tn(mixed[...], low[...]).astype(BF16)
    for b in range(blocks):
        gwo[b][...] = grad[b * PAIR : (b + 1) * PAIR, :]


def finish(residual, branch, bias, mixed, low, blocks):
    tokens, width = residual.shape
    vmem = pl.BlockSpec(memory_space=pltpu.VMEM)
    out = pl.pallas_call(
        functools.partial(finish_kernel, blocks),
        in_specs=[vmem] * 5,
        out_specs=[vmem] * (1 + blocks),
        out_shape=[jax.ShapeDtypeStruct((tokens, width), BF16)]
        + [jax.ShapeDtypeStruct((PAIR, width), BF16)] * blocks,
        compiler_params=pltpu.CompilerParams(vmem_limit_bytes=VMEM_BYTES),
        cost_estimate=pl.CostEstimate(
            flops=2 * tokens * width * width, bytes_accessed=8 << 20, transcendentals=0
        ),
        name="finish",
    )(residual, branch, bias, mixed, low)
    return out[0], out[1:]


def attend_back_kernel(blocks, dw, tg, gone, *refs):
    refs = list(refs)
    groups = blocks // 2
    q, k, v, held, far = ([refs.pop(0) for _ in range(groups)] for _ in range(5))
    cols, doc_row, grads, state = refs

    @pl.when(pl.program_id(0) == 0)
    def _():
        state[...] = gone[...].astype(F32) * cols[0:1, FIRST_HALF : FIRST_HALF + 1]

    reads = cols[:, READ_CHUNK : READ_CHUNK + 1]
    reads_far = cols[:, READ_HALF : READ_HALF + 1]
    in_last = cols[:, IN_LAST : IN_LAST + 1]
    carried = cols[0:1, CARRIED : CARRIED + 1]
    mask = allowed_mask(cols[:, DOC : DOC + 1], doc_row[...])
    here = head_lanes((CHUNK, PAIR))
    block_diagonal = pair_mask(2 * PAIR)
    ones = jnp.ones((CHUNK, PAIR), BF16)
    zeros = jnp.zeros((CHUNK, PAIR), BF16)
    share = 1.0 / HEAD_DIM
    for b in range(blocks):
        g, i = divmod(b, 2)
        lanes = slice(b * PAIR, (b + 1) * PAIR)
        qb, kb, vb = q[g][i], k[g][i], v[g][i]
        dwb, tgb = dw[:, lanes], tg[:, lanes]
        q_t, dw_t = qb.T, dwb.T
        value_ones = jnp.concatenate([vb, ones], axis=1)
        grad_wide = jnp.concatenate([dwb, tgb * share], axis=1)
        dq = reads * nt(grad_wide, held[g][0, i]) + reads_far * nt(grad_wide, far[g][i])
        dk_t, dv_t = [], []
        for h, own in enumerate((here, jnp.logical_not(here))):
            feats = slice(h * HEAD_DIM, (h + 1) * HEAD_DIM)
            scores = nt(jnp.where(own, qb, zeros), kb)
            scores = jnp.where(mask, scores, 0.0).astype(BF16)
            own_wide = jnp.concatenate([own, own], axis=1)
            sgrad = nt(jnp.where(own_wide, grad_wide, jnp.zeros_like(grad_wide)), value_ones)
            sgrad = jnp.where(mask, sgrad, 0.0).astype(BF16)
            dq = dq + nn(sgrad, jnp.where(own, kb, zeros))
            dk_t.append(nn(q_t[feats], sgrad))
            dv_t.append(nn(dw_t[feats], scores))
        low = state[b].astype(BF16)
        dk = jnp.concatenate(dk_t, axis=0).T
        dv = jnp.concatenate(dv_t, axis=0).T
        dk = dk + in_last * nt(jnp.concatenate([vb, ones * share], axis=1), low)
        dv = dv + in_last * nn(kb, low[:, :PAIR])
        grads[b, 0] = (dq * jnp.minimum(qb.astype(F32), 1.0)).astype(BF16)
        grads[b, 1] = (dk * jnp.minimum(kb.astype(F32), 1.0)).astype(BF16)
        grads[b, 2] = dv.astype(BF16)
        grown = tn(qb * reads.astype(BF16), jnp.concatenate([dwb, tgb], axis=1))
        state[b] = carried * state[b] + jnp.where(block_diagonal, grown, 0.0)


def attend_back(dw, tg, gone, q, k, v, held, far, cols, doc_row):
    tokens, width = dw.shape
    groups = len(q)
    blocks, chunks = 2 * groups, tokens // CHUNK
    whole = lambda shape: pl.BlockSpec(shape, lambda i: (0,) * len(shape))
    rows = lambda n: pl.BlockSpec((CHUNK, n), lambda i: (chunks - 1 - i, 0))
    part = pl.BlockSpec((2, CHUNK, PAIR), lambda i: (0, chunks - 1 - i, 0))
    return pl.pallas_call(
        functools.partial(attend_back_kernel, blocks),
        grid=(chunks,),
        in_specs=[rows(width)] * 2
        + [whole((blocks, PAIR, 2 * PAIR))]
        + [part] * (3 * groups)
        + [pl.BlockSpec((1, 2, PAIR, 2 * PAIR), lambda i: (chunks - 1 - i, 0, 0, 0))] * groups
        + [whole((2, PAIR, 2 * PAIR))] * groups
        + [rows(8), pl.BlockSpec((1, CHUNK), lambda i: (0, chunks - 1 - i))],
        out_specs=pl.BlockSpec((blocks, 3, CHUNK, PAIR), lambda i: (0, 0, chunks - 1 - i, 0)),
        out_shape=jax.ShapeDtypeStruct((blocks, 3, tokens, PAIR), BF16),
        scratch_shapes=[pltpu.VMEM((blocks, PAIR, 2 * PAIR), F32)],
        compiler_params=pltpu.CompilerParams(
            dimension_semantics=("arbitrary",), vmem_limit_bytes=VMEM_BYTES
        ),
        cost_estimate=pl.CostEstimate(
            flops=20 * tokens * width * CHUNK, bytes_accessed=8 << 20, transcendentals=0
        ),
        name="attend_back",
    )(dw, tg, gone, *q, *k, *v, *held, *far, cols, doc_row)


def project_back_kernel(n1, grads, *outs):
    for b, out in enumerate(outs):
        both = jnp.concatenate([grads[b, p] for p in range(3)], axis=1)
        grad = tn(n1[...], both).astype(BF16)
        for p in range(3):
            out[p] = grad[:, p * PAIR : (p + 1) * PAIR]


def project_back(n1, grads):
    tokens, width = n1.shape
    blocks = grads.shape[0]
    vmem = pl.BlockSpec(memory_space=pltpu.VMEM)
    return pl.pallas_call(
        project_back_kernel,
        in_specs=[vmem] * 2,
        out_specs=[vmem] * blocks,
        out_shape=[jax.ShapeDtypeStruct((3, width, PAIR), BF16)] * blocks,
        compiler_params=pltpu.CompilerParams(vmem_limit_bytes=VMEM_BYTES),
        cost_estimate=pl.CostEstimate(
            flops=6 * tokens * width * width, bytes_accessed=6 << 20, transcendentals=0
        ),
        name="project_back",
    )(n1, grads)


def input_back_kernel(blocks, tok, rgrad, grads, gain, *refs):
    w, (out, small_out, w_all, small) = refs[:blocks], refs[blocks:]
    step, last = pl.program_id(0), pl.num_programs(0) - 1

    @pl.when(step == 0)
    def _():
        for b in range(blocks):
            for p in range(3):
                at = (3 * b + p) * PAIR
                w_all[:, at : at + PAIR] = w[b][p]
        small[...] = jnp.zeros_like(small)

    both = jnp.concatenate([grads[b, p] for b in range(blocks) for p in range(3)], axis=1)
    grad = nt(both, w_all[...])
    xhat, rstd = normalise(tok[...].astype(F32))
    scaled = grad * gain[...].astype(F32)
    mean_one = jnp.mean(scaled, axis=-1, keepdims=True)
    mean_two = jnp.mean(scaled * xhat, axis=-1, keepdims=True)
    out[...] = rgrad[...] + rstd * (scaled - mean_one - xhat * mean_two)
    eight = lambda x: jnp.sum(x.reshape(CHUNK // 8, 8, x.shape[1]), axis=0)
    small[0] += eight(grad * xhat)
    small[1] += eight(grad)

    @pl.when(step == last)
    def _():
        small_out[...] = small[...]


def input_back(tok, rgrad, grads, gain, w):
    tokens, width = tok.shape
    blocks = len(w)
    whole = lambda shape: pl.BlockSpec(shape, lambda i: (0,) * len(shape))
    rows = lambda n: pl.BlockSpec((CHUNK, n), lambda i: (i, 0))
    return pl.pallas_call(
        functools.partial(input_back_kernel, blocks),
        grid=(tokens // CHUNK,),
        in_specs=[rows(width)] * 2
        + [pl.BlockSpec((blocks, 3, CHUNK, PAIR), lambda i: (0, 0, i, 0)), whole((1, width))]
        + [whole((3, width, PAIR))] * blocks,
        out_specs=[rows(width), whole((2, 8, width))],
        out_shape=[
            jax.ShapeDtypeStruct((tokens, width), F32),
            jax.ShapeDtypeStruct((2, 8, width), F32),
        ],
        scratch_shapes=[
            pltpu.VMEM((width, 3 * blocks * PAIR), BF16),
            pltpu.VMEM((2, 8, width), F32),
        ],
        compiler_params=pltpu.CompilerParams(
            dimension_semantics=("arbitrary",), vmem_limit_bytes=VMEM_BYTES
        ),
        cost_estimate=pl.CostEstimate(
            flops=6 * tokens * width * width, bytes_accessed=10 << 20, transcendentals=0
        ),
        name="input_back",
    )(tok, rgrad, grads, gain, *w)


def swap(x, axis, size, bit):
    return lax.ppermute(x, axis, [(i, i ^ bit) for i in range(size)])


def piece(x, index, count):
    rows = x.shape[0] // count
    return lax.dynamic_slice_in_dim(x, index * rows, rows, 0)


def sum_over_dp(x, count):
    me = lax.axis_index("dp")
    near, far = me % 2, me // 2
    rest = count // 2
    mine = piece(x, near, 2).astype(F32) + swap(piece(x, 1 - near, 2), "dp", count, 1).astype(F32)
    low = mine.astype(BF16)
    total = piece(low, far, rest).astype(F32)
    for s in range(1, rest):
        total = total + swap(piece(low, far ^ s, rest), "dp", count, 2 * s).astype(F32)
    own = total.astype(BF16)
    rows = own.shape[0]
    half = jnp.zeros((rest,) + own.shape, BF16)
    half = lax.dynamic_update_index_in_dim(half, own, far, 0)
    for s in range(1, rest):
        half = lax.dynamic_update_index_in_dim(half, swap(own, "dp", count, 2 * s), far ^ s, 0)
    half = half.reshape((rows * rest,) + own.shape[1:])
    other = swap(half, "dp", count, 1)
    return jnp.where(
        near == 0, jnp.concatenate([half, other]), jnp.concatenate([other, half])
    ).astype(F32)


def body(
    dp,
    head,
    tokens,
    doc_ids,
    pad_mask,
    norm1_gain,
    norm1_shift,
    w_qkv,
    w_out,
    norm2_gain,
    norm2_shift,
    w_hidden,
    hidden_bias,
    w_return,
    return_bias,
    out_grad,
):
    count, width = tokens.shape
    length = doc_ids.shape[1]
    halves = length // count
    me = lax.axis_index("head")
    row, place = me // halves, me % halves

    def gather(x):
        across = swap(x, "head", head, 2)
        return [x, swap(x, "head", head, 1), across, swap(across, "head", head, 1)]

    extra = jnp.concatenate([w_out, jnp.broadcast_to(hidden_bias[None], (16, width))])
    wq = gather(w_qkv)
    wo = gather(extra)
    wh = gather(w_hidden)
    wr = gather(w_return)

    docs_row = lax.dynamic_index_in_dim(doc_ids, row, 0, keepdims=False)
    docs = lax.dynamic_slice_in_dim(docs_row, place * count, count, 0)
    live = lax.dynamic_slice_in_dim(
        lax.dynamic_index_in_dim(pad_mask, row, 0, keepdims=False), place * count, count, 0
    ).astype(F32)
    edge = docs_row[count - 1]
    second = (place > 0).astype(F32)
    chunks = count // CHUNK
    in_chunks = docs.reshape(chunks, CHUNK)
    ends = in_chunks[:, -1]
    before = jnp.concatenate([jnp.full((1,), -1, jnp.int32), ends[:-1]])
    spread = lambda x: jnp.broadcast_to(x[:, None], (chunks, CHUNK)).reshape(count)
    flags = [
        docs.astype(F32),
        live,
        (docs == edge).astype(F32) * second,
        (in_chunks == before[:, None]).astype(F32).reshape(count),
        (in_chunks == ends[:, None]).astype(F32).reshape(count),
        spread((ends == before).astype(F32)),
        jnp.broadcast_to(1.0 - second, (count,)),
        jnp.zeros((count,), F32),
    ]
    cols = jnp.stack(flags, axis=1)
    doc_row = docs.astype(F32)[None]
    line = lambda x: x[None]

    n1, *near = attend(tokens, (line(norm1_gain), line(norm1_shift)), wq[:2], cols, doc_row)
    far = attend(n1, None, wq[2:], cols, doc_row)
    q, k, v, num, tot, held, last = zip(near, far)
    come = [swap(x, "head", head, 1) for x in last]
    mixed, inv, residual, n2 = mix(
        tokens, q, num, tot, come, wo, cols, line(norm2_gain), line(norm2_shift)
    )
    partial, gwh_a, gwr_a, ghb_a = feed(n2, out_grad, wh[:2], wr[:2], wo[:2], None)
    partial, gwh_b, gwr_b, ghb_b = feed(n2, out_grad, wh[2:], wr[2:], wo[2:], partial)
    branch, dn2 = partial
    rgrad, low, dw, tg, gone, small2 = unmix(
        dn2, residual, out_grad, mixed, inv, wo, q, cols, line(norm2_gain)
    )
    gone_in = swap(gone, "head", head, 1)
    output, gwo = finish(residual, branch, line(return_bias), mixed, low, head)
    pgrads = attend_back(dw, tg, gone_in, q, k, v, held, come, cols, doc_row)
    gq = project_back(n1, pgrads)
    tokens_grad, small1 = input_back(tokens, rgrad, pgrads, line(norm1_gain), wq)

    def share(blocks):
        first = lambda a, b: (a.astype(F32) + swap(b, "head", head, 1).astype(F32))
        mine = first(blocks[0], blocks[1])
        theirs = first(blocks[2], blocks[3]).astype(BF16)
        return (mine + swap(theirs, "head", head, 2).astype(F32)).astype(BF16)

    gwh = sum_over_dp(share([*gwh_a, *gwh_b]), dp)
    gwr = sum_over_dp(share([*gwr_a, *gwr_b]), dp)
    ghb = [jnp.sum(x, axis=0) for x in (*ghb_a, *ghb_b)]
    rest = [
        jnp.concatenate([a, jnp.broadcast_to(b[None].astype(BF16), (PAIR, width))])
        for a, b in zip(gwo, ghb)
    ]
    rest = sum_over_dp(share(rest), dp)
    gw_out, g_bias = rest[:PAIR], rest[PAIR]
    gq = sum_over_dp(share([x.reshape(3 * width, PAIR) for x in gq]), dp).reshape(3, width, PAIR)

    small = jnp.concatenate([jnp.sum(small1, axis=1), jnp.sum(small2, axis=1)])
    bit = 1
    while bit < head:
        small = small + swap(small, "head", head, bit)
        bit *= 2
    bit = 1
    while bit < dp:
        small = small + swap(small, "dp", dp, bit)
        bit *= 2
    return (
        output,
        tokens_grad,
        small[0],
        small[1],
        gq,
        gw_out,
        small[2],
        small[3],
        gwh,
        g_bias,
        gwr,
        small[4],
    )


def solution(mesh):
    return jax.shard_map(
        functools.partial(body, mesh.shape["dp"], mesh.shape["head"]),
        mesh=mesh,
        in_specs=(
            P(("dp", "head"), None),
            P("dp", None),
            P("dp", None),
            P(),
            P(),
            P(None, None, "head"),
            P("head", None),
            P(),
            P(),
            P(None, "head"),
            P("head"),
            P("head", None),
            P(),
            P(("dp", "head"), None),
        ),
        out_specs=(
            P(("dp", "head"), None),
            P(("dp", "head"), None),
            P(),
            P(),
            P(None, None, "head"),
            P("head", None),
            P(),
            P(),
            P(None, "head"),
            P("head"),
            P("head", None),
            P(),
        ),
        check_vma=False,
    )
```

```python
import functools

import jax
import jax.numpy as jnp
from jax import lax
from jax.experimental import pallas as pl
from jax.experimental.pallas import tpu as pltpu
from jax.sharding import PartitionSpec as P

HEAD_DIM = 64
PAIR = 2 * HEAD_DIM
WIDE = 2 * PAIR
CHUNK = 256
LANES = 128
EPSILON = 1e-05
BELOW_ONE = 1.0 - 2.0**-8
F32 = jnp.float32
BF16 = jnp.bfloat16
VMEM_BYTES = 60 * 1024 * 1024

DOC, LIVE, READ_HALF, READ_CHUNK, IN_LAST, CARRIED, FIRST_HALF = range(7)


def nn(a, b):
    return lax.dot_general(a, b, (((1,), (0,)), ((), ())), preferred_element_type=F32)


def nt(a, b):
    return lax.dot_general(a, b, (((1,), (1,)), ((), ())), preferred_element_type=F32)


def tn(a, b):
    return lax.dot_general(a, b, (((0,), (0,)), ((), ())), preferred_element_type=F32)


def normalise(x):
    centre = x - jnp.mean(x, axis=-1, keepdims=True)
    rstd = lax.rsqrt(jnp.mean(centre * centre, axis=-1, keepdims=True) + EPSILON)
    return centre * rstd, rstd


def norm_back(grad, xhat, rstd, gain):
    scaled = grad * gain
    mean_one = jnp.mean(scaled, axis=-1, keepdims=True)
    mean_two = jnp.mean(scaled * xhat, axis=-1, keepdims=True)
    return rstd * (scaled - mean_one - xhat * mean_two)


def line(ref):
    return ref[...].astype(F32).reshape(1, ref.shape[0])


def eight(x):
    return jnp.sum(x.reshape(x.shape[0] // 8, 8, x.shape[1]), axis=0)


def head_lanes(shape):
    return lax.broadcasted_iota(jnp.int32, shape, len(shape) - 1) % PAIR < HEAD_DIM


def pair_mask(width):
    rows = lax.broadcasted_iota(jnp.int32, (PAIR, width), 0) < HEAD_DIM
    return rows == head_lanes((PAIR, width))


def allowed_mask(doc_col, doc_row):
    t = lax.broadcasted_iota(jnp.int32, (CHUNK, CHUNK), 0)
    s = lax.broadcasted_iota(jnp.int32, (CHUNK, CHUNK), 1)
    return (doc_col == doc_row) & (s <= t)


def feature(x):
    return jnp.where(x > 0, x + 1.0, jnp.exp(jnp.minimum(x, 0.0)))


def chunk_rows(c):
    return slice(c * CHUNK, (c + 1) * CHUNK)


def column(cols, which):
    return cols[:, which : which + 1]


def stack(x, masks):
    return jnp.concatenate([jnp.where(mask, x, jnp.zeros_like(x)) for mask in masks], axis=0)


class Rows:
    def __init__(self, array, first, columns=None):
        self.array = array
        self.columns = columns or slice(0, array.shape[-1])
        self.shape = array.shape[:-1] + (self.columns.stop - self.columns.start,)
        rows = self.shape[-2]
        rest = slice(CHUNK, rows) if first == 0 else slice(0, rows - CHUNK)
        self.first, self.parts = first, [chunk_rows(first), rest]

    def index(self, rows, columns):
        return (slice(None),) * (len(self.shape) - 2) + (rows, columns)


class Staged:
    def __init__(self, specs, ins, outs, scratch, in_sem, out_sem):
        self.specs, self.ins, self.outs, self.scratch = specs, ins, outs, scratch
        self.out_sem, self.sent = out_sem, []
        self.pending = {}
        for turn in range(2):
            for name, (src, dst) in ins.items():
                spec = specs[name]
                if isinstance(spec, Rows):
                    rows = spec.parts[turn]
                    src = src.at[spec.index(rows, spec.columns)]
                    dst = dst.at[spec.index(rows, slice(None))]
                elif turn > 0:
                    continue
                copy = pltpu.make_async_copy(src, dst, in_sem.at[len(self.pending)])
                copy.start()
                self.pending[name, turn] = copy

    def __getitem__(self, name):
        for key in [key for key in self.pending if key[0] == name]:
            self.pending.pop(key).wait()
        return self.ins[name][1] if name in self.ins else self.scratch[name]

    def rows(self, name, c):
        spec = self.specs[name]
        if not isinstance(spec, Rows):
            return self[name][chunk_rows(c), :]
        key = (name, int(c != spec.first))
        if key in self.pending:
            self.pending.pop(key).wait()
        return self.ins[name][1][spec.index(chunk_rows(c), slice(None))]

    def out(self, name):
        return self.outs[name][1]

    def send(self, name, *index):
        dst, src = self.outs[name]
        if index:
            dst, src = dst.at[index], src.at[index]
        copy = pltpu.make_async_copy(src, dst, self.out_sem.at[len(self.sent)])
        copy.start()
        self.sent.append(copy)

    def finish(self):
        for copy in list(self.pending.values()) + self.sent:
            copy.wait()


def staged(name, body, ins, outs, scratch, flops, sends, filled=None):
    in_names, out_names, scratch_names = list(ins), list(outs), list(scratch)
    arrays, in_specs, own = [], [], []
    for value in ins.values():
        value = value.array if isinstance(value, Rows) else value
        arrays.append(value[0] if isinstance(value, tuple) else value)
        in_specs.append(pl.BlockSpec(memory_space=pl.ANY))
        if not isinstance(value, tuple):
            own.append(pltpu.VMEM(ins[in_names[len(arrays) - 1]].shape, value.dtype))

    if filled is not None:
        arrays.append(filled)
        in_specs.append(pl.BlockSpec(memory_space=pl.ANY))

    def kernel(*refs):
        refs = list(refs)
        take = lambda n: [refs.pop(0) for _ in range(n)]
        src = take(len(arrays))[: len(in_names)]
        dst = take(len(out_names))
        own_refs, out_refs = take(len(own)), take(len(out_names))
        held = dict(zip(scratch_names, take(len(scratch_names))))
        in_sem, out_sem = refs
        ends = {}
        for key, ref in zip(in_names, src):
            value = ins[key]
            if not isinstance(value, tuple):
                ends[key] = (ref, own_refs.pop(0))
            else:
                ends[key] = (ref.at[value[3:]] if value[3:] else ref, held[value[1]].at[value[2]])
        stage = Staged(ins, ends, dict(zip(out_names, zip(dst, out_refs))), held, in_sem, out_sem)
        body(stage)
        stage.finish()

    shapes = list(outs.values())
    copies = sum(2 if isinstance(x, Rows) else 1 for x in ins.values())
    out = pl.pallas_call(
        kernel,
        in_specs=in_specs,
        out_specs=[pl.BlockSpec(memory_space=pl.ANY)] * len(out_names),
        out_shape=[jax.ShapeDtypeStruct(*s) for s in shapes],
        scratch_shapes=own
        + [pltpu.VMEM(*s) for s in shapes]
        + [pltpu.VMEM(*s) for s in scratch.values()]
        + [pltpu.SemaphoreType.DMA((copies,)), pltpu.SemaphoreType.DMA((sends,))],
        input_output_aliases={} if filled is None else {len(in_names): 0},
        compiler_params=pltpu.CompilerParams(vmem_limit_bytes=VMEM_BYTES),
        cost_estimate=pl.CostEstimate(flops=flops, bytes_accessed=4 << 20, transcendentals=0),
        name=name,
    )(*arrays)
    return dict(zip(out_names, out))


def attend_chunk(st, blocks, c, n1, cols, doc_row):
    w, state, every = st["w"], st["state"], range(blocks)
    rows = chunk_rows(c)
    live, reads = column(cols, LIVE), column(cols, READ_CHUNK)
    in_last = column(cols, IN_LAST).astype(BF16)
    carried = cols[0:1, CARRIED : CARRIED + 1]
    mask = allowed_mask(column(cols, DOC), doc_row[:, rows])
    mask = jnp.concatenate([mask, mask], axis=0)
    q_all = feature(nn(n1, w[0])).astype(BF16)
    k_all = (feature(nn(n1, w[1])) * live).astype(BF16)
    v_all = nn(n1, w[2]).astype(BF16)
    here = head_lanes((CHUNK, WIDE))
    own = [here[:, :PAIR], jnp.logical_not(here[:, :PAIR])]
    block_diagonal = pair_mask(WIDE)
    ones = jnp.ones((CHUNK, PAIR), BF16)
    part = lambda x, b: x[:, b * PAIR : (b + 1) * PAIR]
    q, k, v = ([part(x, b) for b in every] for x in (q_all, k_all, v_all))
    for b in every:
        st.out("q")[b, rows], st.out("k")[b, rows], st.out("v")[b, rows] = q[b], k[b], v[b]
    scores = [nt(stack(q[b], own), k[b]) for b in every]
    wide = [jnp.concatenate([v[b], ones], axis=1) for b in every]
    grown = [tn(k[b] * in_last, wide[b]) for b in every]
    scores = [jnp.where(mask, scores[b], 0.0).astype(BF16) for b in every]
    both = [nn(scores[b], wide[b]) for b in every]
    total = [jnp.where(here, both[b][:CHUNK], both[b][CHUNK:]) for b in every]
    for b in every:
        if c > 0:
            low = state[b].astype(BF16)
            st.out("held")[c, b] = low
            total[b] = total[b] + reads * nn(q[b], low)
        else:
            st.out("held")[c, b] = jnp.zeros((PAIR, WIDE), BF16)
        st.out("num")[b, rows], st.out("tot")[b, rows] = total[b][:, :PAIR], total[b][:, PAIR:]
        more = jnp.where(block_diagonal, grown[b], 0.0)
        state[b] = more if c == 0 else carried * state[b] + more
    for name in ("q", "k", "v", "num", "tot"):
        st.send(name, slice(None), rows)


def attend_finish(st, blocks):
    for b in range(blocks):
        st.out("last")[b ^ 1] = st["state"][b].astype(BF16)
    st.send("last")
    st.send("held")


def attend_outs(tokens, blocks):
    part = (blocks, tokens, PAIR)
    return dict(
        q=(part, BF16),
        k=(part, BF16),
        v=(part, BF16),
        num=(part, F32),
        tot=(part, F32),
        held=((tokens // CHUNK, blocks, PAIR, WIDE), BF16),
        last=((blocks, PAIR, WIDE), BF16),
    )


def attend_scratch(width, blocks):
    return dict(w=((3, width, blocks * PAIR), BF16), state=((blocks, PAIR, WIDE), F32))


def attend_weights(w):
    everything = slice(None)
    return {
        f"w{b}": (x, "w", (everything, everything, slice(b * PAIR, (b + 1) * PAIR)))
        for b, x in enumerate(w)
    }


def attend_flops(tokens, width, blocks):
    return 2 * tokens * blocks * PAIR * (3 * width + 4 * CHUNK)


def make_flags(doc_ids, pad_mask, count):
    halves = doc_ids.shape[1] // count
    me = lax.axis_index("head")
    row, place = lax.div(me, halves), lax.rem(me, halves)

    def here(x):
        whole = x[0:1, :]
        for r in range(1, x.shape[0]):
            whole = jnp.where(row == r, x[r : r + 1, :], whole)
        part = whole[:, :count]
        for i in range(1, x.shape[1] // count):
            part = jnp.where(place == i, whole[:, i * count : (i + 1) * count], part)
        return whole, part

    whole, docs = here(doc_ids)
    _, live = here(pad_mask)
    edge = whole[:, count - 1 : count]
    second = jnp.where(place > 0, 1.0, 0.0)
    as_float = lambda x: jnp.where(x, 1.0, 0.0)
    reads, in_last, carried = [], [], []
    before = None
    for c in range(count // CHUNK):
        part = docs[:, chunk_rows(c)]
        end = part[:, CHUNK - 1 : CHUNK]
        in_last.append(as_float(part == end))
        if before is None:
            reads.append(jnp.zeros((1, CHUNK), F32))
            carried.append(jnp.zeros((1, CHUNK), F32))
        else:
            reads.append(as_float(part == before))
            carried.append(as_float(jnp.broadcast_to(end, part.shape) == before))
        before = end
    join = lambda x: jnp.concatenate(x, axis=1)
    doc_line = docs.astype(F32)
    lines = [
        doc_line,
        live.astype(F32),
        as_float(docs == edge) * second,
        join(reads),
        join(in_last),
        join(carried),
        jnp.broadcast_to(1.0 - second, (1, count)).astype(F32),
    ]
    lines.append(jnp.zeros((LANES - len(lines), count), F32))
    return jnp.concatenate(lines, axis=0).T, doc_line


def open_layer(doc_ids, pad_mask, tok, gain, shift, w, w_hidden, hidden_bias):
    tokens, width = tok.shape
    blocks, chunks, hidden = len(w), tokens // CHUNK, w_hidden.shape[1]

    def body(st):
        cols, doc_row = make_flags(st["doc_ids"], st["pad_mask"], tokens)
        st.out("cols")[...], st.out("doc_row")[...] = cols, doc_row
        st.send("cols")
        st.send("doc_row")
        cols, doc_row, n1 = st.out("cols"), st.out("doc_row"), st.out("n1")
        gain, shift = line(st["gain"]), line(st["shift"])
        for c in range(chunks):
            xhat, _ = normalise(st.rows("tok", c).astype(F32))
            n1[chunk_rows(c), :] = (xhat * gain + shift).astype(BF16)
        st.send("n1")
        for b in range(blocks):
            st[f"w{b}"]
        for c in range(chunks):
            attend_chunk(st, blocks, c, n1[chunk_rows(c), :], cols[chunk_rows(c), :], doc_row)
        attend_finish(st, blocks)
        st["wh"][width:, :] = jnp.broadcast_to(line(st["bias"]).astype(BF16), (16, hidden))
        st["w_hidden"]
        st.out("wh")[...] = st["wh"][...]
        st.send("wh")

    ins = dict(doc_ids=doc_ids, pad_mask=pad_mask, tok=Rows(tok, 0))
    ins.update(gain=gain, shift=shift, **attend_weights(w), bias=hidden_bias)
    ins.update(w_hidden=(w_hidden, "wh", (slice(0, width),)))
    outs = dict(
        cols=((tokens, LANES), F32),
        doc_row=((1, tokens), F32),
        n1=((tokens, width), BF16),
        wh=((width + 16, hidden), BF16),
    )
    outs.update(attend_outs(tokens, blocks))
    scratch = attend_scratch(width, blocks)
    scratch["wh"] = ((width + 16, hidden), BF16)
    flops = attend_flops(tokens, width, blocks)
    return staged("open", body, ins, outs, scratch, flops, 5 * chunks + 6)


def attend(n1, w, cols, doc_row):
    tokens, width = n1.shape
    blocks, chunks = len(w), tokens // CHUNK

    def body(st):
        doc_row = st["doc_row"]
        for b in range(blocks):
            st[f"w{b}"]
        for c in range(chunks):
            attend_chunk(st, blocks, c, st.rows("n1", c), st.rows("cols", c), doc_row)
        attend_finish(st, blocks)

    ins = dict(doc_row=doc_row, **attend_weights(w))
    ins.update(n1=Rows(n1, 0), cols=Rows(cols, 0))
    flops = attend_flops(tokens, width, blocks)
    return staged(
        "attend",
        body,
        ins,
        attend_outs(tokens, blocks),
        attend_scratch(width, blocks),
        flops,
        5 * chunks + 2,
    )


def gelu_pair(x):
    cdf = 0.5 + 0.5 * lax.erf(x * 0.7071067811865476)
    density = 0.3989422804014327 * jnp.exp(-0.5 * x * x)
    return x * cdf, cdf + x * density


def mix_chunk(st, groups, c):
    cols, w, rows = st.rows("cols", c), st["wo"], chunk_rows(c)
    live, reads = column(cols, LIVE), column(cols, READ_HALF)
    q, num, tot = ([st.rows(f"{x}{g}", c) for g in range(groups)] for x in ("q", "num", "tot"))
    mixed, inv_out = st.out("mixed"), st.out("inv")
    for b in range(2 * groups):
        g, i = divmod(b, 2)
        lanes = slice(b * PAIR, (b + 1) * PAIR)
        far = reads * nn(q[g][i], st[f"come{g}"][i])
        inv = 1.0 / jnp.maximum(tot[g][i] + far[:, PAIR:], 1.0)
        inv_out[rows, lanes] = jnp.where(inv < 1.0, jnp.minimum(inv, BELOW_ONE), 1.0).astype(BF16)
        value = (num[g][i] + far[:, :PAIR]) * inv * live
        mixed[rows, lanes] = value.astype(BF16)
    residual = st.rows("tok", c).astype(F32) + nn(mixed[rows, :], w[...])
    st.out("residual")[rows, :] = residual
    xhat, _ = normalise(residual)
    n2 = (xhat * line(st["gain"]) + line(st["shift"])).astype(BF16)
    st.out("n2")[rows, :] = n2
    for name in ("mixed", "inv", "residual", "n2"):
        st.send(name, rows)


def feed_chunk(st, c, n2, bias, resume):
    rows = chunk_rows(c)
    wh, wr = st["wh"].at[: n2.shape[1]], st["wr"]
    value, slope = gelu_pair(nn(n2, wh[...]) + bias)
    st.out("act")[rows, :] = value.astype(BF16)
    st.send("act", rows)
    grad = nt(st.rows("dy", c), wr[...]) * slope
    low = grad.astype(BF16)
    st["hg"][rows, :] = low
    back = nt(low, wh[...])
    st.out("dn2")[rows, :] = back + st.rows("dn2_in", c) if resume else back
    st.send("dn2", rows)
    return eight(grad)


def feed_grads(st, blocks, pieces, n2, bias_grad):
    width, hidden = n2.shape[1], bias_grad.shape[1] // blocks
    bias_grad = jnp.sum(bias_grad, axis=0, keepdims=True).astype(BF16)
    for b in range(blocks):
        part = slice(b * hidden, (b + 1) * hidden)
        down, up = st.out(f"down{b}"), st.out(f"up{b}")
        down[...] = tn(st.out("act")[:, part], st["dy"][...]).astype(BF16)
        st.send(f"down{b}")
        grad = tn(n2[...], st["hg"][:, part]).astype(BF16)
        rows, step = width // pieces, up.shape[0] // pieces
        for i in range(pieces):
            up[i * step : i * step + rows, :] = grad[i * rows : (i + 1) * rows, :]
            tail = jnp.broadcast_to(bias_grad[:, part], (step - rows, hidden))
            up[i * step + rows : (i + 1) * step, :] = tail
        st.send(f"up{b}")


def feed_parts(tokens, width, pieces, wh, wr):
    blocks, hidden = len(wr), wr[0].shape[0]
    everything = slice(None)
    ins = {}
    for b in range(blocks):
        part = slice(b * hidden, (b + 1) * hidden)
        ins[f"wh{b}"] = (wh[b], "wh", (everything, part))
        ins[f"wr{b}"] = (wr[b], "wr", (part, everything))
    outs = dict(act=((tokens, blocks * hidden), BF16), dn2=((tokens, width), F32))
    for b in range(blocks):
        outs[f"down{b}"] = ((hidden, width), BF16)
        outs[f"up{b}"] = ((width + 16 * pieces, hidden), BF16)
    scratch = dict(
        wh=((width + 16, blocks * hidden), BF16),
        wr=((blocks * hidden, width), BF16),
        hg=((tokens, blocks * hidden), BF16),
    )
    return ins, outs, scratch, 10 * tokens * width * hidden * blocks


def feed_start(st, blocks, width):
    for b in range(blocks):
        st[f"wh{b}"], st[f"wr{b}"]
    return st["wh"][width : width + 1, :].astype(F32)


def mix_feed(pieces, tok, dy, parts, come, wo, cols, gain, shift, wh, wr):
    tokens, width = tok.shape
    blocks, groups, chunks = len(wh), len(parts), tokens // CHUNK

    def body(st):
        for b in range(2 * groups):
            st[f"wo{b}"]
        for c in range(chunks):
            mix_chunk(st, groups, c)
        n2 = st.out("n2")
        bias = feed_start(st, blocks, width)
        bias_grad = 0.0
        for c in range(chunks):
            bias_grad = bias_grad + feed_chunk(st, c, n2[chunk_rows(c), :], bias, False)
        feed_grads(st, blocks, pieces, n2, bias_grad)

    ins = dict(cols=Rows(cols, 0), tok=Rows(tok, 0), gain=gain, shift=shift)
    for g, part in enumerate(parts):
        ins.update({f"{x}{g}": Rows(part[x], 0) for x in ("q", "num", "tot")})
        ins[f"come{g}"] = come[g]
    for b, x in enumerate(wo):
        ins[f"wo{b}"] = (x, "wo", (slice(b * PAIR, (b + 1) * PAIR),))
    ins["dy"] = Rows(dy, 0)
    more, outs, scratch, flops = feed_parts(tokens, width, pieces, wh, wr)
    ins.update(more)
    outs.update(
        mixed=((tokens, width), BF16),
        inv=((tokens, width), BF16),
        residual=((tokens, width), F32),
        n2=((tokens, width), BF16),
    )
    scratch["wo"] = ((width, width), BF16)
    return staged("mix_feed", body, ins, outs, scratch, 0, 6 * chunks + 2 * blocks)


def feed(pieces, n2, dy, wh, wr, dn2):
    tokens, width = n2.shape
    blocks, chunks = len(wh), tokens // CHUNK

    def body(st):
        bias = feed_start(st, blocks, width)
        bias_grad = 0.0
        for c in range(chunks):
            bias_grad = bias_grad + feed_chunk(st, c, st.rows("n2", c), bias, True)
        feed_grads(st, blocks, pieces, st["n2"], bias_grad)

    ins = dict(n2=n2)
    more, outs, scratch, flops = feed_parts(tokens, width, pieces, wh, wr)
    ins.update(more)
    ins.update(dy=dy, dn2_in=dn2)
    return staged("feed", body, ins, outs, scratch, flops, 2 * chunks + 2 * blocks)


def unmix_chunk(st, blocks, c):
    cols, rows = st.rows("cols", c), chunk_rows(c)
    live, reads = column(cols, LIVE), column(cols, READ_HALF).astype(BF16)
    xhat, rstd = normalise(st.rows("residual", c))
    grad = st.rows("dn2", c)
    wide = st.rows("dy", c).astype(F32)
    rgrad = wide + norm_back(grad, xhat, rstd, line(st["gain"]))
    low = rgrad.astype(BF16)
    st.out("rgrad")[rows, :] = low
    mgrad = nt(low, st["wo"][...]) * live
    sums = pair_mask(PAIR).astype(BF16)
    sums = jnp.concatenate([sums, sums], axis=0)
    inv, mixed = st.rows("inv", c).astype(F32), st.rows("mixed", c).astype(F32)
    q = [st.rows(f"q{g}", c) for g in range(blocks // 2)]
    for b in range(blocks):
        lanes = slice(b * PAIR, (b + 1) * PAIR)
        one, scale = mgrad[:, lanes], inv[:, lanes]
        dw = (one * scale).astype(BF16)
        terms = one * mixed[:, lanes]
        high = terms.astype(BF16)
        rest = (terms - high.astype(F32)).astype(BF16)
        total = nn(jnp.concatenate([high, rest], axis=1), sums)
        tg = jnp.where(scale < 1.0, -total * scale, 0.0).astype(BF16)
        st.out("dw")[rows, b * WIDE : b * WIDE + PAIR] = dw
        st.out("dw")[rows, b * WIDE + PAIR : (b + 1) * WIDE] = tg
        st["reading"][rows, lanes] = q[b // 2][b % 2] * reads
    st.send("rgrad", rows)
    st.send("dw", rows)
    return eight(grad * xhat), eight(grad), eight(wide)


def unmix(dn2, residual, dy, mixed, inv, wo, q, cols, gain):
    tokens, width = dy.shape
    blocks, chunks = len(wo), tokens // CHUNK

    def body(st):
        for b in range(blocks):
            st[f"wo{b}"]
        small = [0.0, 0.0, 0.0]
        for c in range(chunks):
            small = [a + b for a, b in zip(small, unmix_chunk(st, blocks, c))]
        small = [jnp.sum(x, axis=0, keepdims=True) for x in small]
        st.out("small")[...] = jnp.concatenate(small + [jnp.zeros((5, width), F32)], axis=0)
        st.send("small")
        block_diagonal = pair_mask(WIDE)
        for b in range(blocks):
            lanes, wide = slice(b * PAIR, (b + 1) * PAIR), slice(b * WIDE, (b + 1) * WIDE)
            grown = tn(st["reading"][:, lanes], st.out("dw")[:, wide])
            st.out("gone")[b ^ 1] = jnp.where(block_diagonal, grown, 0.0).astype(BF16)
        st.send("gone")
        st.out("gwo")[...] = tn(st["mixed"][...], st.out("rgrad")[...]).astype(BF16)
        st.send("gwo")

    ins = dict(gain=gain, cols=Rows(cols, 0))
    ins.update(residual=Rows(residual, 0), dn2=Rows(dn2, 0), dy=Rows(dy, 0))
    for b, x in enumerate(wo):
        ins[f"wo{b}"] = (x, "wo", (slice(b * PAIR, (b + 1) * PAIR),))
    ins.update(inv=Rows(inv, 0), mixed=Rows(mixed, 0))
    ins.update({f"q{g}": Rows(x, 0) for g, x in enumerate(q)})
    outs = dict(
        rgrad=((tokens, width), BF16),
        dw=((tokens, 2 * width), BF16),
        gone=((blocks, PAIR, WIDE), BF16),
        gwo=((width, width), BF16),
        small=((8, width), F32),
    )
    scratch = dict(wo=((width, width), BF16), reading=((tokens, width), BF16))
    return staged(
        "unmix", body, ins, outs, scratch, 6 * tokens * width * width, 2 * chunks + 3
    )


def finish(residual, act, wr, bias):
    tokens, width = residual.shape

    def body(st):
        total = 0.0
        for i in range(len(wr)):
            total = total + nn(st[f"act{i}"][...], st[f"wr{i}"][...])
        out = st["residual"][...] + total + line(st["bias"])
        st.out("out")[...] = out.astype(BF16)
        st.send("out")

    ins, own = {}, []
    for x in act:
        own += [(x, slice(i, i + wr[0].shape[0])) for i in range(0, x.shape[1], wr[0].shape[0])]
    scratch = {}
    for i, (x, columns) in enumerate(own):
        scratch[f"part{i}"] = ((tokens, wr[i].shape[0]), BF16)
        ins[f"act{i}"] = (x, f"part{i}", (slice(None),), slice(None), columns)
        ins[f"wr{i}"] = wr[i]
    ins.update(residual=residual, bias=bias)
    outs = dict(out=((tokens, width), BF16))
    flops = 2 * tokens * width * width * len(wr)
    return staged("finish", body, ins, outs, scratch, flops, 1)["out"]


def attend_back_chunk(st, blocks, c):
    cols, rows = st.rows("cols", c), chunk_rows(c)
    reads, reads_far = column(cols, READ_CHUNK), column(cols, READ_HALF)
    in_last = column(cols, IN_LAST)
    carried = cols[0:1, CARRIED : CARRIED + 1]
    mask = allowed_mask(column(cols, DOC), st["doc_row"][:, rows])
    here = head_lanes((CHUNK, PAIR))
    block_diagonal = pair_mask(WIDE)
    share = jnp.full((CHUNK, PAIR), 1.0 / HEAD_DIM, BF16)
    once = lax.broadcasted_iota(jnp.int32, (PAIR, WIDE), 1) < PAIR
    once = jnp.where(once, 1.0, 1.0 / HEAD_DIM).astype(BF16)
    out, state = st.out("pgrads"), st["state"]
    every = range(blocks)
    own = [here, jnp.logical_not(here)]
    mask2 = jnp.concatenate([mask, mask], axis=0)
    own_wide = [jnp.concatenate([o, o], axis=1) for o in own]
    pick = lambda x: jnp.where(here, x[:CHUNK], x[CHUNK:])
    q, k, v = ([st.rows(x, c)[b] for b in every] for x in ("q", "k", "v"))
    dw = st.rows("dw", c)
    dw = [dw[:, b * WIDE : (b + 1) * WIDE] for b in every]
    value_share = [jnp.concatenate([v[b], share], axis=1) for b in every]
    scores = [nt(stack(q[b], own), k[b]) for b in every]
    sgrad = [nt(stack(dw[b], own_wide), value_share[b]) for b in every]
    q_t = [q[b].T for b in every]
    dw_t = [dw[b][:, :PAIR].T for b in every]
    scores = [jnp.where(mask2, scores[b], 0.0).astype(BF16) for b in every]
    sgrad = [jnp.where(mask2, sgrad[b], 0.0).astype(BF16) for b in every]
    low = [state[b].astype(BF16) for b in every]
    dq = [reads_far * nt(dw[b], st["come"][b] * once) for b in every]
    if c > 0:
        dq = [dq[b] + reads * nt(dw[b], st["held"][c, b] * once) for b in every]
    dq = [dq[b] + pick(nn(sgrad[b], k[b])) for b in every]
    dk, dv = [], []
    for b in every:
        for out_t, left, right in ((dk, q_t[b], sgrad[b]), (dv, dw_t[b], scores[b])):
            both = []
            for h in range(2):
                feats = slice(h * HEAD_DIM, (h + 1) * HEAD_DIM)
                both.append(nn(left[feats], right[h * CHUNK : (h + 1) * CHUNK]))
            out_t.append(jnp.concatenate(both, axis=0).T)
    for b in every:
        dk_b = dk[b] + in_last * nt(value_share[b], low[b])
        dv_b = dv[b] + in_last * nn(k[b], low[b][:, :PAIR])
        at = 3 * b * PAIR
        dq_b = dq[b] * jnp.minimum(q[b].astype(F32), 1.0)
        dk_b = dk_b * jnp.minimum(k[b].astype(F32), 1.0)
        out[rows, at : at + PAIR] = dq_b.astype(BF16)
        out[rows, at + PAIR : at + 2 * PAIR] = dk_b.astype(BF16)
        out[rows, at + 2 * PAIR : at + 3 * PAIR] = dv_b.astype(BF16)
        if c > 0:
            grown = tn(q[b] * reads.astype(BF16), dw[b])
            state[b] = carried * state[b] + jnp.where(block_diagonal, grown, 0.0)
    st.send("pgrads", rows)


class PieceRows:
    def __init__(self, out, rows_one, rows_two, pieces):
        self.out, self.one, self.two = out, rows_one // pieces, rows_two // pieces

    def write(self, at, rows, share, offset):
        done, total = 0, rows.shape[0]
        while done < total:
            piece, inside = divmod(at + done, share)
            take = min(total - done, share - inside)
            start = piece * (self.one + self.two) + offset + inside
            self.out[start : start + take, :] = rows[done : done + take, :]
            done += take

    def first(self, at, rows):
        self.write(at, rows, self.one, 0)

    def second(self, at, rows):
        self.write(at, rows, self.two, self.one)


def attend_back(pieces, first, dw, gone, part, come, cols, doc_row, n1, gwo):
    tokens, width = n1.shape
    blocks, chunks = part["q"].shape[0], tokens // CHUNK

    def body(st):
        flag = st.rows("cols", chunks - 1)[0:1, FIRST_HALF : FIRST_HALF + 1]
        for b in range(blocks):
            st["state"][b] = st["gone"][first + b].astype(F32) * flag
        for c in reversed(range(chunks)):
            attend_back_chunk(st, blocks, c)
        for b in range(blocks):
            grad = tn(st["n1"][...], st.out("pgrads")[:, 3 * b * PAIR : 3 * (b + 1) * PAIR])
            grad = grad.astype(BF16)
            block = st["gwo"][b * PAIR : (b + 1) * PAIR, :]
            fill = PieceRows(st.out(f"grad{b}"), 3 * width, width, pieces)
            for p in range(3):
                fill.first(p * width, grad[:, p * PAIR : (p + 1) * PAIR])
            for j in range(width // PAIR):
                fill.second(j * PAIR, block[:, j * PAIR : (j + 1) * PAIR])
            st.send(f"grad{b}")

    ins = dict(doc_row=doc_row, gone=gone, come=come, held=part["held"])
    ins.update({x: Rows(part[x], chunks - 1) for x in ("q", "k", "v")})
    ins.update(cols=Rows(cols, chunks - 1))
    ins.update(dw=Rows(dw, chunks - 1, slice(first * WIDE, (first + blocks) * WIDE)), n1=n1)
    own = slice(first * PAIR, (first + blocks) * PAIR)
    ins.update(gwo=(gwo, "gwo", (slice(None),), own))
    outs = dict(pgrads=((tokens, 3 * blocks * PAIR), BF16))
    for b in range(blocks):
        outs[f"grad{b}"] = ((4 * width, PAIR), BF16)
    scratch = dict(state=((blocks, PAIR, WIDE), F32), gwo=((blocks * PAIR, width), BF16))
    flops = 2 * tokens * blocks * PAIR * (3 * width + 12 * CHUNK)
    return staged("attend_back", body, ins, outs, scratch, flops, chunks + blocks)


def input_back(tok, rgrad, pgrads, gain, w):
    tokens, width = tok.shape
    blocks, chunks = len(w), tokens // CHUNK

    def body(st):
        for key in w_keys:
            st[key]
        gain = line(st["gain"])
        one = two = 0.0
        for c in range(chunks):
            rows = chunk_rows(c)
            both = jnp.concatenate([st.rows(f"pgrads{g}", c) for g in range(len(pgrads))], axis=1)
            grad = nt(both, st["w"][...])
            xhat, rstd = normalise(st.rows("tok", c).astype(F32))
            st.out("out")[rows, :] = st.rows("rgrad", c).astype(F32) + norm_back(grad, xhat, rstd, gain)
            st.send("out", rows)
            one, two = one + eight(grad * xhat), two + eight(grad)
        small = [jnp.sum(x, axis=0, keepdims=True) for x in (one, two)]
        st.out("small")[...] = jnp.concatenate(small + [jnp.zeros((6, width), F32)], axis=0)
        st.send("small")

    ins, w_keys = {}, []
    for b in range(blocks):
        for p in range(3):
            at = (3 * b + p) * PAIR
            w_keys.append(f"w{b}_{p}")
            ins[w_keys[-1]] = (w[b], "w", (slice(None), slice(at, at + PAIR)), p)
    ins.update({f"pgrads{g}": Rows(x, 0) for g, x in enumerate(pgrads)})
    ins.update(gain=gain, tok=Rows(tok, 0), rgrad=Rows(rgrad, 0))
    outs = dict(out=((tokens, width), F32), small=((8, width), F32))
    scratch = dict(w=((width, 3 * blocks * PAIR), BF16))
    return staged(
        "input_back", body, ins, outs, scratch, 6 * tokens * width * width, chunks + 1
    )


def swap(x, axis, size, bit):
    return lax.ppermute(x, axis, [(i, i ^ bit) for i in range(size)])


def tie(x, *others):
    return lax.optimization_barrier((x, *others))[0]


def gate(*xs):
    return lax.optimization_barrier(xs)


def add(a, b):
    return (a.astype(F32) + b.astype(F32)).astype(BF16)


def cut(x, like):
    at, out = 0, []
    for y in like:
        out.append(x[at : at + y.shape[0]])
        at += y.shape[0]
    return out


def half(x, which):
    rows = x.shape[0] // 2
    return lax.dynamic_slice_in_dim(x, which * rows, rows, 0)


def join(x, other, side):
    return jnp.where(side == 0, jnp.concatenate([x, other]), jnp.concatenate([other, x]))


def lockstep(*chains):
    results, sent = [None] * len(chains), {}
    for i, chain in enumerate(chains):
        sent[i] = next(chain)
    while sent:
        flat, tree = jax.tree.flatten(sent)
        sent = jax.tree.unflatten(tree, gate(*flat))
        for i in list(sent):
            try:
                sent[i] = chains[i].send(sent[i])
            except StopIteration as stop:
                results[i] = stop.value
                del sent[i]
    return results


def body(
    dp,
    head,
    tokens,
    doc_ids,
    pad_mask,
    norm1_gain,
    norm1_shift,
    w_qkv,
    w_out,
    norm2_gain,
    norm2_shift,
    w_hidden,
    hidden_bias,
    w_return,
    return_bias,
    out_grad,
):
    count, width = tokens.shape
    pieces = dp // 2
    core = lambda x: swap(x, "head", head, 1)
    cross = lambda x: swap(x, "head", head, 2)
    bits = dp.bit_length() - 1
    spot = lax.axis_index("dp")
    side = [(spot >> b) & 1 for b in range(bits)]
    along = lambda x, b: swap(x, "dp", dp, 1 << b)

    def leave(xs, b):
        return along(jnp.concatenate([half(x, 1 - side[b]) for x in xs]), b)

    def meet(xs, b, got):
        halves = [half(x, side[b]) for x in xs]
        return [add(x, y) for x, y in zip(halves, cut(got, halves))]

    def rest_of(xs):
        for b in range(2, bits - 1):
            xs = meet(xs, b, leave(xs, b))
        return xs

    def unfold(x, other, *shares):
        shape = (pieces // 2, -1, x.shape[1])
        low = jnp.where(side[0] == 0, x, other).reshape(shape)
        high = jnp.where(side[0] == 0, other, x).reshape(shape)
        at, out = 0, []
        for share in shares:
            parts = [y[:, at : at + share].reshape(-1, x.shape[1]) for y in (low, high)]
            out.append(jnp.concatenate(parts).astype(F32))
            at += share
        return out

    wq, wo, wr = ([x, core(x), cross(x)] for x in (w_qkv, w_out, w_return))

    near = open_layer(
        doc_ids, pad_mask, tokens, norm1_gain, norm1_shift, wq[:2], w_hidden, hidden_bias
    )
    n1, cols, doc_row = near["n1"], near["cols"], near["doc_row"]
    wh = [near["wh"], core(near["wh"]), cross(near["wh"])]
    n1, wq[2], wo[2] = gate(n1, wq[2], wo[2])
    wq.append(core(wq[2]))
    wo.append(core(wo[2]))
    come_near = core(near["last"])
    far = attend(n1, wq[2:], cols, doc_row)
    come = [come_near, core(far["last"])]
    mid = mix_feed(
        pieces,
        tokens,
        out_grad,
        [near, far],
        come,
        wo,
        cols,
        norm2_gain,
        norm2_shift,
        wh[:2],
        wr[:2],
    )
    down1, up1 = core(mid["down1"]), core(mid["up1"])
    wh.append(core(tie(wh[2], mid["n2"])))
    wr.append(core(tie(wr[2], mid["n2"])))
    end = feed(pieces, mid["n2"], out_grad, wh[2:], wr[2:], mid["dn2"])

    down3, up3, down1, up1 = gate(end["down1"], end["up1"], down1, up1)
    down3, up3 = core(down3), core(up3)
    down0, up0 = add(mid["down0"], down1), add(mid["up0"], up1)
    down2, up2 = add(end["down0"], down3), add(end["up0"], up3)

    ups, down_wire = [up0, up2], cross(down2)
    ups_wire = leave(ups, 0)
    back = unmix(
        end["dn2"],
        mid["residual"],
        out_grad,
        mid["mixed"],
        mid["inv"],
        wo,
        [near["q"], far["q"]],
        cols,
        tie(norm2_gain, down3, up3),
    )
    gone, down_wire = gate(back["gone"], down_wire)
    gone = core(gone)
    down = [add(down0, down_wire)]
    down_wire = leave(down, 0)
    args = cols, doc_row, n1, back["gwo"]
    side_b = attend_back(pieces, 2, back["dw"], gone, far, come[1], *args)
    grad3, down_wire, ups_wire = gate(side_b["grad1"], down_wire, ups_wire)
    grad3 = core(grad3)
    down, ups = meet(down, 0, down_wire), meet(ups, 0, ups_wire)
    down_wire, ups_wire = leave(down, 1), leave(ups, 1)
    grad2 = add(side_b["grad0"], grad3)
    grad_wire = cross(grad2)
    args = cols, tie(doc_row, grad3), n1, back["gwo"]
    side_a = attend_back(pieces, 0, back["dw"], gone, near, come[0], *args)
    grad1, down_wire, ups_wire, grad_wire = gate(
        side_a["grad1"], down_wire, ups_wire, grad_wire
    )
    grad1 = core(grad1)
    (down,) = rest_of(meet(down, 1, down_wire))
    ups = rest_of(meet(ups, 1, ups_wire))
    down_wire, up_wire = along(down, bits - 1), cross(ups[1])
    grad = [add(add(side_a["grad0"], grad1), grad_wire)]
    grad_wire = leave(grad, 0)
    last = input_back(
        tokens,
        back["rgrad"],
        [side_a["pgrads"], side_b["pgrads"]],
        tie(norm1_gain, grad1),
        wq,
    )
    small, down_wire, up_wire, grad_wire = gate(last["small"], down_wire, up_wire, grad_wire)
    down, up, grad = add(down, down_wire), add(ups[0], up_wire), meet(grad, 0, grad_wire)

    def spread(xs, *shares):
        for b in reversed(range(1, bits - 1)):
            got = yield along(jnp.concatenate(xs), b)
            xs = [join(x, y, side[b]) for x, y in zip(xs, cut(got, xs))]
        got = yield along(jnp.concatenate(xs), 0)
        return [unfold(x, y, *s) for x, y, s in zip(xs, cut(got, xs), shares)]

    def finish_up(x):
        got = yield along(x, bits - 1)
        return (yield from spread([add(x, got)], (width // pieces, 16)))

    def finish_output(after):
        for _ in range(after):
            yield []
        out = finish(mid["residual"], [mid["act"], end["act"]], wr, return_bias)
        return (yield out)

    def finish_grad(xs):
        for b in range(1, bits - 1):
            got = yield leave(xs, b)
            xs = meet(xs, b, got)
        got = yield along(xs[0], bits - 1)
        return (yield from spread([add(xs[0], got)], (3 * width // pieces, width // pieces)))

    def finish_small(x):
        for axis, size in (("head", head), ("dp", dp)):
            for b in range(size.bit_length() - 1):
                got = yield swap(x, axis, size, 1 << b)
                x = x + got
        return x

    small = jnp.concatenate([small[:2], back["small"][:3]])
    (grads,), (downs,), (ups,), output, small = lockstep(
        finish_grad(grad),
        spread([down], (width // pieces,)),
        finish_up(up),
        finish_output(1),
        finish_small(small),
    )
    g_qkv, g_out = grads
    (down,), (up, bias_grad) = downs, ups
    g_out = g_out.reshape(width // PAIR, PAIR, PAIR)
    g_out = jnp.concatenate([g_out[i] for i in range(width // PAIR)], axis=1)
    return (
        output,
        last["out"],
        small[0],
        small[1],
        g_qkv.reshape(3, width, PAIR),
        g_out,
        small[2],
        small[3],
        up,
        bias_grad[0],
        down,
        small[4],
    )


def solution(mesh):
    return jax.shard_map(
        functools.partial(body, mesh.shape["dp"], mesh.shape["head"]),
        mesh=mesh,
        in_specs=(
            P(("dp", "head"), None),
            P("dp", None),
            P("dp", None),
            P(),
            P(),
            P(None, None, "head"),
            P("head", None),
            P(),
            P(),
            P(None, "head"),
            P("head"),
            P("head", None),
            P(),
            P(("dp", "head"), None),
        ),
        out_specs=(
            P(("dp", "head"), None),
            P(("dp", "head"), None),
            P(),
            P(),
            P(None, None, "head"),
            P("head", None),
            P(),
            P(),
            P(None, "head"),
            P("head"),
            P("head", None),
            P(),
        ),
        check_vma=False,
    )
```

```python
import functools

import jax
import jax.numpy as jnp
from jax import lax
from jax.experimental import pallas as pl
from jax.experimental.pallas import tpu as pltpu
from jax.sharding import PartitionSpec as P

HEAD_DIM = 64
PAIR = 2 * HEAD_DIM
WIDE = 2 * PAIR
CHUNK = 256
LANES = 128
EPSILON = 1e-05
BELOW_ONE = 1.0 - 2.0**-8
F32 = jnp.float32
BF16 = jnp.bfloat16
VMEM_BYTES = 60 * 1024 * 1024

DOC, LIVE, READ_HALF, READ_CHUNK, IN_LAST, CARRIED, FIRST_HALF = range(7)


def nn(a, b):
    return lax.dot_general(a, b, (((1,), (0,)), ((), ())), preferred_element_type=F32)


def nt(a, b):
    return lax.dot_general(a, b, (((1,), (1,)), ((), ())), preferred_element_type=F32)


def tn(a, b):
    return lax.dot_general(a, b, (((0,), (0,)), ((), ())), preferred_element_type=F32)


def normalise(x):
    centre = x - jnp.mean(x, axis=-1, keepdims=True)
    rstd = lax.rsqrt(jnp.mean(centre * centre, axis=-1, keepdims=True) + EPSILON)
    return centre * rstd, rstd


def norm_back(grad, xhat, rstd, gain):
    scaled = grad * gain
    mean_one = jnp.mean(scaled, axis=-1, keepdims=True)
    mean_two = jnp.mean(scaled * xhat, axis=-1, keepdims=True)
    return rstd * (scaled - mean_one - xhat * mean_two)


def line(ref):
    return ref[...].astype(F32).reshape(1, ref.shape[0])


def eight(x):
    return jnp.sum(x.reshape(x.shape[0] // 8, 8, x.shape[1]), axis=0)


def head_lanes(shape):
    return lax.broadcasted_iota(jnp.int32, shape, len(shape) - 1) % PAIR < HEAD_DIM


def pair_mask(width):
    rows = lax.broadcasted_iota(jnp.int32, (PAIR, width), 0) < HEAD_DIM
    return rows == head_lanes((PAIR, width))


def allowed_mask(doc_col, doc_row):
    t = lax.broadcasted_iota(jnp.int32, (CHUNK, CHUNK), 0)
    s = lax.broadcasted_iota(jnp.int32, (CHUNK, CHUNK), 1)
    return (doc_col == doc_row) & (s <= t)


def feature(x):
    return jnp.where(x > 0, x + 1.0, jnp.exp(jnp.minimum(x, 0.0)))


def chunk_rows(c):
    return slice(c * CHUNK, (c + 1) * CHUNK)


def column(cols, which):
    return cols[:, which : which + 1]


def stack(x, masks):
    return jnp.concatenate([jnp.where(mask, x, jnp.zeros_like(x)) for mask in masks], axis=0)


class Rows:
    def __init__(self, array, first, columns=None):
        self.array = array
        self.columns = columns or slice(0, array.shape[-1])
        self.shape = array.shape[:-1] + (self.columns.stop - self.columns.start,)
        rows = self.shape[-2]
        rest = slice(CHUNK, rows) if first == 0 else slice(0, rows - CHUNK)
        self.first, self.parts = first, [chunk_rows(first), rest]

    def index(self, rows, columns):
        return (slice(None),) * (len(self.shape) - 2) + (rows, columns)


class Staged:
    def __init__(self, specs, late, ins, outs, scratch, in_sem, out_sem):
        self.specs, self.ins, self.outs, self.scratch = specs, ins, outs, scratch
        self.out_sem, self.sent = out_sem, []
        self.pending = {}
        begin = list(ins)[: len(ins) - late]
        for turn, names in enumerate((begin, begin, list(ins)[len(ins) - late :])):
            for name in names:
                spec, (src, dst) = specs[name], ins[name]
                if isinstance(spec, Rows):
                    rows = spec.parts[turn]
                    src = src.at[spec.index(rows, spec.columns)]
                    dst = dst.at[spec.index(rows, slice(None))]
                elif turn == 1:
                    continue
                copy = pltpu.make_async_copy(src, dst, in_sem.at[len(self.pending)])
                copy.start()
                self.pending[name, turn % 2] = copy

    def __getitem__(self, name):
        for key in [key for key in self.pending if key[0] == name]:
            self.pending.pop(key).wait()
        return self.ins[name][1] if name in self.ins else self.scratch[name]

    def rows(self, name, c):
        spec = self.specs[name]
        if not isinstance(spec, Rows):
            return self[name][chunk_rows(c), :]
        key = (name, int(c != spec.first))
        if key in self.pending:
            self.pending.pop(key).wait()
        return self.ins[name][1][spec.index(chunk_rows(c), slice(None))]

    def out(self, name):
        return self.outs[name][1]

    def send(self, name, *index):
        dst, src = self.outs[name]
        if index:
            dst, src = dst.at[index], src.at[index]
        copy = pltpu.make_async_copy(src, dst, self.out_sem.at[len(self.sent)])
        copy.start()
        self.sent.append(copy)

    def finish(self):
        for copy in list(self.pending.values()) + self.sent:
            copy.wait()


def staged(name, body, ins, outs, scratch, flops, sends, late=0):
    in_names, out_names, scratch_names = list(ins), list(outs), list(scratch)
    arrays, in_specs, own = [], [], []
    for value in ins.values():
        value = value.array if isinstance(value, Rows) else value
        arrays.append(value[0] if isinstance(value, tuple) else value)
        in_specs.append(pl.BlockSpec(memory_space=pl.ANY))
        if not isinstance(value, tuple):
            own.append(pltpu.VMEM(ins[in_names[len(arrays) - 1]].shape, value.dtype))

    def kernel(*refs):
        refs = list(refs)
        take = lambda n: [refs.pop(0) for _ in range(n)]
        src, dst = take(len(in_names)), take(len(out_names))
        own_refs, out_refs = take(len(own)), take(len(out_names))
        held = dict(zip(scratch_names, take(len(scratch_names))))
        in_sem, out_sem = refs
        ends = {}
        for key, ref in zip(in_names, src):
            value = ins[key]
            if not isinstance(value, tuple):
                ends[key] = (ref, own_refs.pop(0))
            else:
                ends[key] = (ref.at[value[3:]] if value[3:] else ref, held[value[1]].at[value[2]])
        stage = Staged(ins, late, ends, dict(zip(out_names, zip(dst, out_refs))), held, in_sem, out_sem)
        body(stage)
        stage.finish()

    shapes = list(outs.values())
    copies = sum(2 if isinstance(x, Rows) else 1 for x in ins.values())
    out = pl.pallas_call(
        kernel,
        in_specs=in_specs,
        out_specs=[pl.BlockSpec(memory_space=pl.ANY)] * len(out_names),
        out_shape=[jax.ShapeDtypeStruct(*s) for s in shapes],
        scratch_shapes=own
        + [pltpu.VMEM(*s) for s in shapes]
        + [pltpu.VMEM(*s) for s in scratch.values()]
        + [pltpu.SemaphoreType.DMA((copies,)), pltpu.SemaphoreType.DMA((sends,))],
        compiler_params=pltpu.CompilerParams(vmem_limit_bytes=VMEM_BYTES),
        cost_estimate=pl.CostEstimate(flops=flops, bytes_accessed=4 << 20, transcendentals=0),
        name=name,
    )(*arrays)
    return dict(zip(out_names, out))


def attend_chunk(st, blocks, c, n1, cols, doc_row):
    w, state, every = st["w"], st["state"], range(blocks)
    rows = chunk_rows(c)
    live, reads = column(cols, LIVE), column(cols, READ_CHUNK)
    in_last = column(cols, IN_LAST).astype(BF16)
    carried = cols[0:1, CARRIED : CARRIED + 1]
    mask = allowed_mask(column(cols, DOC), doc_row[:, rows])
    mask = jnp.concatenate([mask, mask], axis=0)
    q_all = feature(nn(n1, w[0])).astype(BF16)
    k_all = (feature(nn(n1, w[1])) * live).astype(BF16)
    v_all = nn(n1, w[2]).astype(BF16)
    here = head_lanes((CHUNK, WIDE))
    own = [here[:, :PAIR], jnp.logical_not(here[:, :PAIR])]
    block_diagonal = pair_mask(WIDE)
    ones = jnp.ones((CHUNK, PAIR), BF16)
    part = lambda x, b: x[:, b * PAIR : (b + 1) * PAIR]
    q, k, v = ([part(x, b) for b in every] for x in (q_all, k_all, v_all))
    for b in every:
        st.out("q")[b, rows], st.out("k")[b, rows], st.out("v")[b, rows] = q[b], k[b], v[b]
    scores = [nt(stack(q[b], own), k[b]) for b in every]
    wide = [jnp.concatenate([v[b], ones], axis=1) for b in every]
    grown = [tn(k[b] * in_last, wide[b]) for b in every]
    scores = [jnp.where(mask, scores[b], 0.0).astype(BF16) for b in every]
    both = [nn(scores[b], wide[b]) for b in every]
    total = [jnp.where(here, both[b][:CHUNK], both[b][CHUNK:]) for b in every]
    for b in every:
        if c > 0:
            low = state[b].astype(BF16)
            st.out("held")[c, b] = low
            total[b] = total[b] + reads * nn(q[b], low)
        else:
            st.out("held")[c, b] = jnp.zeros((PAIR, WIDE), BF16)
        st.out("num")[b, rows], st.out("tot")[b, rows] = total[b][:, :PAIR], total[b][:, PAIR:]
        more = jnp.where(block_diagonal, grown[b], 0.0)
        state[b] = more if c == 0 else carried * state[b] + more
    for name in ("q", "k", "v", "num", "tot"):
        st.send(name, slice(None), rows)


def attend_finish(st, blocks):
    for b in range(blocks):
        st.out("last")[b ^ 1] = st["state"][b].astype(BF16)
    st.send("last")
    st.send("held")


def attend_outs(tokens, blocks):
    part = (blocks, tokens, PAIR)
    return dict(
        q=(part, BF16),
        k=(part, BF16),
        v=(part, BF16),
        num=(part, F32),
        tot=(part, F32),
        held=((tokens // CHUNK, blocks, PAIR, WIDE), BF16),
        last=((blocks, PAIR, WIDE), BF16),
    )


def attend_scratch(width, blocks):
    return dict(w=((3, width, blocks * PAIR), BF16), state=((blocks, PAIR, WIDE), F32))


def attend_weights(w):
    everything = slice(None)
    return {
        f"w{b}": (x, "w", (everything, everything, slice(b * PAIR, (b + 1) * PAIR)))
        for b, x in enumerate(w)
    }


def attend_flops(tokens, width, blocks):
    return 2 * tokens * blocks * PAIR * (3 * width + 4 * CHUNK)


def make_flags(doc_ids, pad_mask, count):
    halves = doc_ids.shape[1] // count
    me = lax.axis_index("head")
    row, place = lax.div(me, halves), lax.rem(me, halves)

    def here(x):
        whole = x[0:1, :]
        for r in range(1, x.shape[0]):
            whole = jnp.where(row == r, x[r : r + 1, :], whole)
        part = whole[:, :count]
        for i in range(1, x.shape[1] // count):
            part = jnp.where(place == i, whole[:, i * count : (i + 1) * count], part)
        return whole, part

    whole, docs = here(doc_ids)
    _, live = here(pad_mask)
    edge = whole[:, count - 1 : count]
    second = jnp.where(place > 0, 1.0, 0.0)
    as_float = lambda x: jnp.where(x, 1.0, 0.0)
    reads, in_last, carried = [], [], []
    before = None
    for c in range(count // CHUNK):
        part = docs[:, chunk_rows(c)]
        end = part[:, CHUNK - 1 : CHUNK]
        in_last.append(as_float(part == end))
        if before is None:
            reads.append(jnp.zeros((1, CHUNK), F32))
            carried.append(jnp.zeros((1, CHUNK), F32))
        else:
            reads.append(as_float(part == before))
            carried.append(as_float(jnp.broadcast_to(end, part.shape) == before))
        before = end
    join = lambda x: jnp.concatenate(x, axis=1)
    doc_line = docs.astype(F32)
    lines = [
        doc_line,
        live.astype(F32),
        as_float(docs == edge) * second,
        join(reads),
        join(in_last),
        join(carried),
        jnp.broadcast_to(1.0 - second, (1, count)).astype(F32),
    ]
    lines.append(jnp.zeros((LANES - len(lines), count), F32))
    return jnp.concatenate(lines, axis=0).T, doc_line


def open_layer(doc_ids, pad_mask, tok, gain, shift, w, w_hidden, hidden_bias):
    tokens, width = tok.shape
    blocks, chunks, hidden = len(w), tokens // CHUNK, w_hidden.shape[1]

    def body(st):
        cols, doc_row = make_flags(st["doc_ids"], st["pad_mask"], tokens)
        st.out("cols")[...], st.out("doc_row")[...] = cols, doc_row
        st.send("cols")
        st.send("doc_row")
        cols, doc_row, n1 = st.out("cols"), st.out("doc_row"), st.out("n1")
        gain, shift = line(st["gain"]), line(st["shift"])
        for c in range(chunks):
            xhat, _ = normalise(st.rows("tok", c).astype(F32))
            n1[chunk_rows(c), :] = (xhat * gain + shift).astype(BF16)
        st.send("n1")
        for b in range(blocks):
            st[f"w{b}"]
        for c in range(chunks):
            attend_chunk(st, blocks, c, n1[chunk_rows(c), :], cols[chunk_rows(c), :], doc_row)
        attend_finish(st, blocks)
        st["wh"][width:, :] = jnp.broadcast_to(line(st["bias"]).astype(BF16), (16, hidden))
        st["w_hidden"]
        st.out("wh")[...] = st["wh"][...]
        st.send("wh")

    ins = dict(doc_ids=doc_ids, pad_mask=pad_mask, tok=Rows(tok, 0))
    ins.update(gain=gain, shift=shift, **attend_weights(w), bias=hidden_bias)
    ins.update(w_hidden=(w_hidden, "wh", (slice(0, width),)))
    outs = dict(
        cols=((tokens, LANES), F32),
        doc_row=((1, tokens), F32),
        n1=((tokens, width), BF16),
        wh=((width + 16, hidden), BF16),
    )
    outs.update(attend_outs(tokens, blocks))
    scratch = attend_scratch(width, blocks)
    scratch["wh"] = ((width + 16, hidden), BF16)
    flops = attend_flops(tokens, width, blocks)
    return staged("open", body, ins, outs, scratch, flops, 5 * chunks + 6, 1)


def attend(n1, w, cols, doc_row):
    tokens, width = n1.shape
    blocks, chunks = len(w), tokens // CHUNK

    def body(st):
        doc_row = st["doc_row"]
        for b in range(blocks):
            st[f"w{b}"]
        for c in range(chunks):
            attend_chunk(st, blocks, c, st.rows("n1", c), st.rows("cols", c), doc_row)
        attend_finish(st, blocks)

    ins = dict(doc_row=doc_row, **attend_weights(w))
    ins.update(n1=Rows(n1, 0), cols=Rows(cols, 0))
    flops = attend_flops(tokens, width, blocks)
    return staged(
        "attend",
        body,
        ins,
        attend_outs(tokens, blocks),
        attend_scratch(width, blocks),
        flops,
        5 * chunks + 2,
    )


def gelu_pair(x):
    cdf = 0.5 + 0.5 * lax.erf(x * 0.7071067811865476)
    density = 0.3989422804014327 * jnp.exp(-0.5 * x * x)
    return x * cdf, cdf + x * density


def mix_chunk(st, groups, c):
    cols, w, rows = st.rows("cols", c), st["wo"], chunk_rows(c)
    live, reads = column(cols, LIVE), column(cols, READ_HALF)
    q, num, tot = ([st.rows(f"{x}{g}", c) for g in range(groups)] for x in ("q", "num", "tot"))
    mixed, inv_out = st.out("mixed"), st.out("inv")
    for b in range(2 * groups):
        g, i = divmod(b, 2)
        lanes = slice(b * PAIR, (b + 1) * PAIR)
        far = reads * nn(q[g][i], st[f"come{g}"][i])
        inv = 1.0 / jnp.maximum(tot[g][i] + far[:, PAIR:], 1.0)
        inv_out[rows, lanes] = jnp.where(inv < 1.0, jnp.minimum(inv, BELOW_ONE), 1.0).astype(BF16)
        value = (num[g][i] + far[:, :PAIR]) * inv * live
        mixed[rows, lanes] = value.astype(BF16)
    residual = st.rows("tok", c).astype(F32) + nn(mixed[rows, :], w[...])
    st.out("residual")[rows, :] = residual
    xhat, _ = normalise(residual)
    n2 = (xhat * line(st["gain"]) + line(st["shift"])).astype(BF16)
    st.out("n2")[rows, :] = n2
    for name in ("mixed", "inv", "residual", "n2"):
        st.send(name, rows)


def feed_chunk(st, c, n2, bias, resume):
    rows = chunk_rows(c)
    wh, wr = st["wh"].at[: n2.shape[1]], st["wr"]
    value, slope = gelu_pair(nn(n2, wh[...]) + bias)
    st.out("act")[rows, :] = value.astype(BF16)
    st.send("act", rows)
    grad = nt(st.rows("dy", c), wr[...]) * slope
    low = grad.astype(BF16)
    st["hg"][rows, :] = low
    back = nt(low, wh[...])
    st.out("dn2")[rows, :] = back + st.rows("dn2_in", c) if resume else back
    st.send("dn2", rows)
    return eight(grad)


def feed_grads(st, blocks, pieces, n2, bias_grad):
    width, hidden = n2.shape[1], bias_grad.shape[1] // blocks
    bias_grad = jnp.sum(bias_grad, axis=0, keepdims=True).astype(BF16)
    for b in range(blocks):
        part = slice(b * hidden, (b + 1) * hidden)
        down, up = st.out(f"down{b}"), st.out(f"up{b}")
        down[...] = tn(st.out("act")[:, part], st["dy"][...]).astype(BF16)
        st.send(f"down{b}")
        grad = tn(n2[...], st["hg"][:, part]).astype(BF16)
        rows, step = width // pieces, up.shape[0] // pieces
        for i in range(pieces):
            up[i * step : i * step + rows, :] = grad[i * rows : (i + 1) * rows, :]
            tail = jnp.broadcast_to(bias_grad[:, part], (step - rows, hidden))
            up[i * step + rows : (i + 1) * step, :] = tail
        st.send(f"up{b}")


def feed_parts(tokens, width, pieces, wh, wr):
    blocks, hidden = len(wr), wr[0].shape[0]
    everything = slice(None)
    ins = {}
    for b in range(blocks):
        part = slice(b * hidden, (b + 1) * hidden)
        ins[f"wh{b}"] = (wh[b], "wh", (everything, part))
        ins[f"wr{b}"] = (wr[b], "wr", (part, everything))
    outs = dict(act=((tokens, blocks * hidden), BF16), dn2=((tokens, width), F32))
    for b in range(blocks):
        outs[f"down{b}"] = ((hidden, width), BF16)
        outs[f"up{b}"] = ((width + 16 * pieces, hidden), BF16)
    scratch = dict(
        wh=((width + 16, blocks * hidden), BF16),
        wr=((blocks * hidden, width), BF16),
        hg=((tokens, blocks * hidden), BF16),
    )
    return ins, outs, scratch, 10 * tokens * width * hidden * blocks


def feed_start(st, blocks, width):
    for b in range(blocks):
        st[f"wh{b}"], st[f"wr{b}"]
    return st["wh"][width : width + 1, :].astype(F32)


def mix_feed(pieces, tok, dy, parts, come, wo, cols, gain, shift, wh, wr):
    tokens, width = tok.shape
    blocks, groups, chunks = len(wh), len(parts), tokens // CHUNK

    def body(st):
        for b in range(2 * groups):
            st[f"wo{b}"]
        for c in range(chunks):
            mix_chunk(st, groups, c)
        n2 = st.out("n2")
        bias = feed_start(st, blocks, width)
        bias_grad = 0.0
        for c in range(chunks):
            bias_grad = bias_grad + feed_chunk(st, c, n2[chunk_rows(c), :], bias, False)
        feed_grads(st, blocks, pieces, n2, bias_grad)

    ins = dict(cols=Rows(cols, 0), tok=Rows(tok, 0), gain=gain, shift=shift)
    for g, part in enumerate(parts):
        ins.update({f"{x}{g}": Rows(part[x], 0) for x in ("q", "num", "tot")})
        ins[f"come{g}"] = come[g]
    for b, x in enumerate(wo):
        ins[f"wo{b}"] = (x, "wo", (slice(b * PAIR, (b + 1) * PAIR),))
    more, outs, scratch, flops = feed_parts(tokens, width, pieces, wh, wr)
    ins.update(dy=dy, **more)
    outs.update(
        mixed=((tokens, width), BF16),
        inv=((tokens, width), BF16),
        residual=((tokens, width), F32),
        n2=((tokens, width), BF16),
    )
    scratch["wo"] = ((width, width), BF16)
    late = 1 + len(more)
    return staged("mix_feed", body, ins, outs, scratch, 0, 6 * chunks + 2 * blocks, late)


def feed(pieces, n2, dy, wh, wr, dn2):
    tokens, width = n2.shape
    blocks, chunks = len(wh), tokens // CHUNK

    def body(st):
        bias = feed_start(st, blocks, width)
        bias_grad = 0.0
        for c in range(chunks):
            bias_grad = bias_grad + feed_chunk(st, c, st.rows("n2", c), bias, True)
        feed_grads(st, blocks, pieces, st["n2"], bias_grad)

    ins = dict(n2=n2)
    more, outs, scratch, flops = feed_parts(tokens, width, pieces, wh, wr)
    ins.update(more)
    ins.update(dy=dy, dn2_in=dn2)
    return staged("feed", body, ins, outs, scratch, flops, 2 * chunks + 2 * blocks)


def unmix_chunk(st, blocks, c):
    cols, rows = st.rows("cols", c), chunk_rows(c)
    live, reads = column(cols, LIVE), column(cols, READ_HALF).astype(BF16)
    xhat, rstd = normalise(st.rows("residual", c))
    grad = st.rows("dn2", c)
    wide = st.rows("dy", c).astype(F32)
    rgrad = wide + norm_back(grad, xhat, rstd, line(st["gain"]))
    low = rgrad.astype(BF16)
    st.out("rgrad")[rows, :] = low
    mgrad = nt(low, st["wo"][...]) * live
    sums = pair_mask(PAIR).astype(BF16)
    sums = jnp.concatenate([sums, sums], axis=0)
    inv, mixed = st.rows("inv", c).astype(F32), st.rows("mixed", c).astype(F32)
    q = [st.rows(f"q{g}", c) for g in range(blocks // 2)]
    for b in range(blocks):
        lanes = slice(b * PAIR, (b + 1) * PAIR)
        one, scale = mgrad[:, lanes], inv[:, lanes]
        dw = (one * scale).astype(BF16)
        terms = one * mixed[:, lanes]
        high = terms.astype(BF16)
        rest = (terms - high.astype(F32)).astype(BF16)
        total = nn(jnp.concatenate([high, rest], axis=1), sums)
        tg = jnp.where(scale < 1.0, -total * scale, 0.0).astype(BF16)
        st.out("dw")[rows, b * WIDE : b * WIDE + PAIR] = dw
        st.out("dw")[rows, b * WIDE + PAIR : (b + 1) * WIDE] = tg
        st["reading"][rows, lanes] = q[b // 2][b % 2] * reads
    st.send("rgrad", rows)
    st.send("dw", rows)
    return eight(grad * xhat), eight(grad), eight(wide)


def unmix(dn2, residual, dy, mixed, inv, wo, q, cols, gain):
    tokens, width = dy.shape
    blocks, chunks = len(wo), tokens // CHUNK

    def body(st):
        for b in range(blocks):
            st[f"wo{b}"]
        small = [0.0, 0.0, 0.0]
        for c in range(chunks):
            small = [a + b for a, b in zip(small, unmix_chunk(st, blocks, c))]
        small = [jnp.sum(x, axis=0, keepdims=True) for x in small]
        st.out("small")[...] = jnp.concatenate(small + [jnp.zeros((5, width), F32)], axis=0)
        st.send("small")
        block_diagonal = pair_mask(WIDE)
        for b in range(blocks):
            lanes, wide = slice(b * PAIR, (b + 1) * PAIR), slice(b * WIDE, (b + 1) * WIDE)
            grown = tn(st["reading"][:, lanes], st.out("dw")[:, wide])
            st.out("gone")[b ^ 1] = jnp.where(block_diagonal, grown, 0.0).astype(BF16)
        st.send("gone")
        st.out("gwo")[...] = tn(st["mixed"][...], st.out("rgrad")[...]).astype(BF16)
        st.send("gwo")

    ins = dict(gain=gain, cols=Rows(cols, 0))
    ins.update(residual=Rows(residual, 0), dn2=Rows(dn2, 0), dy=Rows(dy, 0))
    for b, x in enumerate(wo):
        ins[f"wo{b}"] = (x, "wo", (slice(b * PAIR, (b + 1) * PAIR),))
    ins.update(inv=Rows(inv, 0), mixed=Rows(mixed, 0))
    ins.update({f"q{g}": Rows(x, 0) for g, x in enumerate(q)})
    outs = dict(
        rgrad=((tokens, width), BF16),
        dw=((tokens, 2 * width), BF16),
        gone=((blocks, PAIR, WIDE), BF16),
        gwo=((width, width), BF16),
        small=((8, width), F32),
    )
    scratch = dict(wo=((width, width), BF16), reading=((tokens, width), BF16))
    return staged(
        "unmix", body, ins, outs, scratch, 6 * tokens * width * width, 2 * chunks + 3
    )


def finish(residual, act, wr, bias):
    tokens, width = residual.shape

    def body(st):
        total = 0.0
        for i in range(len(wr)):
            total = total + nn(st[f"act{i}"][...], st[f"wr{i}"][...])
        total = total + st["residual"][...] + line(st["bias"])
        st.out("out")[...] = total.astype(BF16)
        st.send("out")

    ins, own, scratch = {}, [], {}
    for x in act:
        own += [(x, slice(i, i + wr[0].shape[0])) for i in range(0, x.shape[1], wr[0].shape[0])]
    for i, (x, columns) in enumerate(own):
        scratch[f"part{i}"] = ((tokens, wr[i].shape[0]), BF16)
        ins[f"act{i}"] = (x, f"part{i}", (slice(None),), slice(None), columns)
        ins[f"wr{i}"] = wr[i]
    ins.update(residual=residual, bias=bias)
    outs = dict(out=((tokens, width), BF16))
    flops = 2 * tokens * width * width * len(wr)
    return staged("finish", body, ins, outs, scratch, flops, 1)["out"]


def attend_back_chunk(st, blocks, c):
    cols, rows = st.rows("cols", c), chunk_rows(c)
    reads, reads_far = column(cols, READ_CHUNK), column(cols, READ_HALF)
    in_last = column(cols, IN_LAST)
    carried = cols[0:1, CARRIED : CARRIED + 1]
    mask = allowed_mask(column(cols, DOC), st["doc_row"][:, rows])
    here = head_lanes((CHUNK, PAIR))
    block_diagonal = pair_mask(WIDE)
    share = jnp.full((CHUNK, PAIR), 1.0 / HEAD_DIM, BF16)
    once = lax.broadcasted_iota(jnp.int32, (PAIR, WIDE), 1) < PAIR
    once = jnp.where(once, 1.0, 1.0 / HEAD_DIM).astype(BF16)
    out, state = st.out("pgrads"), st["state"]
    every = range(blocks)
    own = [here, jnp.logical_not(here)]
    mask2 = jnp.concatenate([mask, mask], axis=0)
    own_wide = [jnp.concatenate([o, o], axis=1) for o in own]
    pick = lambda x: jnp.where(here, x[:CHUNK], x[CHUNK:])
    q, k, v = ([st.rows(x, c)[b] for b in every] for x in ("q", "k", "v"))
    dw = st.rows("dw", c)
    dw = [dw[:, b * WIDE : (b + 1) * WIDE] for b in every]
    value_share = [jnp.concatenate([v[b], share], axis=1) for b in every]
    scores = [nt(stack(q[b], own), k[b]) for b in every]
    sgrad = [nt(stack(dw[b], own_wide), value_share[b]) for b in every]
    q_t = [q[b].T for b in every]
    dw_t = [dw[b][:, :PAIR].T for b in every]
    scores = [jnp.where(mask2, scores[b], 0.0).astype(BF16) for b in every]
    sgrad = [jnp.where(mask2, sgrad[b], 0.0).astype(BF16) for b in every]
    low = [state[b].astype(BF16) for b in every]
    dq = [reads_far * nt(dw[b], st["come"][b] * once) for b in every]
    if c > 0:
        dq = [dq[b] + reads * nt(dw[b], st["held"][c, b] * once) for b in every]
    dq = [dq[b] + pick(nn(sgrad[b], k[b])) for b in every]
    dk, dv = [], []
    for b in every:
        for out_t, left, right in ((dk, q_t[b], sgrad[b]), (dv, dw_t[b], scores[b])):
            both = []
            for h in range(2):
                feats = slice(h * HEAD_DIM, (h + 1) * HEAD_DIM)
                both.append(nn(left[feats], right[h * CHUNK : (h + 1) * CHUNK]))
            out_t.append(jnp.concatenate(both, axis=0).T)
    for b in every:
        dk_b = dk[b] + in_last * nt(value_share[b], low[b])
        dv_b = dv[b] + in_last * nn(k[b], low[b][:, :PAIR])
        at = 3 * b * PAIR
        dq_b = dq[b] * jnp.minimum(q[b].astype(F32), 1.0)
        dk_b = dk_b * jnp.minimum(k[b].astype(F32), 1.0)
        out[rows, at : at + PAIR] = dq_b.astype(BF16)
        out[rows, at + PAIR : at + 2 * PAIR] = dk_b.astype(BF16)
        out[rows, at + 2 * PAIR : at + 3 * PAIR] = dv_b.astype(BF16)
        if c > 0:
            grown = tn(q[b] * reads.astype(BF16), dw[b])
            state[b] = carried * state[b] + jnp.where(block_diagonal, grown, 0.0)
    st.send("pgrads", rows)


class PieceRows:
    def __init__(self, out, rows_one, rows_two, pieces):
        self.out, self.one, self.two = out, rows_one // pieces, rows_two // pieces

    def write(self, at, rows, share, offset):
        done, total = 0, rows.shape[0]
        while done < total:
            piece, inside = divmod(at + done, share)
            take = min(total - done, share - inside)
            start = piece * (self.one + self.two) + offset + inside
            self.out[start : start + take, :] = rows[done : done + take, :]
            done += take

    def first(self, at, rows):
        self.write(at, rows, self.one, 0)

    def second(self, at, rows):
        self.write(at, rows, self.two, self.one)


def attend_back(pieces, first, dw, gone, part, come, cols, doc_row, n1, gwo):
    tokens, width = n1.shape
    blocks, chunks = part["q"].shape[0], tokens // CHUNK

    def body(st):
        flag = st.rows("cols", chunks - 1)[0:1, FIRST_HALF : FIRST_HALF + 1]
        for b in range(blocks):
            st["state"][b] = st["gone"][first + b].astype(F32) * flag
        for c in reversed(range(chunks)):
            attend_back_chunk(st, blocks, c)
        for b in range(blocks):
            grad = tn(st["n1"][...], st.out("pgrads")[:, 3 * b * PAIR : 3 * (b + 1) * PAIR])
            grad = grad.astype(BF16)
            block = st["gwo"][b * PAIR : (b + 1) * PAIR, :]
            fill = PieceRows(st.out(f"grad{b}"), 3 * width, width, pieces)
            for p in range(3):
                fill.first(p * width, grad[:, p * PAIR : (p + 1) * PAIR])
            for j in range(width // PAIR):
                fill.second(j * PAIR, block[:, j * PAIR : (j + 1) * PAIR])
            st.send(f"grad{b}")

    ins = dict(doc_row=doc_row, gone=gone, come=come, held=part["held"])
    ins.update({x: Rows(part[x], chunks - 1) for x in ("q", "k", "v")})
    ins.update(cols=Rows(cols, chunks - 1))
    ins.update(dw=Rows(dw, chunks - 1, slice(first * WIDE, (first + blocks) * WIDE)), n1=n1)
    own = slice(first * PAIR, (first + blocks) * PAIR)
    ins.update(gwo=(gwo, "gwo", (slice(None),), own))
    outs = dict(pgrads=((tokens, 3 * blocks * PAIR), BF16))
    for b in range(blocks):
        outs[f"grad{b}"] = ((4 * width, PAIR), BF16)
    scratch = dict(state=((blocks, PAIR, WIDE), F32), gwo=((blocks * PAIR, width), BF16))
    flops = 2 * tokens * blocks * PAIR * (3 * width + 12 * CHUNK)
    return staged("attend_back", body, ins, outs, scratch, flops, chunks + blocks, 2)


def input_back(tok, rgrad, pgrads, gain, w):
    tokens, width = tok.shape
    blocks, chunks = len(w), tokens // CHUNK

    def body(st):
        for key in w_keys:
            st[key]
        gain = line(st["gain"])
        one = two = 0.0
        for c in range(chunks):
            rows = chunk_rows(c)
            both = jnp.concatenate([st.rows(f"pgrads{g}", c) for g in range(len(pgrads))], axis=1)
            grad = nt(both, st["w"][...])
            xhat, rstd = normalise(st.rows("tok", c).astype(F32))
            st.out("out")[rows, :] = st.rows("rgrad", c).astype(F32) + norm_back(grad, xhat, rstd, gain)
            st.send("out", rows)
            one, two = one + eight(grad * xhat), two + eight(grad)
        small = [jnp.sum(x, axis=0, keepdims=True) for x in (one, two)]
        st.out("small")[...] = jnp.concatenate(small + [jnp.zeros((6, width), F32)], axis=0)
        st.send("small")

    ins, w_keys = {}, []
    for b in range(blocks):
        for p in range(3):
            at = (3 * b + p) * PAIR
            w_keys.append(f"w{b}_{p}")
            ins[w_keys[-1]] = (w[b], "w", (slice(None), slice(at, at + PAIR)), p)
    ins.update({f"pgrads{g}": Rows(x, 0) for g, x in enumerate(pgrads)})
    ins.update(gain=gain, tok=Rows(tok, 0), rgrad=Rows(rgrad, 0))
    outs = dict(out=((tokens, width), F32), small=((8, width), F32))
    scratch = dict(w=((width, 3 * blocks * PAIR), BF16))
    return staged(
        "input_back", body, ins, outs, scratch, 6 * tokens * width * width, chunks + 1
    )


def swap(x, axis, size, bit):
    return lax.ppermute(x, axis, [(i, i ^ bit) for i in range(size)])


def tie(x, *others):
    return lax.optimization_barrier((x, *others))[0]


def gate(*xs):
    return lax.optimization_barrier(xs)


def add(a, b):
    return (a.astype(F32) + b.astype(F32)).astype(BF16)


def cut(x, like):
    at, out = 0, []
    for y in like:
        out.append(x[at : at + y.shape[0]])
        at += y.shape[0]
    return out


def part(x, parts, which):
    rows = x.shape[0] // parts
    return lax.dynamic_slice_in_dim(x, which * rows, rows, 0)


def half(x, which):
    return part(x, 2, which)


def join(x, other, side):
    return jnp.where(side == 0, jnp.concatenate([x, other]), jnp.concatenate([other, x]))


def lockstep(*chains):
    results, sent = [None] * len(chains), {}
    for i, chain in enumerate(chains):
        sent[i] = next(chain)
    while sent:
        flat, tree = jax.tree.flatten(sent)
        sent = jax.tree.unflatten(tree, gate(*flat))
        for i in list(sent):
            try:
                sent[i] = chains[i].send(sent[i])
            except StopIteration as stop:
                results[i] = stop.value
                del sent[i]
    return results


def body(
    dp,
    head,
    tokens,
    doc_ids,
    pad_mask,
    norm1_gain,
    norm1_shift,
    w_qkv,
    w_out,
    norm2_gain,
    norm2_shift,
    w_hidden,
    hidden_bias,
    w_return,
    return_bias,
    out_grad,
):
    count, width = tokens.shape
    pieces = dp // 2
    core = lambda x: swap(x, "head", head, 1)
    cross = lambda x: swap(x, "head", head, 2)
    bits = dp.bit_length() - 1
    spot = lax.axis_index("dp")
    side = [(spot >> b) & 1 for b in range(bits)]
    along = lambda x, b: swap(x, "dp", dp, 1 << b)

    def leave(xs, b):
        return along(jnp.concatenate([half(x, 1 - side[b]) for x in xs]), b)

    def meet(xs, b, got):
        halves = [half(x, side[b]) for x in xs]
        return [add(x, y) for x, y in zip(halves, cut(got, halves))]

    def leave_quad(x):
        spot = lambda one, two: 2 * (side[0] ^ one) + (side[1] ^ two)
        return [
            swap(part(x, 4, spot(one, two)), "dp", dp, one + 2 * two)
            for one, two in ((1, 0), (1, 1), (0, 1))
        ]

    def meet_quad(x, got):
        x = part(x, 4, 2 * side[0] + side[1]).astype(F32)
        for y in got:
            x = x + y.astype(F32)
        return x.astype(BF16)

    def rest_of(xs):
        for b in range(2, bits - 1):
            xs = meet(xs, b, leave(xs, b))
        return xs

    def unfold(x, other, *shares):
        shape = (pieces // 2, -1, x.shape[1])
        low = jnp.where(side[0] == 0, x, other).reshape(shape)
        high = jnp.where(side[0] == 0, other, x).reshape(shape)
        at, out = 0, []
        for share in shares:
            parts = [y[:, at : at + share].reshape(-1, x.shape[1]) for y in (low, high)]
            out.append(jnp.concatenate(parts).astype(F32))
            at += share
        return out

    def spread(xs, late, *shares):
        for b in reversed(range(1, bits - 1)):
            got = yield along(jnp.concatenate(xs), b)
            xs = [join(x, y, side[b]) for x, y in zip(xs, cut(got, xs))]
        wire = along(jnp.concatenate(xs), 0)
        for _ in range(late):
            yield []
        got = yield wire
        return [unfold(x, y, *s) for x, y, s in zip(xs, cut(got, xs), shares)]

    wq, wo, wr = ([x, core(x), cross(x)] for x in (w_qkv, w_out, w_return))

    near = open_layer(
        doc_ids, pad_mask, tokens, norm1_gain, norm1_shift, wq[:2], w_hidden, hidden_bias
    )
    n1, cols, doc_row = near["n1"], near["cols"], near["doc_row"]
    wh = [near["wh"], core(near["wh"]), cross(near["wh"])]
    wq.append(core(tie(wq[2], n1)))
    come_near = core(near["last"])
    far = attend(n1, wq[2:], cols, tie(doc_row, wo[2]))
    come_far, across = gate(far["last"], wo[2])
    come = [come_near, core(come_far)]
    wo.append(core(across))
    mid = mix_feed(
        pieces,
        tokens,
        out_grad,
        [near, far],
        come,
        wo,
        cols,
        norm2_gain,
        norm2_shift,
        wh[:2],
        wr[:2],
    )
    wh.append(core(tie(wh[2], mid["n2"])))
    wr.append(core(tie(wr[2], mid["n2"])))
    down1, up1 = tie((mid["down1"], mid["up1"]), wh[3], wr[3])
    down1, up1 = core(down1), core(up1)
    end = feed(pieces, mid["n2"], out_grad, wh[2:], wr[2:], mid["dn2"])

    down3, up3, down1, up1 = gate(end["down1"], end["up1"], down1, up1)
    down3, up3 = core(down3), core(up3)
    down0, up0 = add(mid["down0"], down1), add(mid["up0"], up1)
    down2, up2 = add(end["down0"], down3), add(end["up0"], up3)

    ups, down_wire = [up0, up2], cross(down2)
    ups_wire = leave(ups, 0)
    back = unmix(
        end["dn2"],
        mid["residual"],
        out_grad,
        mid["mixed"],
        mid["inv"],
        wo,
        [near["q"], far["q"]],
        cols,
        tie(norm2_gain, down3, up3),
    )
    gone = core(back["gone"])
    acts = [mid["act"], end["act"]]
    output = finish(mid["residual"], acts, wr, tie(return_bias, back["small"]))
    gone, down_wire, ups_wire, output = gate(gone, down_wire, ups_wire, output)
    down, ups = add(down0, down_wire), meet(ups, 0, ups_wire)
    down_wires, up_wire = leave_quad(down), cross(ups[1])
    args = cols, tie(doc_row, output), n1, back["gwo"]
    side_b = attend_back(pieces, 2, back["dw"], gone, far, come[1], *args)
    grad3, up_wire, *down_wires = gate(side_b["grad1"], up_wire, *down_wires)
    grad3 = core(grad3)
    (down,) = rest_of([meet_quad(down, down_wires)])
    up = [add(ups[0], up_wire)]
    down_wire, up_wire = along(down, bits - 1), leave(up, 1)
    grad2 = add(side_b["grad0"], grad3)
    grad_wire = cross(grad2)
    args = cols, tie(doc_row, grad3), n1, back["gwo"]
    side_a = attend_back(pieces, 0, back["dw"], gone, near, come[0], *args)
    grad1, down_wire, up_wire, grad_wire = gate(
        side_a["grad1"], down_wire, up_wire, grad_wire
    )
    grad1 = core(grad1)
    down, (up,) = add(down, down_wire), rest_of(meet(up, 1, up_wire))
    up_wire = along(up, bits - 1)
    spread_down = spread([down], 1, (width // pieces,))
    down_wire = next(spread_down)
    grad = [add(add(side_a["grad0"], grad1), grad_wire)]
    grad_wire = leave(grad, 0)
    last = input_back(
        tokens,
        back["rgrad"],
        [side_a["pgrads"], side_b["pgrads"]],
        tie(norm1_gain, grad1),
        wq,
    )
    small, down_wire, up_wire, grad_wire = gate(last["small"], down_wire, up_wire, grad_wire)
    up, grad = add(up, up_wire), meet(grad, 0, grad_wire)

    def finish_grad(xs):
        for b in range(1, bits - 1):
            got = yield leave(xs, b)
            xs = meet(xs, b, got)
        got = yield along(xs[0], bits - 1)
        return (yield from spread([add(xs[0], got)], 0, (3 * width // pieces, width // pieces)))

    def finish_small(x):
        got = yield core(x)
        x = x + got
        flat = lambda x, axis_bit, dp_bit: lax.ppermute(
            x,
            ("dp", "head"),
            [
                (i * head + j, (i ^ dp_bit) * head + (j ^ axis_bit))
                for i in range(dp)
                for j in range(head)
            ],
        )
        one, two, three = yield [flat(x, 2, 0), flat(x, 0, 1), flat(x, 2, 1)]
        x = (x + one) + (two + three)
        for b in range(1, bits):
            got = yield along(x, b)
            x = x + got
        return x

    def go_on(chain, got):
        try:
            while True:
                got = yield chain.send(got)
        except StopIteration as stop:
            return stop.value

    small = jnp.concatenate([small[:2], back["small"][:3]])
    (grads,), (downs,), (ups,), small = lockstep(
        finish_grad(grad),
        go_on(spread_down, down_wire),
        spread([up], 1, (width // pieces, 16)),
        finish_small(small),
    )
    g_qkv, g_out = grads
    (down,), (up, bias_grad) = downs, ups
    g_out = g_out.reshape(width // PAIR, PAIR, PAIR)
    g_out = jnp.concatenate([g_out[i] for i in range(width // PAIR)], axis=1)
    return (
        output,
        last["out"],
        small[0],
        small[1],
        g_qkv.reshape(3, width, PAIR),
        g_out,
        small[2],
        small[3],
        up,
        bias_grad[0],
        down,
        small[4],
    )


def solution(mesh):
    return jax.shard_map(
        functools.partial(body, mesh.shape["dp"], mesh.shape["head"]),
        mesh=mesh,
        in_specs=(
            P(("dp", "head"), None),
            P("dp", None),
            P("dp", None),
            P(),
            P(),
            P(None, None, "head"),
            P("head", None),
            P(),
            P(),
            P(None, "head"),
            P("head"),
            P("head", None),
            P(),
            P(("dp", "head"), None),
        ),
        out_specs=(
            P(("dp", "head"), None),
            P(("dp", "head"), None),
            P(),
            P(),
            P(None, None, "head"),
            P("head", None),
            P(),
            P(),
            P(None, "head"),
            P("head"),
            P("head", None),
            P(),
        ),
        check_vma=False,
    )
```

```python
import functools

import jax
import jax.numpy as jnp
from jax import lax
from jax.experimental import pallas as pl
from jax.experimental.pallas import tpu as pltpu
from jax.sharding import PartitionSpec as P

HEAD_DIM = 64
PAIR = 2 * HEAD_DIM
WIDE = 2 * PAIR
CHUNK = 256
LANES = 128
EPSILON = 1e-05
BELOW_ONE = 1.0 - 2.0**-8
F32 = jnp.float32
BF16 = jnp.bfloat16
VMEM_BYTES = 60 * 1024 * 1024

DOC, LIVE, READ_HALF, READ_CHUNK, IN_LAST, CARRIED, FIRST_HALF = range(7)


def nn(a, b):
    return lax.dot_general(a, b, (((1,), (0,)), ((), ())), preferred_element_type=F32)


def nt(a, b):
    return lax.dot_general(a, b, (((1,), (1,)), ((), ())), preferred_element_type=F32)


def tn(a, b):
    return lax.dot_general(a, b, (((0,), (0,)), ((), ())), preferred_element_type=F32)


def normalise(x):
    centre = x - jnp.mean(x, axis=-1, keepdims=True)
    rstd = lax.rsqrt(jnp.mean(centre * centre, axis=-1, keepdims=True) + EPSILON)
    return centre * rstd, rstd


def norm_back(grad, xhat, rstd, gain):
    scaled = grad * gain
    mean_one = jnp.mean(scaled, axis=-1, keepdims=True)
    mean_two = jnp.mean(scaled * xhat, axis=-1, keepdims=True)
    return rstd * (scaled - mean_one - xhat * mean_two)


def line(ref):
    return ref[...].astype(F32).reshape(1, ref.shape[0])


def eight(x):
    return jnp.sum(x.reshape(x.shape[0] // 8, 8, x.shape[1]), axis=0)


def head_lanes(shape):
    return lax.broadcasted_iota(jnp.int32, shape, len(shape) - 1) % PAIR < HEAD_DIM


def pair_mask(width):
    rows = lax.broadcasted_iota(jnp.int32, (PAIR, width), 0) < HEAD_DIM
    return rows == head_lanes((PAIR, width))


def allowed_mask(doc_col, doc_row):
    t = lax.broadcasted_iota(jnp.int32, (CHUNK, CHUNK), 0)
    s = lax.broadcasted_iota(jnp.int32, (CHUNK, CHUNK), 1)
    return (doc_col == doc_row) & (s <= t)


def feature(x):
    return jnp.where(x > 0, x + 1.0, jnp.exp(jnp.minimum(x, 0.0)))


def chunk_rows(c):
    return slice(c * CHUNK, (c + 1) * CHUNK)


def column(cols, which):
    return cols[:, which : which + 1]


def stack(x, masks):
    return jnp.concatenate([jnp.where(mask, x, jnp.zeros_like(x)) for mask in masks], axis=0)


class Rows:
    def __init__(self, array, first, columns=None):
        self.array = array
        self.columns = columns or slice(0, array.shape[-1])
        self.shape = array.shape[:-1] + (self.columns.stop - self.columns.start,)
        rows = self.shape[-2]
        rest = slice(CHUNK, rows) if first == 0 else slice(0, rows - CHUNK)
        self.first, self.parts = first, [chunk_rows(first), rest]

    def index(self, rows, columns):
        return (slice(None),) * (len(self.shape) - 2) + (rows, columns)


class Staged:
    def __init__(self, specs, late, ins, outs, scratch, in_sem, out_sem):
        self.specs, self.ins, self.outs, self.scratch = specs, ins, outs, scratch
        self.out_sem, self.sent = out_sem, []
        self.pending = {}
        begin = list(ins)[: len(ins) - late]
        for turn, names in enumerate((begin, begin, list(ins)[len(ins) - late :])):
            for name in names:
                spec, (src, dst) = specs[name], ins[name]
                if isinstance(spec, Rows):
                    rows = spec.parts[turn]
                    src = src.at[spec.index(rows, spec.columns)]
                    dst = dst.at[spec.index(rows, slice(None))]
                elif turn == 1:
                    continue
                copy = pltpu.make_async_copy(src, dst, in_sem.at[len(self.pending)])
                copy.start()
                self.pending[name, turn % 2] = copy

    def __getitem__(self, name):
        for key in [key for key in self.pending if key[0] == name]:
            self.pending.pop(key).wait()
        return self.ins[name][1] if name in self.ins else self.scratch[name]

    def rows(self, name, c):
        spec = self.specs[name]
        if not isinstance(spec, Rows):
            return self[name][chunk_rows(c), :]
        key = (name, int(c != spec.first))
        if key in self.pending:
            self.pending.pop(key).wait()
        return self.ins[name][1][spec.index(chunk_rows(c), slice(None))]

    def out(self, name):
        return self.outs[name][1]

    def send(self, name, *index):
        dst, src = self.outs[name]
        if index:
            dst, src = dst.at[index], src.at[index]
        copy = pltpu.make_async_copy(src, dst, self.out_sem.at[len(self.sent)])
        copy.start()
        self.sent.append(copy)

    def finish(self):
        for copy in list(self.pending.values()) + self.sent:
            copy.wait()


def staged(name, body, ins, outs, scratch, flops, sends, late=0):
    in_names, out_names, scratch_names = list(ins), list(outs), list(scratch)
    arrays, in_specs, own = [], [], []
    for value in ins.values():
        value = value.array if isinstance(value, Rows) else value
        arrays.append(value[0] if isinstance(value, tuple) else value)
        in_specs.append(pl.BlockSpec(memory_space=pl.ANY))
        if not isinstance(value, tuple):
            own.append(pltpu.VMEM(ins[in_names[len(arrays) - 1]].shape, value.dtype))

    def kernel(*refs):
        refs = list(refs)
        take = lambda n: [refs.pop(0) for _ in range(n)]
        src, dst = take(len(in_names)), take(len(out_names))
        own_refs, out_refs = take(len(own)), take(len(out_names))
        held = dict(zip(scratch_names, take(len(scratch_names))))
        in_sem, out_sem = refs
        ends = {}
        for key, ref in zip(in_names, src):
            value = ins[key]
            if not isinstance(value, tuple):
                ends[key] = (ref, own_refs.pop(0))
            else:
                ends[key] = (ref.at[value[3:]] if value[3:] else ref, held[value[1]].at[value[2]])
        stage = Staged(ins, late, ends, dict(zip(out_names, zip(dst, out_refs))), held, in_sem, out_sem)
        body(stage)
        stage.finish()

    shapes = list(outs.values())
    copies = sum(2 if isinstance(x, Rows) else 1 for x in ins.values())
    out = pl.pallas_call(
        kernel,
        in_specs=in_specs,
        out_specs=[pl.BlockSpec(memory_space=pl.ANY)] * len(out_names),
        out_shape=[jax.ShapeDtypeStruct(*s) for s in shapes],
        scratch_shapes=own
        + [pltpu.VMEM(*s) for s in shapes]
        + [pltpu.VMEM(*s) for s in scratch.values()]
        + [pltpu.SemaphoreType.DMA((copies,)), pltpu.SemaphoreType.DMA((sends,))],
        compiler_params=pltpu.CompilerParams(vmem_limit_bytes=VMEM_BYTES),
        cost_estimate=pl.CostEstimate(flops=flops, bytes_accessed=4 << 20, transcendentals=0),
        name=name,
    )(*arrays)
    return dict(zip(out_names, out))


def attend_chunk(st, blocks, c, n1, cols, doc_row):
    w, state, every = st["w"], st["state"], range(blocks)
    rows = chunk_rows(c)
    live, reads = column(cols, LIVE), column(cols, READ_CHUNK)
    in_last = column(cols, IN_LAST).astype(BF16)
    carried = cols[0:1, CARRIED : CARRIED + 1]
    mask = allowed_mask(column(cols, DOC), doc_row[:, rows])
    mask = jnp.concatenate([mask, mask], axis=0)
    q_all = feature(nn(n1, w[0])).astype(BF16)
    k_all = (feature(nn(n1, w[1])) * live).astype(BF16)
    v_all = nn(n1, w[2]).astype(BF16)
    here = head_lanes((CHUNK, WIDE))
    own = [here[:, :PAIR], jnp.logical_not(here[:, :PAIR])]
    block_diagonal = pair_mask(WIDE)
    ones = jnp.ones((CHUNK, PAIR), BF16)
    part = lambda x, b: x[:, b * PAIR : (b + 1) * PAIR]
    q, k, v = ([part(x, b) for b in every] for x in (q_all, k_all, v_all))
    for b in every:
        st.out("q")[b, rows], st.out("k")[b, rows], st.out("v")[b, rows] = q[b], k[b], v[b]
    scores = [nt(stack(q[b], own), k[b]) for b in every]
    wide = [jnp.concatenate([v[b], ones], axis=1) for b in every]
    grown = [tn(k[b] * in_last, wide[b]) for b in every]
    scores = [jnp.where(mask, scores[b], 0.0).astype(BF16) for b in every]
    both = [nn(scores[b], wide[b]) for b in every]
    total = [jnp.where(here, both[b][:CHUNK], both[b][CHUNK:]) for b in every]
    for b in every:
        if c > 0:
            low = state[b].astype(BF16)
            st.out("held")[c, b] = low
            total[b] = total[b] + reads * nn(q[b], low)
        else:
            st.out("held")[c, b] = jnp.zeros((PAIR, WIDE), BF16)
        st.out("num")[b, rows], st.out("tot")[b, rows] = total[b][:, :PAIR], total[b][:, PAIR:]
        more = jnp.where(block_diagonal, grown[b], 0.0)
        state[b] = more if c == 0 else carried * state[b] + more
    for name in ("q", "k", "v", "num", "tot"):
        st.send(name, slice(None), rows)


def attend_finish(st, blocks):
    for b in range(blocks):
        st.out("last")[b ^ 1] = st["state"][b].astype(BF16)
    st.send("last")
    st.send("held")


def attend_outs(tokens, blocks):
    part = (blocks, tokens, PAIR)
    return dict(
        q=(part, BF16),
        k=(part, BF16),
        v=(part, BF16),
        num=(part, F32),
        tot=(part, F32),
        held=((tokens // CHUNK, blocks, PAIR, WIDE), BF16),
        last=((blocks, PAIR, WIDE), BF16),
    )


def attend_scratch(width, blocks):
    return dict(w=((3, width, blocks * PAIR), BF16), state=((blocks, PAIR, WIDE), F32))


def attend_weights(w):
    everything = slice(None)
    return {
        f"w{b}": (x, "w", (everything, everything, slice(b * PAIR, (b + 1) * PAIR)))
        for b, x in enumerate(w)
    }


def attend_flops(tokens, width, blocks):
    return 2 * tokens * blocks * PAIR * (3 * width + 4 * CHUNK)


def make_flags(doc_ids, pad_mask, count):
    halves = doc_ids.shape[1] // count
    me = lax.axis_index("head")
    row, place = lax.div(me, halves), lax.rem(me, halves)

    def here(x):
        whole = x[0:1, :]
        for r in range(1, x.shape[0]):
            whole = jnp.where(row == r, x[r : r + 1, :], whole)
        part = whole[:, :count]
        for i in range(1, x.shape[1] // count):
            part = jnp.where(place == i, whole[:, i * count : (i + 1) * count], part)
        return whole, part

    whole, docs = here(doc_ids)
    _, live = here(pad_mask)
    edge = whole[:, count - 1 : count]
    second = jnp.where(place > 0, 1.0, 0.0)
    as_float = lambda x: jnp.where(x, 1.0, 0.0)
    reads, in_last, carried = [], [], []
    before = None
    for c in range(count // CHUNK):
        part = docs[:, chunk_rows(c)]
        end = part[:, CHUNK - 1 : CHUNK]
        in_last.append(as_float(part == end))
        if before is None:
            reads.append(jnp.zeros((1, CHUNK), F32))
            carried.append(jnp.zeros((1, CHUNK), F32))
        else:
            reads.append(as_float(part == before))
            carried.append(as_float(jnp.broadcast_to(end, part.shape) == before))
        before = end
    join = lambda x: jnp.concatenate(x, axis=1)
    doc_line = docs.astype(F32)
    lines = [
        doc_line,
        live.astype(F32),
        as_float(docs == edge) * second,
        join(reads),
        join(in_last),
        join(carried),
        jnp.broadcast_to(1.0 - second, (1, count)).astype(F32),
    ]
    lines.append(jnp.zeros((LANES - len(lines), count), F32))
    return jnp.concatenate(lines, axis=0).T, doc_line


def open_layer(doc_ids, pad_mask, tok, gain, shift, w, w_hidden, hidden_bias):
    tokens, width = tok.shape
    blocks, chunks, hidden = len(w), tokens // CHUNK, w_hidden.shape[1]

    def body(st):
        cols, doc_row = make_flags(st["doc_ids"], st["pad_mask"], tokens)
        st.out("cols")[...], st.out("doc_row")[...] = cols, doc_row
        st.send("cols")
        st.send("doc_row")
        cols, doc_row, n1 = st.out("cols"), st.out("doc_row"), st.out("n1")
        gain, shift = line(st["gain"]), line(st["shift"])
        for c in range(chunks):
            xhat, _ = normalise(st.rows("tok", c).astype(F32))
            n1[chunk_rows(c), :] = (xhat * gain + shift).astype(BF16)
        st.send("n1")
        for b in range(blocks):
            st[f"w{b}"]
        for c in range(chunks):
            attend_chunk(st, blocks, c, n1[chunk_rows(c), :], cols[chunk_rows(c), :], doc_row)
        attend_finish(st, blocks)
        st["wh"][width:, :] = jnp.broadcast_to(line(st["bias"]).astype(BF16), (16, hidden))
        st["w_hidden"]
        st.out("wh")[...] = st["wh"][...]
        st.send("wh")

    ins = dict(doc_ids=doc_ids, pad_mask=pad_mask, tok=Rows(tok, 0))
    ins.update(gain=gain, shift=shift, **attend_weights(w), bias=hidden_bias)
    ins.update(w_hidden=(w_hidden, "wh", (slice(0, width),)))
    outs = dict(
        cols=((tokens, LANES), F32),
        doc_row=((1, tokens), F32),
        n1=((tokens, width), BF16),
        wh=((width + 16, hidden), BF16),
    )
    outs.update(attend_outs(tokens, blocks))
    scratch = attend_scratch(width, blocks)
    scratch["wh"] = ((width + 16, hidden), BF16)
    flops = attend_flops(tokens, width, blocks)
    return staged("open", body, ins, outs, scratch, flops, 5 * chunks + 6, 1)


def attend(n1, w, cols, doc_row):
    tokens, width = n1.shape
    blocks, chunks = len(w), tokens // CHUNK

    def body(st):
        doc_row = st["doc_row"]
        for b in range(blocks):
            st[f"w{b}"]
        for c in range(chunks):
            attend_chunk(st, blocks, c, st.rows("n1", c), st.rows("cols", c), doc_row)
        attend_finish(st, blocks)

    ins = dict(doc_row=doc_row, **attend_weights(w))
    ins.update(n1=Rows(n1, 0), cols=Rows(cols, 0))
    flops = attend_flops(tokens, width, blocks)
    return staged(
        "attend",
        body,
        ins,
        attend_outs(tokens, blocks),
        attend_scratch(width, blocks),
        flops,
        5 * chunks + 2,
    )


def gelu_pair(x):
    cdf = 0.5 + 0.5 * lax.erf(x * 0.7071067811865476)
    density = 0.3989422804014327 * jnp.exp(-0.5 * x * x)
    return x * cdf, cdf + x * density


def mix_chunk(st, groups, c):
    cols, w, rows = st.rows("cols", c), st["wo"], chunk_rows(c)
    live, reads = column(cols, LIVE), column(cols, READ_HALF)
    q, num, tot = ([st.rows(f"{x}{g}", c) for g in range(groups)] for x in ("q", "num", "tot"))
    mixed, inv_out = st.out("mixed"), st.out("inv")
    for b in range(2 * groups):
        g, i = divmod(b, 2)
        lanes = slice(b * PAIR, (b + 1) * PAIR)
        far = reads * nn(q[g][i], st[f"come{g}"][i])
        inv = 1.0 / jnp.maximum(tot[g][i] + far[:, PAIR:], 1.0)
        inv_out[rows, lanes] = jnp.where(inv < 1.0, jnp.minimum(inv, BELOW_ONE), 1.0).astype(BF16)
        value = (num[g][i] + far[:, :PAIR]) * inv * live
        mixed[rows, lanes] = value.astype(BF16)
    residual = st.rows("tok", c).astype(F32) + nn(mixed[rows, :], w[...])
    st.out("residual")[rows, :] = residual
    xhat, _ = normalise(residual)
    n2 = (xhat * line(st["gain"]) + line(st["shift"])).astype(BF16)
    st.out("n2")[rows, :] = n2
    for name in ("mixed", "inv", "residual", "n2"):
        st.send(name, rows)


def feed_chunk(st, c, n2, bias, resume):
    rows = chunk_rows(c)
    wh, wr = st["wh"].at[: n2.shape[1]], st["wr"]
    value, slope = gelu_pair(nn(n2, wh[...]) + bias)
    st.out("act")[rows, :] = value.astype(BF16)
    st.send("act", rows)
    grad = nt(st.rows("dy", c), wr[...]) * slope
    low = grad.astype(BF16)
    st["hg"][rows, :] = low
    back = nt(low, wh[...])
    st.out("dn2")[rows, :] = back + st.rows("dn2_in", c) if resume else back
    st.send("dn2", rows)
    return eight(grad)


def feed_grads(st, blocks, pieces, n2, bias_grad):
    width, hidden = n2.shape[1], bias_grad.shape[1] // blocks
    bias_grad = jnp.sum(bias_grad, axis=0, keepdims=True).astype(BF16)
    for b in range(blocks):
        part = slice(b * hidden, (b + 1) * hidden)
        down, up = st.out(f"down{b}"), st.out(f"up{b}")
        down[...] = tn(st.out("act")[:, part], st["dy"][...]).astype(BF16)
        st.send(f"down{b}")
        grad = tn(n2[...], st["hg"][:, part]).astype(BF16)
        rows, step = width // pieces, up.shape[0] // pieces
        for i in range(pieces):
            up[i * step : i * step + rows, :] = grad[i * rows : (i + 1) * rows, :]
            tail = jnp.broadcast_to(bias_grad[:, part], (step - rows, hidden))
            up[i * step + rows : (i + 1) * step, :] = tail
        st.send(f"up{b}")


def feed_parts(tokens, width, pieces, wh, wr):
    blocks, hidden = len(wr), wr[0].shape[0]
    everything = slice(None)
    ins = {}
    for b in range(blocks):
        part = slice(b * hidden, (b + 1) * hidden)
        ins[f"wh{b}"] = (wh[b], "wh", (everything, part))
        ins[f"wr{b}"] = (wr[b], "wr", (part, everything))
    outs = dict(act=((tokens, blocks * hidden), BF16), dn2=((tokens, width), F32))
    for b in range(blocks):
        outs[f"down{b}"] = ((hidden, width), BF16)
        outs[f"up{b}"] = ((width + 16 * pieces, hidden), BF16)
    scratch = dict(
        wh=((width + 16, blocks * hidden), BF16),
        wr=((blocks * hidden, width), BF16),
        hg=((tokens, blocks * hidden), BF16),
    )
    return ins, outs, scratch, 10 * tokens * width * hidden * blocks


def feed_start(st, blocks, width):
    for b in range(blocks):
        st[f"wh{b}"], st[f"wr{b}"]
    return st["wh"][width : width + 1, :].astype(F32)


def mix_feed(pieces, tok, dy, parts, come, wo, cols, gain, shift, wh, wr):
    tokens, width = tok.shape
    blocks, groups, chunks = len(wh), len(parts), tokens // CHUNK

    def body(st):
        for b in range(2 * groups):
            st[f"wo{b}"]
        for c in range(chunks):
            mix_chunk(st, groups, c)
        n2 = st.out("n2")
        bias = feed_start(st, blocks, width)
        bias_grad = 0.0
        for c in range(chunks):
            bias_grad = bias_grad + feed_chunk(st, c, n2[chunk_rows(c), :], bias, False)
        feed_grads(st, blocks, pieces, n2, bias_grad)

    ins = dict(cols=Rows(cols, 0), tok=Rows(tok, 0), gain=gain, shift=shift)
    for g, part in enumerate(parts):
        ins.update({f"{x}{g}": Rows(part[x], 0) for x in ("q", "num", "tot")})
        ins[f"come{g}"] = come[g]
    for b, x in enumerate(wo):
        ins[f"wo{b}"] = (x, "wo", (slice(b * PAIR, (b + 1) * PAIR),))
    more, outs, scratch, flops = feed_parts(tokens, width, pieces, wh, wr)
    ins.update(dy=dy, **more)
    outs.update(
        mixed=((tokens, width), BF16),
        inv=((tokens, width), BF16),
        residual=((tokens, width), F32),
        n2=((tokens, width), BF16),
    )
    scratch["wo"] = ((width, width), BF16)
    late = 1 + len(more)
    return staged("mix_feed", body, ins, outs, scratch, 0, 6 * chunks + 2 * blocks, late)


def feed(pieces, n2, dy, wh, wr, dn2):
    tokens, width = n2.shape
    blocks, chunks = len(wh), tokens // CHUNK

    def body(st):
        bias = feed_start(st, blocks, width)
        bias_grad = 0.0
        for c in range(chunks):
            bias_grad = bias_grad + feed_chunk(st, c, st.rows("n2", c), bias, True)
        feed_grads(st, blocks, pieces, st["n2"], bias_grad)

    ins = dict(n2=n2)
    more, outs, scratch, flops = feed_parts(tokens, width, pieces, wh, wr)
    ins.update(more)
    ins.update(dy=dy, dn2_in=dn2)
    return staged("feed", body, ins, outs, scratch, flops, 2 * chunks + 2 * blocks)


def unmix_chunk(st, blocks, c):
    cols, rows = st.rows("cols", c), chunk_rows(c)
    live, reads = column(cols, LIVE), column(cols, READ_HALF).astype(BF16)
    xhat, rstd = normalise(st.rows("residual", c))
    grad = st.rows("dn2", c)
    wide = st.rows("dy", c).astype(F32)
    rgrad = wide + norm_back(grad, xhat, rstd, line(st["gain"]))
    low = rgrad.astype(BF16)
    st.out("rgrad")[rows, :] = low
    mgrad = nt(low, st["wo"][...]) * live
    sums = pair_mask(PAIR).astype(BF16)
    sums = jnp.concatenate([sums, sums], axis=0)
    inv, mixed = st.rows("inv", c).astype(F32), st.rows("mixed", c).astype(F32)
    q = [st.rows(f"q{g}", c) for g in range(blocks // 2)]
    for b in range(blocks):
        lanes = slice(b * PAIR, (b + 1) * PAIR)
        one, scale = mgrad[:, lanes], inv[:, lanes]
        dw = (one * scale).astype(BF16)
        terms = one * mixed[:, lanes]
        high = terms.astype(BF16)
        rest = (terms - high.astype(F32)).astype(BF16)
        total = nn(jnp.concatenate([high, rest], axis=1), sums)
        tg = jnp.where(scale < 1.0, -total * scale, 0.0).astype(BF16)
        st.out("dw")[rows, b * WIDE : b * WIDE + PAIR] = dw
        st.out("dw")[rows, b * WIDE + PAIR : (b + 1) * WIDE] = tg
        st["reading"][rows, lanes] = q[b // 2][b % 2] * reads
    st.send("rgrad", rows)
    st.send("dw", rows)
    return eight(grad * xhat), eight(grad), eight(wide)


def unmix(dn2, residual, dy, mixed, inv, wo, q, cols, gain):
    tokens, width = dy.shape
    blocks, chunks = len(wo), tokens // CHUNK

    def body(st):
        for b in range(blocks):
            st[f"wo{b}"]
        small = [0.0, 0.0, 0.0]
        for c in range(chunks):
            small = [a + b for a, b in zip(small, unmix_chunk(st, blocks, c))]
        small = [jnp.sum(x, axis=0, keepdims=True) for x in small]
        st.out("small")[...] = jnp.concatenate(small + [jnp.zeros((5, width), F32)], axis=0)
        st.send("small")
        block_diagonal = pair_mask(WIDE)
        for b in range(blocks):
            lanes, wide = slice(b * PAIR, (b + 1) * PAIR), slice(b * WIDE, (b + 1) * WIDE)
            grown = tn(st["reading"][:, lanes], st.out("dw")[:, wide])
            st.out("gone")[b ^ 1] = jnp.where(block_diagonal, grown, 0.0).astype(BF16)
        st.send("gone")
        st.out("gwo")[...] = tn(st["mixed"][...], st.out("rgrad")[...]).astype(BF16)
        st.send("gwo")

    ins = dict(gain=gain, cols=Rows(cols, 0))
    ins.update(residual=Rows(residual, 0), dn2=Rows(dn2, 0), dy=Rows(dy, 0))
    for b, x in enumerate(wo):
        ins[f"wo{b}"] = (x, "wo", (slice(b * PAIR, (b + 1) * PAIR),))
    ins.update(inv=Rows(inv, 0), mixed=Rows(mixed, 0))
    ins.update({f"q{g}": Rows(x, 0) for g, x in enumerate(q)})
    outs = dict(
        rgrad=((tokens, width), BF16),
        dw=((tokens, 2 * width), BF16),
        gone=((blocks, PAIR, WIDE), BF16),
        gwo=((width, width), BF16),
        small=((8, width), F32),
    )
    scratch = dict(wo=((width, width), BF16), reading=((tokens, width), BF16))
    return staged(
        "unmix", body, ins, outs, scratch, 6 * tokens * width * width, 2 * chunks + 3
    )


def finish(residual, act, wr, bias):
    tokens, width = residual.shape

    def body(st):
        total = 0.0
        for i in range(len(wr)):
            total = total + nn(st[f"act{i}"][...], st[f"wr{i}"][...])
        total = total + st["residual"][...] + line(st["bias"])
        st.out("out")[...] = total.astype(BF16)
        st.send("out")

    ins, own, scratch = {}, [], {}
    for x in act:
        own += [(x, slice(i, i + wr[0].shape[0])) for i in range(0, x.shape[1], wr[0].shape[0])]
    for i, (x, columns) in enumerate(own):
        scratch[f"part{i}"] = ((tokens, wr[i].shape[0]), BF16)
        ins[f"act{i}"] = (x, f"part{i}", (slice(None),), slice(None), columns)
        ins[f"wr{i}"] = wr[i]
    ins.update(residual=residual, bias=bias)
    outs = dict(out=((tokens, width), BF16))
    flops = 2 * tokens * width * width * len(wr)
    return staged("finish", body, ins, outs, scratch, flops, 1)["out"]


def attend_back_chunk(st, blocks, c):
    cols, rows = st.rows("cols", c), chunk_rows(c)
    reads, reads_far = column(cols, READ_CHUNK), column(cols, READ_HALF)
    in_last = column(cols, IN_LAST)
    carried = cols[0:1, CARRIED : CARRIED + 1]
    mask = allowed_mask(column(cols, DOC), st["doc_row"][:, rows])
    here = head_lanes((CHUNK, PAIR))
    block_diagonal = pair_mask(WIDE)
    share = jnp.full((CHUNK, PAIR), 1.0 / HEAD_DIM, BF16)
    once = lax.broadcasted_iota(jnp.int32, (PAIR, WIDE), 1) < PAIR
    once = jnp.where(once, 1.0, 1.0 / HEAD_DIM).astype(BF16)
    out, state = st.out("pgrads"), st["state"]
    every = range(blocks)
    own = [here, jnp.logical_not(here)]
    mask2 = jnp.concatenate([mask, mask], axis=0)
    own_wide = [jnp.concatenate([o, o], axis=1) for o in own]
    pick = lambda x: jnp.where(here, x[:CHUNK], x[CHUNK:])
    q, k, v = ([st.rows(x, c)[b] for b in every] for x in ("q", "k", "v"))
    dw = st.rows("dw", c)
    dw = [dw[:, b * WIDE : (b + 1) * WIDE] for b in every]
    value_share = [jnp.concatenate([v[b], share], axis=1) for b in every]
    scores = [nt(stack(q[b], own), k[b]) for b in every]
    sgrad = [nt(stack(dw[b], own_wide), value_share[b]) for b in every]
    q_t = [q[b].T for b in every]
    dw_t = [dw[b][:, :PAIR].T for b in every]
    scores = [jnp.where(mask2, scores[b], 0.0).astype(BF16) for b in every]
    sgrad = [jnp.where(mask2, sgrad[b], 0.0).astype(BF16) for b in every]
    low = [state[b].astype(BF16) for b in every]
    dq = [reads_far * nt(dw[b], st["come"][b] * once) for b in every]
    if c > 0:
        dq = [dq[b] + reads * nt(dw[b], st["held"][c, b] * once) for b in every]
    dq = [dq[b] + pick(nn(sgrad[b], k[b])) for b in every]
    dk, dv = [], []
    for b in every:
        for out_t, left, right in ((dk, q_t[b], sgrad[b]), (dv, dw_t[b], scores[b])):
            both = []
            for h in range(2):
                feats = slice(h * HEAD_DIM, (h + 1) * HEAD_DIM)
                both.append(nn(left[feats], right[h * CHUNK : (h + 1) * CHUNK]))
            out_t.append(jnp.concatenate(both, axis=0).T)
    for b in every:
        dk_b = dk[b] + in_last * nt(value_share[b], low[b])
        dv_b = dv[b] + in_last * nn(k[b], low[b][:, :PAIR])
        at = 3 * b * PAIR
        dq_b = dq[b] * jnp.minimum(q[b].astype(F32), 1.0)
        dk_b = dk_b * jnp.minimum(k[b].astype(F32), 1.0)
        out[rows, at : at + PAIR] = dq_b.astype(BF16)
        out[rows, at + PAIR : at + 2 * PAIR] = dk_b.astype(BF16)
        out[rows, at + 2 * PAIR : at + 3 * PAIR] = dv_b.astype(BF16)
        if c > 0:
            grown = tn(q[b] * reads.astype(BF16), dw[b])
            state[b] = carried * state[b] + jnp.where(block_diagonal, grown, 0.0)
    st.send("pgrads", rows)


class PieceRows:
    def __init__(self, out, rows_one, rows_two, pieces):
        self.out, self.one, self.two = out, rows_one // pieces, rows_two // pieces

    def write(self, at, rows, share, offset):
        done, total = 0, rows.shape[0]
        while done < total:
            piece, inside = divmod(at + done, share)
            take = min(total - done, share - inside)
            start = piece * (self.one + self.two) + offset + inside
            self.out[start : start + take, :] = rows[done : done + take, :]
            done += take

    def first(self, at, rows):
        self.write(at, rows, self.one, 0)

    def second(self, at, rows):
        self.write(at, rows, self.two, self.one)


def attend_back(pieces, first, dw, gone, part, come, cols, doc_row, n1, gwo):
    tokens, width = n1.shape
    blocks, chunks = part["q"].shape[0], tokens // CHUNK

    def body(st):
        flag = st.rows("cols", chunks - 1)[0:1, FIRST_HALF : FIRST_HALF + 1]
        for b in range(blocks):
            st["state"][b] = st["gone"][first + b].astype(F32) * flag
        for c in reversed(range(chunks)):
            attend_back_chunk(st, blocks, c)
        for b in range(blocks):
            grad = tn(st["n1"][...], st.out("pgrads")[:, 3 * b * PAIR : 3 * (b + 1) * PAIR])
            grad = grad.astype(BF16)
            block = st["gwo"][b * PAIR : (b + 1) * PAIR, :]
            fill = PieceRows(st.out(f"grad{b}"), 3 * width, width, pieces)
            for p in range(3):
                fill.first(p * width, grad[:, p * PAIR : (p + 1) * PAIR])
            for j in range(width // PAIR):
                fill.second(j * PAIR, block[:, j * PAIR : (j + 1) * PAIR])
            st.send(f"grad{b}")

    ins = dict(doc_row=doc_row, gone=gone, come=come, held=part["held"])
    ins.update({x: Rows(part[x], chunks - 1) for x in ("q", "k", "v")})
    ins.update(cols=Rows(cols, chunks - 1))
    ins.update(dw=Rows(dw, chunks - 1, slice(first * WIDE, (first + blocks) * WIDE)), n1=n1)
    own = slice(first * PAIR, (first + blocks) * PAIR)
    ins.update(gwo=(gwo, "gwo", (slice(None),), own))
    outs = dict(pgrads=((tokens, 3 * blocks * PAIR), BF16))
    for b in range(blocks):
        outs[f"grad{b}"] = ((4 * width, PAIR), BF16)
    scratch = dict(state=((blocks, PAIR, WIDE), F32), gwo=((blocks * PAIR, width), BF16))
    flops = 2 * tokens * blocks * PAIR * (3 * width + 12 * CHUNK)
    return staged("attend_back", body, ins, outs, scratch, flops, chunks + blocks, 2)


def input_back(tok, rgrad, pgrads, gain, w, small):
    tokens, width = tok.shape
    blocks, chunks = len(w), tokens // CHUNK

    def body(st):
        for key in w_keys:
            st[key]
        gain = line(st["gain"])
        one = two = 0.0
        for c in range(chunks):
            rows = chunk_rows(c)
            both = jnp.concatenate([st.rows(f"pgrads{g}", c) for g in range(len(pgrads))], axis=1)
            grad = nt(both, st["w"][...])
            xhat, rstd = normalise(st.rows("tok", c).astype(F32))
            st.out("out")[rows, :] = st.rows("rgrad", c).astype(F32) + norm_back(grad, xhat, rstd, gain)
            st.send("out", rows)
            one, two = one + eight(grad * xhat), two + eight(grad)
        small = [jnp.sum(x, axis=0, keepdims=True) for x in (one, two)]
        st.out("small")[...] = jnp.concatenate(small + [st["small_in"][:6, :]], axis=0)
        st.send("small")

    ins, w_keys = {}, []
    for b in range(blocks):
        for p in range(3):
            at = (3 * b + p) * PAIR
            w_keys.append(f"w{b}_{p}")
            ins[w_keys[-1]] = (w[b], "w", (slice(None), slice(at, at + PAIR)), p)
    ins.update({f"pgrads{g}": Rows(x, 0) for g, x in enumerate(pgrads)})
    ins.update(gain=gain, tok=Rows(tok, 0), rgrad=Rows(rgrad, 0), small_in=small)
    outs = dict(out=((tokens, width), F32), small=((8, width), F32))
    scratch = dict(w=((width, 3 * blocks * PAIR), BF16))
    return staged(
        "input_back", body, ins, outs, scratch, 6 * tokens * width * width, chunks + 1
    )


def swap(x, axis, size, bit):
    return lax.ppermute(x, axis, [(i, i ^ bit) for i in range(size)])


def tie(x, *others):
    return lax.optimization_barrier((x, *others))[0]


def gate(*xs):
    return lax.optimization_barrier(xs)


def add(a, b):
    return (a.astype(F32) + b.astype(F32)).astype(BF16)


def cut(x, like):
    at, out = 0, []
    for y in like:
        out.append(x[at : at + y.shape[0]])
        at += y.shape[0]
    return out


def part(x, parts, which):
    rows = x.shape[0] // parts
    return lax.dynamic_slice_in_dim(x, which * rows, rows, 0)


def half(x, which):
    return part(x, 2, which)


def join(x, other, side):
    return jnp.where(side == 0, jnp.concatenate([x, other]), jnp.concatenate([other, x]))


def lockstep(*chains):
    results, sent = [None] * len(chains), {}
    for i, chain in enumerate(chains):
        sent[i] = next(chain)
    while sent:
        flat, tree = jax.tree.flatten(sent)
        sent = jax.tree.unflatten(tree, gate(*flat))
        for i in list(sent):
            try:
                sent[i] = chains[i].send(sent[i])
            except StopIteration as stop:
                results[i] = stop.value
                del sent[i]
    return results


def body(
    dp,
    head,
    tokens,
    doc_ids,
    pad_mask,
    norm1_gain,
    norm1_shift,
    w_qkv,
    w_out,
    norm2_gain,
    norm2_shift,
    w_hidden,
    hidden_bias,
    w_return,
    return_bias,
    out_grad,
):
    count, width = tokens.shape
    pieces = dp // 2
    core = lambda x: swap(x, "head", head, 1)
    cross = lambda x: swap(x, "head", head, 2)
    bits = dp.bit_length() - 1
    spot = lax.axis_index("dp")
    side = [(spot >> b) & 1 for b in range(bits)]
    along = lambda x, b: swap(x, "dp", dp, 1 << b)

    def leave(xs, b):
        return along(jnp.concatenate([half(x, 1 - side[b]) for x in xs]), b)

    def meet(xs, b, got):
        halves = [half(x, side[b]) for x in xs]
        return [add(x, y) for x, y in zip(halves, cut(got, halves))]

    def leave_quad(x):
        spot = lambda one, two: 2 * (side[0] ^ one) + (side[1] ^ two)
        return [
            swap(part(x, 4, spot(one, two)), "dp", dp, one + 2 * two)
            for one, two in ((1, 0), (1, 1), (0, 1))
        ]

    def meet_quad(x, got):
        x = part(x, 4, 2 * side[0] + side[1]).astype(F32)
        for y in got:
            x = x + y.astype(F32)
        return x.astype(BF16)

    def rest_of(xs):
        for b in range(2, bits - 1):
            xs = meet(xs, b, leave(xs, b))
        return xs

    def unfold(x, other, *shares):
        shape = (pieces // 2, -1, x.shape[1])
        low = jnp.where(side[0] == 0, x, other).reshape(shape)
        high = jnp.where(side[0] == 0, other, x).reshape(shape)
        at, out = 0, []
        for share in shares:
            parts = [y[:, at : at + share].reshape(-1, x.shape[1]) for y in (low, high)]
            out.append(jnp.concatenate(parts).astype(F32))
            at += share
        return out

    def spread(xs, late, *shares):
        for b in reversed(range(1, bits - 1)):
            got = yield along(jnp.concatenate(xs), b)
            xs = [join(x, y, side[b]) for x, y in zip(xs, cut(got, xs))]
        wire = along(jnp.concatenate(xs), 0)
        for _ in range(late):
            yield []
        got = yield wire
        return [unfold(x, y, *s) for x, y, s in zip(xs, cut(got, xs), shares)]

    wq, wo, wr = ([x, core(x), cross(x)] for x in (w_qkv, w_out, w_return))

    near = open_layer(
        doc_ids, pad_mask, tokens, norm1_gain, norm1_shift, wq[:2], w_hidden, hidden_bias
    )
    n1, cols, doc_row = near["n1"], near["cols"], near["doc_row"]
    wh = [near["wh"], core(near["wh"]), cross(near["wh"])]
    wq.append(core(tie(wq[2], n1)))
    come_near = core(near["last"])
    far = attend(n1, wq[2:], cols, tie(doc_row, wo[2]))
    come_far, across = gate(far["last"], wo[2])
    come = [come_near, core(come_far)]
    wo.append(core(across))
    mid = mix_feed(
        pieces,
        tokens,
        out_grad,
        [near, far],
        come,
        wo,
        cols,
        norm2_gain,
        norm2_shift,
        wh[:2],
        wr[:2],
    )
    wh.append(core(tie(wh[2], mid["n2"])))
    wr.append(core(tie(wr[2], mid["n2"])))
    down1, up1 = tie((mid["down1"], mid["up1"]), wh[3], wr[3])
    down1, up1 = core(down1), core(up1)
    end = feed(pieces, mid["n2"], out_grad, wh[2:], wr[2:], mid["dn2"])

    down3, up3, down1, up1 = gate(end["down1"], end["up1"], down1, up1)
    down3, up3 = core(down3), core(up3)
    down0, up0 = add(mid["down0"], down1), add(mid["up0"], up1)
    down2, up2 = add(end["down0"], down3), add(end["up0"], up3)

    ups, down_wire = [up0, up2], cross(down2)
    ups_wire = leave(ups, 0)
    back = unmix(
        end["dn2"],
        mid["residual"],
        out_grad,
        mid["mixed"],
        mid["inv"],
        wo,
        [near["q"], far["q"]],
        cols,
        tie(norm2_gain, down3, up3),
    )
    gone = core(back["gone"])
    acts = [mid["act"], end["act"]]
    output = finish(mid["residual"], acts, wr, tie(return_bias, back["small"]))
    gone, down_wire, ups_wire, output = gate(gone, down_wire, ups_wire, output)
    down, ups = add(down0, down_wire), meet(ups, 0, ups_wire)
    down_wires, up_wire = leave_quad(down), cross(ups[1])
    args = cols, tie(doc_row, output), n1, back["gwo"]
    side_b = attend_back(pieces, 2, back["dw"], gone, far, come[1], *args)
    grad3, up_wire, *down_wires = gate(side_b["grad1"], up_wire, *down_wires)
    grad3 = core(grad3)
    (down,) = rest_of([meet_quad(down, down_wires)])
    up = [add(ups[0], up_wire)]
    down_wire, up_wire = along(down, bits - 1), leave(up, 1)
    grad2 = add(side_b["grad0"], grad3)
    grad_wire = cross(grad2)
    args = cols, tie(doc_row, grad3), n1, back["gwo"]
    side_a = attend_back(pieces, 0, back["dw"], gone, near, come[0], *args)
    grad1, down_wire, up_wire, grad_wire = gate(
        side_a["grad1"], down_wire, up_wire, grad_wire
    )
    grad1 = core(grad1)
    down, (up,) = add(down, down_wire), rest_of(meet(up, 1, up_wire))
    up_wire = along(up, bits - 1)
    spread_down = spread([down], 1, (width // pieces,))
    down_wire = next(spread_down)
    grad = [add(add(side_a["grad0"], grad1), grad_wire)]
    grad_wire = leave(grad, 0)
    last = input_back(
        tokens,
        back["rgrad"],
        [side_a["pgrads"], side_b["pgrads"]],
        tie(norm1_gain, grad1),
        wq,
        back["small"],
    )
    small, down_wire, up_wire, grad_wire = gate(last["small"], down_wire, up_wire, grad_wire)
    up, grad = add(up, up_wire), meet(grad, 0, grad_wire)

    def finish_grad(xs):
        for b in range(1, bits - 1):
            got = yield leave(xs, b)
            xs = meet(xs, b, got)
        got = yield along(xs[0], bits - 1)
        return (yield from spread([add(xs[0], got)], 0, (3 * width // pieces, width // pieces)))

    def finish_small(x):
        one, two, three = yield [swap(x, "head", head, i) for i in (1, 2, 3)]
        x = (x + one) + (two + three)
        for b in range(bits):
            got = yield along(x, b)
            x = x + got
        return x

    def go_on(chain, got):
        try:
            while True:
                got = yield chain.send(got)
        except StopIteration as stop:
            return stop.value

    (grads,), (downs,), (ups,), small = lockstep(
        finish_grad(grad),
        go_on(spread_down, down_wire),
        spread([up], 1, (width // pieces, 16)),
        finish_small(small),
    )
    g_qkv, g_out = grads
    (down,), (up, bias_grad) = downs, ups
    g_out = g_out.reshape(width // PAIR, PAIR, PAIR)
    g_out = jnp.concatenate([g_out[i] for i in range(width // PAIR)], axis=1)
    return (
        output,
        last["out"],
        small[0],
        small[1],
        g_qkv.reshape(3, width, PAIR),
        g_out,
        small[2],
        small[3],
        up,
        bias_grad[0],
        down,
        small[4],
    )


def solution(mesh):
    return jax.shard_map(
        functools.partial(body, mesh.shape["dp"], mesh.shape["head"]),
        mesh=mesh,
        in_specs=(
            P(("dp", "head"), None),
            P("dp", None),
            P("dp", None),
            P(),
            P(),
            P(None, None, "head"),
            P("head", None),
            P(),
            P(),
            P(None, "head"),
            P("head"),
            P("head", None),
            P(),
            P(("dp", "head"), None),
        ),
        out_specs=(
            P(("dp", "head"), None),
            P(("dp", "head"), None),
            P(),
            P(),
            P(None, None, "head"),
            P("head", None),
            P(),
            P(),
            P(None, "head"),
            P("head"),
            P("head", None),
            P(),
        ),
        check_vma=False,
    )
```

```python
import functools

import jax
import jax.numpy as jnp
from jax import lax
from jax.experimental import pallas as pl
from jax.experimental.pallas import tpu as pltpu
from jax.sharding import PartitionSpec as P

HEAD_DIM = 64
PAIR = 2 * HEAD_DIM
WIDE = 2 * PAIR
CHUNK = 256
LANES = 128
EPSILON = 1e-05
BELOW_ONE = 1.0 - 2.0**-8
F32 = jnp.float32
BF16 = jnp.bfloat16
VMEM_BYTES = 60 * 1024 * 1024

DOC, LIVE, READ_HALF, READ_CHUNK, IN_LAST, CARRIED, FIRST_HALF = range(7)


def nn(a, b):
    return lax.dot_general(a, b, (((1,), (0,)), ((), ())), preferred_element_type=F32)


def nt(a, b):
    return lax.dot_general(a, b, (((1,), (1,)), ((), ())), preferred_element_type=F32)


def tn(a, b):
    return lax.dot_general(a, b, (((0,), (0,)), ((), ())), preferred_element_type=F32)


def normalise(x):
    centre = x - jnp.mean(x, axis=-1, keepdims=True)
    rstd = lax.rsqrt(jnp.mean(centre * centre, axis=-1, keepdims=True) + EPSILON)
    return centre * rstd, rstd


def norm_back(grad, xhat, rstd, gain):
    scaled = grad * gain
    mean_one = jnp.mean(scaled, axis=-1, keepdims=True)
    mean_two = jnp.mean(scaled * xhat, axis=-1, keepdims=True)
    return rstd * (scaled - mean_one - xhat * mean_two)


def line(ref):
    return ref[...].astype(F32).reshape(1, ref.shape[0])


def eight(x):
    return jnp.sum(x.reshape(x.shape[0] // 8, 8, x.shape[1]), axis=0)


def head_lanes(shape):
    return lax.broadcasted_iota(jnp.int32, shape, len(shape) - 1) % PAIR < HEAD_DIM


def pair_mask(width):
    rows = lax.broadcasted_iota(jnp.int32, (PAIR, width), 0) < HEAD_DIM
    return rows == head_lanes((PAIR, width))


def allowed_mask(doc_col, doc_row):
    t = lax.broadcasted_iota(jnp.int32, (CHUNK, CHUNK), 0)
    s = lax.broadcasted_iota(jnp.int32, (CHUNK, CHUNK), 1)
    return (doc_col == doc_row) & (s <= t)


def feature(x):
    return jnp.where(x > 0, x + 1.0, jnp.exp(jnp.minimum(x, 0.0)))


def chunk_rows(c):
    return slice(c * CHUNK, (c + 1) * CHUNK)


def column(cols, which):
    return cols[:, which : which + 1]


def stack(x, masks):
    return jnp.concatenate([jnp.where(mask, x, jnp.zeros_like(x)) for mask in masks], axis=0)


class Rows:
    def __init__(self, array, first, columns=None):
        self.array = array
        self.columns = columns or slice(0, array.shape[-1])
        self.shape = array.shape[:-1] + (self.columns.stop - self.columns.start,)
        rows = self.shape[-2]
        rest = slice(CHUNK, rows) if first == 0 else slice(0, rows - CHUNK)
        self.first, self.parts = first, [chunk_rows(first), rest]

    def index(self, rows, columns):
        return (slice(None),) * (len(self.shape) - 2) + (rows, columns)


class Staged:
    def __init__(self, specs, late, ins, outs, scratch, in_sem, out_sem):
        self.specs, self.ins, self.outs, self.scratch = specs, ins, outs, scratch
        self.out_sem, self.sent = out_sem, []
        self.pending = {}
        begin = list(ins)[: len(ins) - late]
        for turn, names in enumerate((begin, begin, list(ins)[len(ins) - late :])):
            for name in names:
                spec, (src, dst) = specs[name], ins[name]
                if src is None:
                    continue
                if isinstance(spec, Rows):
                    rows = spec.parts[turn]
                    src = src.at[spec.index(rows, spec.columns)]
                    dst = dst.at[spec.index(rows, slice(None))]
                elif turn == 1:
                    continue
                copy = pltpu.make_async_copy(src, dst, in_sem.at[len(self.pending)])
                copy.start()
                self.pending[name, turn % 2] = copy

    def __getitem__(self, name):
        for key in [key for key in self.pending if key[0] == name]:
            self.pending.pop(key).wait()
        return self.ins[name][1] if name in self.ins else self.scratch[name]

    def rows(self, name, c):
        spec = self.specs[name]
        if not isinstance(spec, Rows):
            return self[name][chunk_rows(c), :]
        key = (name, int(c != spec.first))
        if key in self.pending:
            self.pending.pop(key).wait()
        return self.ins[name][1][spec.index(chunk_rows(c), slice(None))]

    def out(self, name):
        return self.outs[name][1]

    def send(self, name, *index):
        dst, src = self.outs[name]
        if index:
            dst, src = dst.at[index], src.at[index]
        copy = pltpu.make_async_copy(src, dst, self.out_sem.at[len(self.sent)])
        copy.start()
        self.sent.append(copy)

    def finish(self):
        for copy in list(self.pending.values()) + self.sent:
            copy.wait()


def staged(name, body, ins, outs, scratch, flops, sends, late=0):
    in_names, out_names, scratch_names = list(ins), list(outs), list(scratch)
    arrays, in_specs, own = [], [], []
    for value in ins.values():
        value = value.array if isinstance(value, Rows) else value
        scalars = isinstance(value, tuple) and isinstance(value[0], str)
        arrays.append(value[1] if scalars else value[0] if isinstance(value, tuple) else value)
        space = pltpu.SMEM if scalars else pl.ANY
        in_specs.append(pl.BlockSpec(memory_space=space))
        if not isinstance(value, tuple):
            own.append(pltpu.VMEM(ins[in_names[len(arrays) - 1]].shape, value.dtype))

    def kernel(*refs):
        refs = list(refs)
        take = lambda n: [refs.pop(0) for _ in range(n)]
        src, dst = take(len(in_names)), take(len(out_names))
        own_refs, out_refs = take(len(own)), take(len(out_names))
        held = dict(zip(scratch_names, take(len(scratch_names))))
        in_sem, out_sem = refs
        ends = {}
        for key, ref in zip(in_names, src):
            value = ins[key]
            if not isinstance(value, tuple):
                ends[key] = (ref, own_refs.pop(0))
            elif isinstance(value[0], str):
                ends[key] = (None, ref)
            else:
                ends[key] = (ref.at[value[3:]] if value[3:] else ref, held[value[1]].at[value[2]])
        stage = Staged(ins, late, ends, dict(zip(out_names, zip(dst, out_refs))), held, in_sem, out_sem)
        body(stage)
        stage.finish()

    shapes = list(outs.values())
    copies = sum(2 if isinstance(x, Rows) else 1 for x in ins.values())
    out = pl.pallas_call(
        kernel,
        in_specs=in_specs,
        out_specs=[pl.BlockSpec(memory_space=pl.ANY)] * len(out_names),
        out_shape=[jax.ShapeDtypeStruct(*s) for s in shapes],
        scratch_shapes=own
        + [pltpu.VMEM(*s) for s in shapes]
        + [pltpu.VMEM(*s) for s in scratch.values()]
        + [pltpu.SemaphoreType.DMA((copies,)), pltpu.SemaphoreType.DMA((sends,))],
        compiler_params=pltpu.CompilerParams(vmem_limit_bytes=VMEM_BYTES),
        cost_estimate=pl.CostEstimate(flops=flops, bytes_accessed=4 << 20, transcendentals=0),
        name=name,
    )(*arrays)
    return dict(zip(out_names, out))


def attend_chunk(st, blocks, c, n1, cols, doc_row):
    w, state, every = st["w"], st["state"], range(blocks)
    rows = chunk_rows(c)
    live, reads = column(cols, LIVE), column(cols, READ_CHUNK)
    in_last = column(cols, IN_LAST).astype(BF16)
    carried = cols[0:1, CARRIED : CARRIED + 1]
    mask = allowed_mask(column(cols, DOC), doc_row[:, rows])
    mask = jnp.concatenate([mask, mask], axis=0)
    q_all = feature(nn(n1, w[0])).astype(BF16)
    k_all = (feature(nn(n1, w[1])) * live).astype(BF16)
    v_all = nn(n1, w[2]).astype(BF16)
    here = head_lanes((CHUNK, WIDE))
    own = [here[:, :PAIR], jnp.logical_not(here[:, :PAIR])]
    block_diagonal = pair_mask(WIDE)
    ones = jnp.ones((CHUNK, PAIR), BF16)
    part = lambda x, b: x[:, b * PAIR : (b + 1) * PAIR]
    q, k, v = ([part(x, b) for b in every] for x in (q_all, k_all, v_all))
    for b in every:
        st.out("q")[b, rows], st.out("k")[b, rows], st.out("v")[b, rows] = q[b], k[b], v[b]
    scores = [nt(stack(q[b], own), k[b]) for b in every]
    wide = [jnp.concatenate([v[b], ones], axis=1) for b in every]
    grown = [tn(k[b] * in_last, wide[b]) for b in every]
    scores = [jnp.where(mask, scores[b], 0.0).astype(BF16) for b in every]
    both = [nn(scores[b], wide[b]) for b in every]
    total = [jnp.where(here, both[b][:CHUNK], both[b][CHUNK:]) for b in every]
    for b in every:
        if c > 0:
            low = state[b].astype(BF16)
            st.out("held")[c, b] = low
            total[b] = total[b] + reads * nn(q[b], low)
        else:
            st.out("held")[c, b] = jnp.zeros((PAIR, WIDE), BF16)
        st.out("num")[b, rows], st.out("tot")[b, rows] = total[b][:, :PAIR], total[b][:, PAIR:]
        more = jnp.where(block_diagonal, grown[b], 0.0)
        state[b] = more if c == 0 else carried * state[b] + more
    for name in ("q", "k", "v", "num", "tot"):
        st.send(name, slice(None), rows)


def attend_finish(st, blocks):
    for b in range(blocks):
        st.out("last")[b ^ 1] = st["state"][b].astype(BF16)
    st.send("last")
    st.send("held")


def attend_outs(tokens, blocks):
    part = (blocks, tokens, PAIR)
    return dict(
        q=(part, BF16),
        k=(part, BF16),
        v=(part, BF16),
        num=(part, F32),
        tot=(part, F32),
        held=((tokens // CHUNK, blocks, PAIR, WIDE), BF16),
        last=((blocks, PAIR, WIDE), BF16),
    )


def attend_scratch(width, blocks):
    return dict(w=((3, width, blocks * PAIR), BF16), state=((blocks, PAIR, WIDE), F32))


def attend_weights(w):
    everything = slice(None)
    return {
        f"w{b}": (x, "w", (everything, everything, slice(b * PAIR, (b + 1) * PAIR)))
        for b, x in enumerate(w)
    }


def attend_flops(tokens, width, blocks):
    return 2 * tokens * blocks * PAIR * (3 * width + 4 * CHUNK)


def make_flags(where, doc_ids, pad_mask, count):
    row, place = where[0], where[1]

    def here(x):
        whole = x[0:1, :]
        for r in range(1, x.shape[0]):
            whole = jnp.where(row == r, x[r : r + 1, :], whole)
        part = whole[:, :count]
        for i in range(1, x.shape[1] // count):
            part = jnp.where(place == i, whole[:, i * count : (i + 1) * count], part)
        return whole, part

    whole, docs = here(doc_ids)
    _, live = here(pad_mask)
    edge = whole[:, count - 1 : count]
    second = jnp.where(place > 0, 1.0, 0.0)
    as_float = lambda x: jnp.where(x, 1.0, 0.0)
    reads, in_last, carried = [], [], []
    before = None
    for c in range(count // CHUNK):
        part = docs[:, chunk_rows(c)]
        end = part[:, CHUNK - 1 : CHUNK]
        in_last.append(as_float(part == end))
        if before is None:
            reads.append(jnp.zeros((1, CHUNK), F32))
            carried.append(jnp.zeros((1, CHUNK), F32))
        else:
            reads.append(as_float(part == before))
            carried.append(as_float(jnp.broadcast_to(end, part.shape) == before))
        before = end
    join = lambda x: jnp.concatenate(x, axis=1)
    doc_line = docs.astype(F32)
    lines = [
        doc_line,
        live.astype(F32),
        as_float(docs == edge) * second,
        join(reads),
        join(in_last),
        join(carried),
        jnp.broadcast_to(1.0 - second, (1, count)).astype(F32),
    ]
    lines.append(jnp.zeros((LANES - len(lines), count), F32))
    return jnp.concatenate(lines, axis=0).T, doc_line


def open_layer(where, doc_ids, pad_mask, tok, gain, shift, w, w_hidden, hidden_bias):
    tokens, width = tok.shape
    blocks, chunks, hidden = len(w), tokens // CHUNK, w_hidden.shape[1]

    def body(st):
        cols, doc_row = make_flags(st["where"], st["doc_ids"], st["pad_mask"], tokens)
        st.out("cols")[...], st.out("doc_row")[...] = cols, doc_row
        st.send("cols")
        st.send("doc_row")
        cols, doc_row, n1 = st.out("cols"), st.out("doc_row"), st.out("n1")
        gain, shift = line(st["gain"]), line(st["shift"])
        for c in range(chunks):
            xhat, _ = normalise(st.rows("tok", c).astype(F32))
            n1[chunk_rows(c), :] = (xhat * gain + shift).astype(BF16)
        st.send("n1")
        for b in range(blocks):
            st[f"w{b}"]
        for c in range(chunks):
            attend_chunk(st, blocks, c, n1[chunk_rows(c), :], cols[chunk_rows(c), :], doc_row)
        attend_finish(st, blocks)
        st["wh"][width:, :] = jnp.broadcast_to(line(st["bias"]).astype(BF16), (16, hidden))
        st["w_hidden"]
        st.out("wh")[...] = st["wh"][...]
        st.send("wh")

    ins = dict(where=("smem", where), doc_ids=doc_ids, pad_mask=pad_mask, tok=Rows(tok, 0))
    ins.update(gain=gain, shift=shift, **attend_weights(w), bias=hidden_bias)
    ins.update(w_hidden=(w_hidden, "wh", (slice(0, width),)))
    outs = dict(
        cols=((tokens, LANES), F32),
        doc_row=((1, tokens), F32),
        n1=((tokens, width), BF16),
        wh=((width + 16, hidden), BF16),
    )
    outs.update(attend_outs(tokens, blocks))
    scratch = attend_scratch(width, blocks)
    scratch["wh"] = ((width + 16, hidden), BF16)
    flops = attend_flops(tokens, width, blocks)
    return staged("open", body, ins, outs, scratch, flops, 5 * chunks + 6, 1)


def attend(n1, w, cols, doc_row):
    tokens, width = n1.shape
    blocks, chunks = len(w), tokens // CHUNK

    def body(st):
        doc_row = st["doc_row"]
        for b in range(blocks):
            st[f"w{b}"]
        for c in range(chunks):
            attend_chunk(st, blocks, c, st.rows("n1", c), st.rows("cols", c), doc_row)
        attend_finish(st, blocks)

    ins = dict(doc_row=doc_row, **attend_weights(w))
    ins.update(n1=Rows(n1, 0), cols=Rows(cols, 0))
    flops = attend_flops(tokens, width, blocks)
    return staged(
        "attend",
        body,
        ins,
        attend_outs(tokens, blocks),
        attend_scratch(width, blocks),
        flops,
        5 * chunks + 2,
    )


def gelu_pair(x):
    cdf = 0.5 + 0.5 * lax.erf(x * 0.7071067811865476)
    density = 0.3989422804014327 * jnp.exp(-0.5 * x * x)
    return x * cdf, cdf + x * density


def mix_chunk(st, groups, c):
    cols, w, rows = st.rows("cols", c), st["wo"], chunk_rows(c)
    live, reads = column(cols, LIVE), column(cols, READ_HALF)
    q, num, tot = ([st.rows(f"{x}{g}", c) for g in range(groups)] for x in ("q", "num", "tot"))
    mixed, inv_out = st.out("mixed"), st.out("inv")
    for b in range(2 * groups):
        g, i = divmod(b, 2)
        lanes = slice(b * PAIR, (b + 1) * PAIR)
        far = reads * nn(q[g][i], st[f"come{g}"][i])
        inv = 1.0 / jnp.maximum(tot[g][i] + far[:, PAIR:], 1.0)
        inv_out[rows, lanes] = jnp.where(inv < 1.0, jnp.minimum(inv, BELOW_ONE), 1.0).astype(BF16)
        value = (num[g][i] + far[:, :PAIR]) * inv * live
        mixed[rows, lanes] = value.astype(BF16)
    residual = st.rows("tok", c).astype(F32) + nn(mixed[rows, :], w[...])
    st.out("residual")[rows, :] = residual
    xhat, _ = normalise(residual)
    n2 = (xhat * line(st["gain"]) + line(st["shift"])).astype(BF16)
    st.out("n2")[rows, :] = n2
    for name in ("mixed", "inv", "residual", "n2"):
        st.send(name, rows)


def feed_chunk(st, c, n2, bias, resume):
    rows = chunk_rows(c)
    wh, wr = st["wh"].at[: n2.shape[1]], st["wr"]
    value, slope = gelu_pair(nn(n2, wh[...]) + bias)
    st.out("act")[rows, :] = value.astype(BF16)
    st.send("act", rows)
    grad = nt(st.rows("dy", c), wr[...]) * slope
    low = grad.astype(BF16)
    st["hg"][rows, :] = low
    back = nt(low, wh[...])
    st.out("dn2")[rows, :] = back + st.rows("dn2_in", c) if resume else back
    st.send("dn2", rows)
    return eight(grad)


def feed_grads(st, blocks, pieces, n2, bias_grad):
    width, hidden = n2.shape[1], bias_grad.shape[1] // blocks
    bias_grad = jnp.sum(bias_grad, axis=0, keepdims=True).astype(BF16)
    for b in range(blocks):
        part = slice(b * hidden, (b + 1) * hidden)
        down, up = st.out(f"down{b}"), st.out(f"up{b}")
        down[...] = tn(st.out("act")[:, part], st["dy"][...]).astype(BF16)
        st.send(f"down{b}")
        grad = tn(n2[...], st["hg"][:, part]).astype(BF16)
        rows, step = width // pieces, up.shape[0] // pieces
        for i in range(pieces):
            up[i * step : i * step + rows, :] = grad[i * rows : (i + 1) * rows, :]
            tail = jnp.broadcast_to(bias_grad[:, part], (step - rows, hidden))
            up[i * step + rows : (i + 1) * step, :] = tail
        st.send(f"up{b}")


def feed_parts(tokens, width, pieces, wh, wr):
    blocks, hidden = len(wr), wr[0].shape[0]
    everything = slice(None)
    ins = {}
    for b in range(blocks):
        part = slice(b * hidden, (b + 1) * hidden)
        ins[f"wh{b}"] = (wh[b], "wh", (everything, part))
        ins[f"wr{b}"] = (wr[b], "wr", (part, everything))
    outs = dict(act=((tokens, blocks * hidden), BF16), dn2=((tokens, width), F32))
    for b in range(blocks):
        outs[f"down{b}"] = ((hidden, width), BF16)
        outs[f"up{b}"] = ((width + 16 * pieces, hidden), BF16)
    scratch = dict(
        wh=((width + 16, blocks * hidden), BF16),
        wr=((blocks * hidden, width), BF16),
        hg=((tokens, blocks * hidden), BF16),
    )
    return ins, outs, scratch, 10 * tokens * width * hidden * blocks


def feed_start(st, blocks, width):
    for b in range(blocks):
        st[f"wh{b}"], st[f"wr{b}"]
    return st["wh"][width : width + 1, :].astype(F32)


def mix_feed(pieces, tok, dy, parts, come, wo, cols, gain, shift, wh, wr):
    tokens, width = tok.shape
    blocks, groups, chunks = len(wh), len(parts), tokens // CHUNK

    def body(st):
        for b in range(2 * groups):
            st[f"wo{b}"]
        for c in range(chunks):
            mix_chunk(st, groups, c)
        n2 = st.out("n2")
        bias = feed_start(st, blocks, width)
        bias_grad = 0.0
        for c in range(chunks):
            bias_grad = bias_grad + feed_chunk(st, c, n2[chunk_rows(c), :], bias, False)
        feed_grads(st, blocks, pieces, n2, bias_grad)

    ins = dict(cols=Rows(cols, 0), tok=Rows(tok, 0), gain=gain, shift=shift)
    for g, part in enumerate(parts):
        ins.update({f"{x}{g}": Rows(part[x], 0) for x in ("q", "num", "tot")})
        ins[f"come{g}"] = come[g]
    for b, x in enumerate(wo):
        ins[f"wo{b}"] = (x, "wo", (slice(b * PAIR, (b + 1) * PAIR),))
    more, outs, scratch, flops = feed_parts(tokens, width, pieces, wh, wr)
    ins.update(dy=dy, **more)
    outs.update(
        mixed=((tokens, width), BF16),
        inv=((tokens, width), BF16),
        residual=((tokens, width), F32),
        n2=((tokens, width), BF16),
    )
    scratch["wo"] = ((width, width), BF16)
    late = 1 + len(more)
    return staged("mix_feed", body, ins, outs, scratch, 0, 6 * chunks + 2 * blocks, late)


def feed(pieces, n2, dy, wh, wr, dn2):
    tokens, width = n2.shape
    blocks, chunks = len(wh), tokens // CHUNK

    def body(st):
        bias = feed_start(st, blocks, width)
        bias_grad = 0.0
        for c in range(chunks):
            bias_grad = bias_grad + feed_chunk(st, c, st.rows("n2", c), bias, True)
        feed_grads(st, blocks, pieces, st["n2"], bias_grad)

    ins = dict(n2=n2)
    more, outs, scratch, flops = feed_parts(tokens, width, pieces, wh, wr)
    ins.update(more)
    ins.update(dy=dy, dn2_in=dn2)
    return staged("feed", body, ins, outs, scratch, flops, 2 * chunks + 2 * blocks)


def unmix_chunk(st, blocks, c):
    cols, rows = st.rows("cols", c), chunk_rows(c)
    live, reads = column(cols, LIVE), column(cols, READ_HALF).astype(BF16)
    xhat, rstd = normalise(st.rows("residual", c))
    grad = st.rows("dn2", c)
    wide = st.rows("dy", c).astype(F32)
    rgrad = wide + norm_back(grad, xhat, rstd, line(st["gain"]))
    low = rgrad.astype(BF16)
    st.out("rgrad")[rows, :] = low
    mgrad = nt(low, st["wo"][...]) * live
    sums = pair_mask(PAIR).astype(BF16)
    sums = jnp.concatenate([sums, sums], axis=0)
    inv, mixed = st.rows("inv", c).astype(F32), st.rows("mixed", c).astype(F32)
    q = [st.rows(f"q{g}", c) for g in range(blocks // 2)]
    for b in range(blocks):
        lanes = slice(b * PAIR, (b + 1) * PAIR)
        one, scale = mgrad[:, lanes], inv[:, lanes]
        dw = (one * scale).astype(BF16)
        terms = one * mixed[:, lanes]
        high = terms.astype(BF16)
        rest = (terms - high.astype(F32)).astype(BF16)
        total = nn(jnp.concatenate([high, rest], axis=1), sums)
        tg = jnp.where(scale < 1.0, -total * scale, 0.0).astype(BF16)
        st.out("dw")[rows, b * WIDE : b * WIDE + PAIR] = dw
        st.out("dw")[rows, b * WIDE + PAIR : (b + 1) * WIDE] = tg
        st["reading"][rows, lanes] = q[b // 2][b % 2] * reads
    st.send("rgrad", rows)
    st.send("dw", rows)
    return eight(grad * xhat), eight(grad), eight(wide)


def unmix(dn2, residual, dy, mixed, inv, wo, q, cols, gain):
    tokens, width = dy.shape
    blocks, chunks = len(wo), tokens // CHUNK

    def body(st):
        for b in range(blocks):
            st[f"wo{b}"]
        small = [0.0, 0.0, 0.0]
        for c in range(chunks):
            small = [a + b for a, b in zip(small, unmix_chunk(st, blocks, c))]
        small = [jnp.sum(x, axis=0, keepdims=True) for x in small]
        st.out("small")[...] = jnp.concatenate(small + [jnp.zeros((5, width), F32)], axis=0)
        st.send("small")
        block_diagonal = pair_mask(WIDE)
        for b in range(blocks):
            lanes, wide = slice(b * PAIR, (b + 1) * PAIR), slice(b * WIDE, (b + 1) * WIDE)
            grown = tn(st["reading"][:, lanes], st.out("dw")[:, wide])
            st.out("gone")[b ^ 1] = jnp.where(block_diagonal, grown, 0.0).astype(BF16)
        st.send("gone")
        st.out("gwo")[...] = tn(st["mixed"][...], st.out("rgrad")[...]).astype(BF16)
        st.send("gwo")

    ins = dict(gain=gain, cols=Rows(cols, 0))
    ins.update(residual=Rows(residual, 0), dn2=Rows(dn2, 0), dy=Rows(dy, 0))
    for b, x in enumerate(wo):
        ins[f"wo{b}"] = (x, "wo", (slice(b * PAIR, (b + 1) * PAIR),))
    ins.update(inv=Rows(inv, 0), mixed=Rows(mixed, 0))
    ins.update({f"q{g}": Rows(x, 0) for g, x in enumerate(q)})
    outs = dict(
        rgrad=((tokens, width), BF16),
        dw=((tokens, 2 * width), BF16),
        gone=((blocks, PAIR, WIDE), BF16),
        gwo=((width, width), BF16),
        small=((8, width), F32),
    )
    scratch = dict(wo=((width, width), BF16), reading=((tokens, width), BF16))
    return staged(
        "unmix", body, ins, outs, scratch, 6 * tokens * width * width, 2 * chunks + 3
    )


def finish(residual, act, wr, bias):
    tokens, width = residual.shape

    def body(st):
        total = 0.0
        for i in range(len(wr)):
            total = total + nn(st[f"act{i}"][...], st[f"wr{i}"][...])
        total = total + st["residual"][...] + line(st["bias"])
        st.out("out")[...] = total.astype(BF16)
        st.send("out")

    ins, own, scratch = {}, [], {}
    for x in act:
        own += [(x, slice(i, i + wr[0].shape[0])) for i in range(0, x.shape[1], wr[0].shape[0])]
    for i, (x, columns) in enumerate(own):
        scratch[f"part{i}"] = ((tokens, wr[i].shape[0]), BF16)
        ins[f"act{i}"] = (x, f"part{i}", (slice(None),), slice(None), columns)
        ins[f"wr{i}"] = wr[i]
    ins.update(residual=residual, bias=bias)
    outs = dict(out=((tokens, width), BF16))
    flops = 2 * tokens * width * width * len(wr)
    return staged("finish", body, ins, outs, scratch, flops, 1)["out"]


def attend_back_chunk(st, blocks, c):
    cols, rows = st.rows("cols", c), chunk_rows(c)
    reads, reads_far = column(cols, READ_CHUNK), column(cols, READ_HALF)
    in_last = column(cols, IN_LAST)
    carried = cols[0:1, CARRIED : CARRIED + 1]
    mask = allowed_mask(column(cols, DOC), st["doc_row"][:, rows])
    here = head_lanes((CHUNK, PAIR))
    block_diagonal = pair_mask(WIDE)
    share = jnp.full((CHUNK, PAIR), 1.0 / HEAD_DIM, BF16)
    once = lax.broadcasted_iota(jnp.int32, (PAIR, WIDE), 1) < PAIR
    once = jnp.where(once, 1.0, 1.0 / HEAD_DIM).astype(BF16)
    out, state = st.out("pgrads"), st["state"]
    every = range(blocks)
    own = [here, jnp.logical_not(here)]
    mask2 = jnp.concatenate([mask, mask], axis=0)
    own_wide = [jnp.concatenate([o, o], axis=1) for o in own]
    pick = lambda x: jnp.where(here, x[:CHUNK], x[CHUNK:])
    q, k, v = ([st.rows(x, c)[b] for b in every] for x in ("q", "k", "v"))
    dw = st.rows("dw", c)
    dw = [dw[:, b * WIDE : (b + 1) * WIDE] for b in every]
    value_share = [jnp.concatenate([v[b], share], axis=1) for b in every]
    scores = [nt(stack(q[b], own), k[b]) for b in every]
    sgrad = [nt(stack(dw[b], own_wide), value_share[b]) for b in every]
    q_t = [q[b].T for b in every]
    dw_t = [dw[b][:, :PAIR].T for b in every]
    scores = [jnp.where(mask2, scores[b], 0.0).astype(BF16) for b in every]
    sgrad = [jnp.where(mask2, sgrad[b], 0.0).astype(BF16) for b in every]
    low = [state[b].astype(BF16) for b in every]
    dq = [reads_far * nt(dw[b], st["come"][b] * once) for b in every]
    if c > 0:
        dq = [dq[b] + reads * nt(dw[b], st["held"][c, b] * once) for b in every]
    dq = [dq[b] + pick(nn(sgrad[b], k[b])) for b in every]
    dk, dv = [], []
    for b in every:
        for out_t, left, right in ((dk, q_t[b], sgrad[b]), (dv, dw_t[b], scores[b])):
            both = []
            for h in range(2):
                feats = slice(h * HEAD_DIM, (h + 1) * HEAD_DIM)
                both.append(nn(left[feats], right[h * CHUNK : (h + 1) * CHUNK]))
            out_t.append(jnp.concatenate(both, axis=0).T)
    for b in every:
        dk_b = dk[b] + in_last * nt(value_share[b], low[b])
        dv_b = dv[b] + in_last * nn(k[b], low[b][:, :PAIR])
        at = 3 * b * PAIR
        dq_b = dq[b] * jnp.minimum(q[b].astype(F32), 1.0)
        dk_b = dk_b * jnp.minimum(k[b].astype(F32), 1.0)
        out[rows, at : at + PAIR] = dq_b.astype(BF16)
        out[rows, at + PAIR : at + 2 * PAIR] = dk_b.astype(BF16)
        out[rows, at + 2 * PAIR : at + 3 * PAIR] = dv_b.astype(BF16)
        if c > 0:
            grown = tn(q[b] * reads.astype(BF16), dw[b])
            state[b] = carried * state[b] + jnp.where(block_diagonal, grown, 0.0)
    st.send("pgrads", rows)


class PieceRows:
    def __init__(self, out, rows_one, rows_two, pieces):
        self.out, self.one, self.two = out, rows_one // pieces, rows_two // pieces

    def write(self, at, rows, share, offset):
        done, total = 0, rows.shape[0]
        while done < total:
            piece, inside = divmod(at + done, share)
            take = min(total - done, share - inside)
            start = piece * (self.one + self.two) + offset + inside
            self.out[start : start + take, :] = rows[done : done + take, :]
            done += take

    def first(self, at, rows):
        self.write(at, rows, self.one, 0)

    def second(self, at, rows):
        self.write(at, rows, self.two, self.one)


def attend_back(pieces, first, dw, gone, part, come, cols, doc_row, n1, gwo):
    tokens, width = n1.shape
    blocks, chunks = part["q"].shape[0], tokens // CHUNK

    def body(st):
        flag = st.rows("cols", chunks - 1)[0:1, FIRST_HALF : FIRST_HALF + 1]
        for b in range(blocks):
            st["state"][b] = st["gone"][first + b].astype(F32) * flag
        for c in reversed(range(chunks)):
            attend_back_chunk(st, blocks, c)
        for b in range(blocks):
            grad = tn(st["n1"][...], st.out("pgrads")[:, 3 * b * PAIR : 3 * (b + 1) * PAIR])
            grad = grad.astype(BF16)
            block = st["gwo"][b * PAIR : (b + 1) * PAIR, :]
            fill = PieceRows(st.out(f"grad{b}"), 3 * width, width, pieces)
            for p in range(3):
                fill.first(p * width, grad[:, p * PAIR : (p + 1) * PAIR])
            for j in range(width // PAIR):
                fill.second(j * PAIR, block[:, j * PAIR : (j + 1) * PAIR])
            st.send(f"grad{b}")

    ins = dict(doc_row=doc_row, gone=gone, come=come, held=part["held"])
    ins.update({x: Rows(part[x], chunks - 1) for x in ("q", "k", "v")})
    ins.update(cols=Rows(cols, chunks - 1))
    ins.update(dw=Rows(dw, chunks - 1, slice(first * WIDE, (first + blocks) * WIDE)), n1=n1)
    own = slice(first * PAIR, (first + blocks) * PAIR)
    ins.update(gwo=(gwo, "gwo", (slice(None),), own))
    outs = dict(pgrads=((tokens, 3 * blocks * PAIR), BF16))
    for b in range(blocks):
        outs[f"grad{b}"] = ((4 * width, PAIR), BF16)
    scratch = dict(state=((blocks, PAIR, WIDE), F32), gwo=((blocks * PAIR, width), BF16))
    flops = 2 * tokens * blocks * PAIR * (3 * width + 12 * CHUNK)
    return staged("attend_back", body, ins, outs, scratch, flops, chunks + blocks, 2)


def input_back(tok, rgrad, pgrads, gain, w, small):
    tokens, width = tok.shape
    blocks, chunks = len(w), tokens // CHUNK

    def body(st):
        for key in w_keys:
            st[key]
        gain = line(st["gain"])
        one = two = 0.0
        for c in range(chunks):
            rows = chunk_rows(c)
            both = jnp.concatenate([st.rows(f"pgrads{g}", c) for g in range(len(pgrads))], axis=1)
            grad = nt(both, st["w"][...])
            xhat, rstd = normalise(st.rows("tok", c).astype(F32))
            st.out("out")[rows, :] = st.rows("rgrad", c).astype(F32) + norm_back(grad, xhat, rstd, gain)
            st.send("out", rows)
            one, two = one + eight(grad * xhat), two + eight(grad)
        small = [jnp.sum(x, axis=0, keepdims=True) for x in (one, two)]
        st.out("small")[...] = jnp.concatenate(small + [st["small_in"][:6, :]], axis=0)
        st.send("small")

    ins, w_keys = {}, []
    for b in range(blocks):
        for p in range(3):
            at = (3 * b + p) * PAIR
            w_keys.append(f"w{b}_{p}")
            ins[w_keys[-1]] = (w[b], "w", (slice(None), slice(at, at + PAIR)), p)
    ins.update({f"pgrads{g}": Rows(x, 0) for g, x in enumerate(pgrads)})
    ins.update(gain=gain, tok=Rows(tok, 0), rgrad=Rows(rgrad, 0), small_in=small)
    outs = dict(out=((tokens, width), F32), small=((8, width), F32))
    scratch = dict(w=((width, 3 * blocks * PAIR), BF16))
    return staged(
        "input_back", body, ins, outs, scratch, 6 * tokens * width * width, chunks + 1
    )


def swap(x, axis, size, bit):
    return lax.ppermute(x, axis, [(i, i ^ bit) for i in range(size)])


def tie(x, *others):
    return lax.optimization_barrier((x, *others))[0]


def gate(*xs):
    return lax.optimization_barrier(xs)


def add(a, b):
    return (a.astype(F32) + b.astype(F32)).astype(BF16)


def cut(x, like):
    at, out = 0, []
    for y in like:
        out.append(x[at : at + y.shape[0]])
        at += y.shape[0]
    return out


def part(x, parts, which):
    rows = x.shape[0] // parts
    return lax.dynamic_slice_in_dim(x, which * rows, rows, 0)


def half(x, which):
    return part(x, 2, which)


def join(x, other, side):
    return jnp.where(side == 0, jnp.concatenate([x, other]), jnp.concatenate([other, x]))


def lockstep(*chains):
    results, sent = [None] * len(chains), {}
    for i, chain in enumerate(chains):
        sent[i] = next(chain)
    while sent:
        flat, tree = jax.tree.flatten(sent)
        sent = jax.tree.unflatten(tree, gate(*flat))
        for i in list(sent):
            try:
                sent[i] = chains[i].send(sent[i])
            except StopIteration as stop:
                results[i] = stop.value
                del sent[i]
    return results


def body(
    dp,
    head,
    tokens,
    doc_ids,
    pad_mask,
    norm1_gain,
    norm1_shift,
    w_qkv,
    w_out,
    norm2_gain,
    norm2_shift,
    w_hidden,
    hidden_bias,
    w_return,
    return_bias,
    out_grad,
):
    count, width = tokens.shape
    pieces = dp // 2
    core = lambda x: swap(x, "head", head, 1)
    cross = lambda x: swap(x, "head", head, 2)
    bits = dp.bit_length() - 1
    spot = lax.axis_index("dp")
    side = [(spot >> b) & 1 for b in range(bits)]
    along = lambda x, b: swap(x, "dp", dp, 1 << b)

    def leave(xs, b):
        return along(jnp.concatenate([half(x, 1 - side[b]) for x in xs]), b)

    def meet(xs, b, got):
        halves = [half(x, side[b]) for x in xs]
        return [add(x, y) for x, y in zip(halves, cut(got, halves))]

    def leave_quad(x):
        spot = lambda one, two: 2 * (side[0] ^ one) + (side[1] ^ two)
        return [
            swap(part(x, 4, spot(one, two)), "dp", dp, one + 2 * two)
            for one, two in ((1, 0), (1, 1), (0, 1))
        ]

    def meet_quad(x, got):
        x = part(x, 4, 2 * side[0] + side[1]).astype(F32)
        for y in got:
            x = x + y.astype(F32)
        return x.astype(BF16)

    def rest_of(xs):
        for b in range(2, bits - 1):
            xs = meet(xs, b, leave(xs, b))
        return xs

    def unfold(x, other, *shares):
        shape = (pieces // 2, -1, x.shape[1])
        low = jnp.where(side[0] == 0, x, other).reshape(shape)
        high = jnp.where(side[0] == 0, other, x).reshape(shape)
        at, out = 0, []
        for share in shares:
            parts = [y[:, at : at + share].reshape(-1, x.shape[1]) for y in (low, high)]
            out.append(jnp.concatenate(parts).astype(F32))
            at += share
        return out

    def spread(xs, late, *shares):
        for b in reversed(range(1, bits - 1)):
            got = yield along(jnp.concatenate(xs), b)
            xs = [join(x, y, side[b]) for x, y in zip(xs, cut(got, xs))]
        wire = along(jnp.concatenate(xs), 0)
        for _ in range(late):
            yield []
        got = yield wire
        return [unfold(x, y, *s) for x, y, s in zip(xs, cut(got, xs), shares)]

    wq, wo, wr = ([x, core(x), cross(x)] for x in (w_qkv, w_out, w_return))

    me = lax.axis_index("head")
    halves = doc_ids.shape[1] // count
    where = jnp.stack([me // halves, me % halves])
    near = open_layer(
        where,
        doc_ids, pad_mask, tokens, norm1_gain, norm1_shift, wq[:2], w_hidden, hidden_bias
    )
    n1, cols, doc_row = near["n1"], near["cols"], near["doc_row"]
    wh = [near["wh"], core(near["wh"]), cross(near["wh"])]
    wq.append(core(tie(wq[2], n1)))
    come_near = core(near["last"])
    far = attend(n1, wq[2:], cols, tie(doc_row, wo[2]))
    come_far, across = gate(far["last"], wo[2])
    come = [come_near, core(come_far)]
    wo.append(core(across))
    mid = mix_feed(
        pieces,
        tokens,
        out_grad,
        [near, far],
        come,
        wo,
        cols,
        norm2_gain,
        norm2_shift,
        wh[:2],
        wr[:2],
    )
    wh.append(core(tie(wh[2], mid["n2"])))
    wr.append(core(tie(wr[2], mid["n2"])))
    down1, up1 = tie((mid["down1"], mid["up1"]), wh[3], wr[3])
    down1, up1 = core(down1), core(up1)
    end = feed(pieces, mid["n2"], out_grad, wh[2:], wr[2:], mid["dn2"])

    down3, up3, down1, up1 = gate(end["down1"], end["up1"], down1, up1)
    down3, up3 = core(down3), core(up3)
    down0, up0 = add(mid["down0"], down1), add(mid["up0"], up1)
    down2, up2 = add(end["down0"], down3), add(end["up0"], up3)

    ups, down_wire = [up0, up2], cross(down2)
    ups_wire = leave(ups, 0)
    back = unmix(
        end["dn2"],
        mid["residual"],
        out_grad,
        mid["mixed"],
        mid["inv"],
        wo,
        [near["q"], far["q"]],
        cols,
        tie(norm2_gain, down3, up3),
    )
    gone = core(back["gone"])
    acts = [mid["act"], end["act"]]
    output = finish(mid["residual"], acts, wr, tie(return_bias, back["small"]))
    gone, down_wire, ups_wire, output = gate(gone, down_wire, ups_wire, output)
    down, ups = add(down0, down_wire), meet(ups, 0, ups_wire)
    down_wires, up_wire = leave_quad(down), cross(ups[1])
    args = cols, tie(doc_row, output), n1, back["gwo"]
    side_b = attend_back(pieces, 2, back["dw"], gone, far, come[1], *args)
    grad3, up_wire, *down_wires = gate(side_b["grad1"], up_wire, *down_wires)
    grad3 = core(grad3)
    (down,) = rest_of([meet_quad(down, down_wires)])
    up = [add(ups[0], up_wire)]
    down_wire, up_wire = along(down, bits - 1), leave(up, 1)
    grad2 = add(side_b["grad0"], grad3)
    grad_wire = cross(grad2)
    args = cols, tie(doc_row, grad3), n1, back["gwo"]
    side_a = attend_back(pieces, 0, back["dw"], gone, near, come[0], *args)
    grad1, down_wire, up_wire, grad_wire = gate(
        side_a["grad1"], down_wire, up_wire, grad_wire
    )
    grad1 = core(grad1)
    down, (up,) = add(down, down_wire), rest_of(meet(up, 1, up_wire))
    up_wire = along(up, bits - 1)
    spread_down = spread([down], 1, (width // pieces,))
    down_wire = next(spread_down)
    grad = [add(add(side_a["grad0"], grad1), grad_wire)]
    grad_wire = leave(grad, 0)
    last = input_back(
        tokens,
        back["rgrad"],
        [side_a["pgrads"], side_b["pgrads"]],
        tie(norm1_gain, grad1),
        wq,
        back["small"],
    )
    small, down_wire, up_wire, grad_wire = gate(last["small"], down_wire, up_wire, grad_wire)
    up, grad = add(up, up_wire), meet(grad, 0, grad_wire)

    def finish_grad(xs):
        for b in range(1, bits - 1):
            got = yield leave(xs, b)
            xs = meet(xs, b, got)
        got = yield along(xs[0], bits - 1)
        return (yield from spread([add(xs[0], got)], 0, (3 * width // pieces, width // pieces)))

    def finish_small(x):
        one, two, three = yield [swap(x, "head", head, i) for i in (1, 2, 3)]
        x = (x + one) + (two + three)
        for b in range(bits):
            got = yield along(x, b)
            x = x + got
        return x

    def go_on(chain, got):
        try:
            while True:
                got = yield chain.send(got)
        except StopIteration as stop:
            return stop.value

    (grads,), (downs,), (ups,), small = lockstep(
        finish_grad(grad),
        go_on(spread_down, down_wire),
        spread([up], 1, (width // pieces, 16)),
        finish_small(small),
    )
    g_qkv, g_out = grads
    (down,), (up, bias_grad) = downs, ups
    g_out = g_out.reshape(width // PAIR, PAIR, PAIR)
    g_out = jnp.concatenate([g_out[i] for i in range(width // PAIR)], axis=1)
    return (
        output,
        last["out"],
        small[0],
        small[1],
        g_qkv.reshape(3, width, PAIR),
        g_out,
        small[2],
        small[3],
        up,
        bias_grad[0],
        down,
        small[4],
    )


def solution(mesh):
    return jax.shard_map(
        functools.partial(body, mesh.shape["dp"], mesh.shape["head"]),
        mesh=mesh,
        in_specs=(
            P(("dp", "head"), None),
            P("dp", None),
            P("dp", None),
            P(),
            P(),
            P(None, None, "head"),
            P("head", None),
            P(),
            P(),
            P(None, "head"),
            P("head"),
            P("head", None),
            P(),
            P(("dp", "head"), None),
        ),
        out_specs=(
            P(("dp", "head"), None),
            P(("dp", "head"), None),
            P(),
            P(),
            P(None, None, "head"),
            P("head", None),
            P(),
            P(),
            P(None, "head"),
            P("head"),
            P("head", None),
            P(),
        ),
        check_vma=False,
    )
```

```python
import functools

import jax
import jax.numpy as jnp
from jax import lax
from jax.experimental import pallas as pl
from jax.experimental.pallas import tpu as pltpu
from jax.sharding import PartitionSpec as P

HEAD_DIM = 64
PAIR = 2 * HEAD_DIM
WIDE = 2 * PAIR
CHUNK = 256
LANES = 128
EPSILON = 1e-05
BELOW_ONE = 1.0 - 2.0**-8
F32 = jnp.float32
BF16 = jnp.bfloat16
VMEM_BYTES = 58 * 1024 * 1024

DOC, LIVE, READ_HALF, READ_CHUNK, IN_LAST, CARRIED, FIRST_HALF = range(7)


def nn(a, b):
    return lax.dot_general(a, b, (((1,), (0,)), ((), ())), preferred_element_type=F32)


def nt(a, b):
    return lax.dot_general(a, b, (((1,), (1,)), ((), ())), preferred_element_type=F32)


def tn(a, b):
    return lax.dot_general(a, b, (((0,), (0,)), ((), ())), preferred_element_type=F32)


def normalise(x):
    centre = x - jnp.mean(x, axis=-1, keepdims=True)
    rstd = lax.rsqrt(jnp.mean(centre * centre, axis=-1, keepdims=True) + EPSILON)
    return centre * rstd, rstd


def norm_back(grad, xhat, rstd, gain):
    scaled = grad * gain
    mean_one = jnp.mean(scaled, axis=-1, keepdims=True)
    mean_two = jnp.mean(scaled * xhat, axis=-1, keepdims=True)
    return rstd * (scaled - mean_one - xhat * mean_two)


def line(ref):
    return ref[...].astype(F32).reshape(1, ref.shape[0])


def eight(x):
    return jnp.sum(x.reshape(x.shape[0] // 8, 8, x.shape[1]), axis=0)


def head_lanes(shape):
    return lax.broadcasted_iota(jnp.int32, shape, len(shape) - 1) % PAIR < HEAD_DIM


def pair_mask(width):
    rows = lax.broadcasted_iota(jnp.int32, (PAIR, width), 0) < HEAD_DIM
    return rows == head_lanes((PAIR, width))


def allowed_mask(doc_col, doc_row):
    t = lax.broadcasted_iota(jnp.int32, (CHUNK, CHUNK), 0)
    s = lax.broadcasted_iota(jnp.int32, (CHUNK, CHUNK), 1)
    return (doc_col == doc_row) & (s <= t)


def feature(x):
    return jnp.where(x > 0, x + 1.0, jnp.exp(jnp.minimum(x, 0.0)))


def chunk_rows(c):
    return slice(c * CHUNK, (c + 1) * CHUNK)


def column(cols, which):
    return cols[:, which : which + 1]


def stack(x, masks):
    return jnp.concatenate([jnp.where(mask, x, jnp.zeros_like(x)) for mask in masks], axis=0)


class Rows:
    def __init__(self, array, first, columns=None):
        self.array = array
        self.columns = columns or slice(0, array.shape[-1])
        self.shape = array.shape[:-1] + (self.columns.stop - self.columns.start,)
        rows = self.shape[-2]
        rest = slice(CHUNK, rows) if first == 0 else slice(0, rows - CHUNK)
        self.first, self.parts = first, [chunk_rows(first), rest]

    def index(self, rows, columns):
        return (slice(None),) * (len(self.shape) - 2) + (rows, columns)


class Staged:
    def __init__(self, specs, late, ins, outs, scratch, in_sem, out_sem):
        self.specs, self.ins, self.outs, self.scratch = specs, ins, outs, scratch
        self.out_sem, self.sent = out_sem, []
        self.pending = {}
        begin = list(ins)[: len(ins) - late]
        for turn, names in enumerate((begin, begin, list(ins)[len(ins) - late :])):
            for name in names:
                spec, (src, dst) = specs[name], ins[name]
                if isinstance(spec, Rows):
                    rows = spec.parts[turn]
                    src = src.at[spec.index(rows, spec.columns)]
                    dst = dst.at[spec.index(rows, slice(None))]
                elif turn == 1:
                    continue
                copy = pltpu.make_async_copy(src, dst, in_sem.at[len(self.pending)])
                copy.start()
                self.pending[name, turn % 2] = copy

    def __getitem__(self, name):
        for key in [key for key in self.pending if key[0] == name]:
            self.pending.pop(key).wait()
        return self.ins[name][1] if name in self.ins else self.scratch[name]

    def rows(self, name, c):
        spec = self.specs[name]
        if not isinstance(spec, Rows):
            return self[name][chunk_rows(c), :]
        key = (name, int(c != spec.first))
        if key in self.pending:
            self.pending.pop(key).wait()
        return self.ins[name][1][spec.index(chunk_rows(c), slice(None))]

    def out(self, name):
        return self.outs[name][1]

    def send(self, name, *index):
        dst, src = self.outs[name]
        if index:
            dst, src = dst.at[index], src.at[index]
        copy = pltpu.make_async_copy(src, dst, self.out_sem.at[len(self.sent)])
        copy.start()
        self.sent.append(copy)

    def finish(self):
        for copy in list(self.pending.values()) + self.sent:
            copy.wait()


def staged(name, body, ins, outs, scratch, flops, sends, late=0):
    in_names, out_names, scratch_names = list(ins), list(outs), list(scratch)
    arrays, in_specs, own = [], [], []
    for value in ins.values():
        value = value.array if isinstance(value, Rows) else value
        arrays.append(value[0] if isinstance(value, tuple) else value)
        in_specs.append(pl.BlockSpec(memory_space=pl.ANY))
        if not isinstance(value, tuple):
            own.append(pltpu.VMEM(ins[in_names[len(arrays) - 1]].shape, value.dtype))

    def kernel(*refs):
        refs = list(refs)
        take = lambda n: [refs.pop(0) for _ in range(n)]
        src, dst = take(len(in_names)), take(len(out_names))
        own_refs, out_refs = take(len(own)), take(len(out_names))
        held = dict(zip(scratch_names, take(len(scratch_names))))
        in_sem, out_sem = refs
        ends = {}
        for key, ref in zip(in_names, src):
            value = ins[key]
            if not isinstance(value, tuple):
                ends[key] = (ref, own_refs.pop(0))
            else:
                ends[key] = (ref.at[value[3:]] if value[3:] else ref, held[value[1]].at[value[2]])
        stage = Staged(ins, late, ends, dict(zip(out_names, zip(dst, out_refs))), held, in_sem, out_sem)
        body(stage)
        stage.finish()

    shapes = list(outs.values())
    copies = sum(2 if isinstance(x, Rows) else 1 for x in ins.values())
    out = pl.pallas_call(
        kernel,
        in_specs=in_specs,
        out_specs=[pl.BlockSpec(memory_space=pl.ANY)] * len(out_names),
        out_shape=[jax.ShapeDtypeStruct(*s) for s in shapes],
        scratch_shapes=own
        + [pltpu.VMEM(*s) for s in shapes]
        + [pltpu.VMEM(*s) for s in scratch.values()]
        + [pltpu.SemaphoreType.DMA((copies,)), pltpu.SemaphoreType.DMA((sends,))],
        compiler_params=pltpu.CompilerParams(vmem_limit_bytes=VMEM_BYTES),
        cost_estimate=pl.CostEstimate(flops=flops, bytes_accessed=4 << 20, transcendentals=0),
        name=name,
    )(*arrays)
    return dict(zip(out_names, out))


def attend_chunk(st, blocks, c, n1, cols, doc_row):
    w, state, every = st["w"], st["state"], range(blocks)
    rows = chunk_rows(c)
    live, reads = column(cols, LIVE), column(cols, READ_CHUNK)
    in_last = column(cols, IN_LAST).astype(BF16)
    carried = cols[0:1, CARRIED : CARRIED + 1]
    mask = allowed_mask(column(cols, DOC), doc_row[:, rows])
    mask = jnp.concatenate([mask, mask], axis=0)
    q_all = feature(nn(n1, w[0])).astype(BF16)
    k_all = (feature(nn(n1, w[1])) * live).astype(BF16)
    v_all = nn(n1, w[2]).astype(BF16)
    here = head_lanes((CHUNK, WIDE))
    own = [here[:, :PAIR], jnp.logical_not(here[:, :PAIR])]
    block_diagonal = pair_mask(WIDE)
    ones = jnp.ones((CHUNK, PAIR), BF16)
    part = lambda x, b: x[:, b * PAIR : (b + 1) * PAIR]
    q, k, v = ([part(x, b) for b in every] for x in (q_all, k_all, v_all))
    for b in every:
        st.out("q")[b, rows], st.out("k")[b, rows], st.out("v")[b, rows] = q[b], k[b], v[b]
    scores = [nt(stack(q[b], own), k[b]) for b in every]
    wide = [jnp.concatenate([v[b], ones], axis=1) for b in every]
    grown = [tn(k[b] * in_last, wide[b]) for b in every]
    scores = [jnp.where(mask, scores[b], 0.0).astype(BF16) for b in every]
    both = [nn(scores[b], wide[b]) for b in every]
    total = [jnp.where(here, both[b][:CHUNK], both[b][CHUNK:]) for b in every]
    for b in every:
        if c > 0:
            low = state[b].astype(BF16)
            st.out("held")[c, b] = low
            total[b] = total[b] + reads * nn(q[b], low)
        else:
            st.out("held")[c, b] = jnp.zeros((PAIR, WIDE), BF16)
        st.out("num")[b, rows], st.out("tot")[b, rows] = total[b][:, :PAIR], total[b][:, PAIR:]
        more = jnp.where(block_diagonal, grown[b], 0.0)
        state[b] = more if c == 0 else carried * state[b] + more
    for name in ("q", "k", "v", "num", "tot"):
        st.send(name, slice(None), rows)


def attend_finish(st, blocks):
    for b in range(blocks):
        st.out("last")[b ^ 1] = st["state"][b].astype(BF16)
    st.send("last")
    st.send("held")


def attend_outs(tokens, blocks):
    part = (blocks, tokens, PAIR)
    return dict(
        q=(part, BF16),
        k=(part, BF16),
        v=(part, BF16),
        num=(part, F32),
        tot=(part, F32),
        held=((tokens // CHUNK, blocks, PAIR, WIDE), BF16),
        last=((blocks, PAIR, WIDE), BF16),
    )


def attend_scratch(width, blocks):
    return dict(w=((3, width, blocks * PAIR), BF16), state=((blocks, PAIR, WIDE), F32))


def attend_weights(w):
    everything = slice(None)
    return {
        f"w{b}": (x, "w", (everything, everything, slice(b * PAIR, (b + 1) * PAIR)))
        for b, x in enumerate(w)
    }


def attend_flops(tokens, width, blocks):
    return 2 * tokens * blocks * PAIR * (3 * width + 4 * CHUNK)


def make_flags(doc_ids, pad_mask, count):
    halves = doc_ids.shape[1] // count
    me = lax.axis_index("head")
    row, place = lax.div(me, halves), lax.rem(me, halves)

    def here(x):
        whole = x[0:1, :]
        for r in range(1, x.shape[0]):
            whole = jnp.where(row == r, x[r : r + 1, :], whole)
        part = whole[:, :count]
        for i in range(1, x.shape[1] // count):
            part = jnp.where(place == i, whole[:, i * count : (i + 1) * count], part)
        return whole, part

    whole, docs = here(doc_ids)
    _, live = here(pad_mask)
    edge = whole[:, count - 1 : count]
    second = jnp.where(place > 0, 1.0, 0.0)
    as_float = lambda x: jnp.where(x, 1.0, 0.0)
    reads, in_last, carried = [], [], []
    before = None
    for c in range(count // CHUNK):
        part = docs[:, chunk_rows(c)]
        end = part[:, CHUNK - 1 : CHUNK]
        in_last.append(as_float(part == end))
        if before is None:
            reads.append(jnp.zeros((1, CHUNK), F32))
            carried.append(jnp.zeros((1, CHUNK), F32))
        else:
            reads.append(as_float(part == before))
            carried.append(as_float(jnp.broadcast_to(end, part.shape) == before))
        before = end
    join = lambda x: jnp.concatenate(x, axis=1)
    doc_line = docs.astype(F32)
    lines = [
        doc_line,
        live.astype(F32),
        as_float(docs == edge) * second,
        join(reads),
        join(in_last),
        join(carried),
        jnp.broadcast_to(1.0 - second, (1, count)).astype(F32),
    ]
    lines.append(jnp.zeros((LANES - len(lines), count), F32))
    return jnp.concatenate(lines, axis=0).T, doc_line


def open_layer(doc_ids, pad_mask, tok, gain, shift, w, w_hidden, hidden_bias):
    tokens, width = tok.shape
    blocks, chunks, hidden = len(w), tokens // CHUNK, w_hidden.shape[1]

    def body(st):
        cols, doc_row = make_flags(st["doc_ids"], st["pad_mask"], tokens)
        st.out("cols")[...], st.out("doc_row")[...] = cols, doc_row
        st.send("cols")
        st.send("doc_row")
        cols, doc_row, n1 = st.out("cols"), st.out("doc_row"), st.out("n1")
        gain, shift = line(st["gain"]), line(st["shift"])
        for c in range(chunks):
            xhat, _ = normalise(st.rows("tok", c).astype(F32))
            n1[chunk_rows(c), :] = (xhat * gain + shift).astype(BF16)
        st.send("n1")
        for b in range(blocks):
            st[f"w{b}"]
        for c in range(chunks):
            attend_chunk(st, blocks, c, n1[chunk_rows(c), :], cols[chunk_rows(c), :], doc_row)
        attend_finish(st, blocks)
        st["wh"][width:, :] = jnp.broadcast_to(line(st["bias"]).astype(BF16), (16, hidden))
        st["w_hidden"]
        st.out("wh")[...] = st["wh"][...]
        st.send("wh")

    ins = dict(doc_ids=doc_ids, pad_mask=pad_mask, tok=Rows(tok, 0))
    ins.update(gain=gain, shift=shift, **attend_weights(w), bias=hidden_bias)
    ins.update(w_hidden=(w_hidden, "wh", (slice(0, width),)))
    outs = dict(
        cols=((tokens, LANES), F32),
        doc_row=((1, tokens), F32),
        n1=((tokens, width), BF16),
        wh=((width + 16, hidden), BF16),
    )
    outs.update(attend_outs(tokens, blocks))
    scratch = attend_scratch(width, blocks)
    scratch["wh"] = ((width + 16, hidden), BF16)
    flops = attend_flops(tokens, width, blocks)
    return staged("open", body, ins, outs, scratch, flops, 5 * chunks + 6, 1)


def attend(n1, w, cols, doc_row):
    tokens, width = n1.shape
    blocks, chunks = len(w), tokens // CHUNK

    def body(st):
        doc_row = st["doc_row"]
        for b in range(blocks):
            st[f"w{b}"]
        for c in range(chunks):
            attend_chunk(st, blocks, c, st.rows("n1", c), st.rows("cols", c), doc_row)
        attend_finish(st, blocks)

    ins = dict(doc_row=doc_row, **attend_weights(w))
    ins.update(n1=Rows(n1, 0), cols=Rows(cols, 0))
    flops = attend_flops(tokens, width, blocks)
    return staged(
        "attend",
        body,
        ins,
        attend_outs(tokens, blocks),
        attend_scratch(width, blocks),
        flops,
        5 * chunks + 2,
    )


def gelu_pair(x):
    cdf = 0.5 + 0.5 * lax.erf(x * 0.7071067811865476)
    density = 0.3989422804014327 * jnp.exp(-0.5 * x * x)
    return x * cdf, cdf + x * density


def mix_chunk(st, groups, c):
    cols, w, rows = st.rows("cols", c), st["wo"], chunk_rows(c)
    live, reads = column(cols, LIVE), column(cols, READ_HALF)
    q, num, tot = ([st.rows(f"{x}{g}", c) for g in range(groups)] for x in ("q", "num", "tot"))
    mixed, inv_out = st.out("mixed"), st.out("inv")
    for b in range(2 * groups):
        g, i = divmod(b, 2)
        lanes = slice(b * PAIR, (b + 1) * PAIR)
        far = reads * nn(q[g][i], st[f"come{g}"][i])
        inv = 1.0 / jnp.maximum(tot[g][i] + far[:, PAIR:], 1.0)
        inv_out[rows, lanes] = jnp.where(inv < 1.0, jnp.minimum(inv, BELOW_ONE), 1.0).astype(BF16)
        value = (num[g][i] + far[:, :PAIR]) * inv * live
        mixed[rows, lanes] = value.astype(BF16)
    residual = st.rows("tok", c).astype(F32) + nn(mixed[rows, :], w[...])
    st.out("residual")[rows, :] = residual
    xhat, _ = normalise(residual)
    n2 = (xhat * line(st["gain"]) + line(st["shift"])).astype(BF16)
    st.out("n2")[rows, :] = n2
    for name in ("mixed", "inv", "residual", "n2"):
        st.send(name, rows)


def feed_chunk(st, c, n2, bias, resume):
    rows = chunk_rows(c)
    wh, wr = st["wh"].at[: n2.shape[1]], st["wr"]
    value, slope = gelu_pair(nn(n2, wh[...]) + bias)
    st.out("act")[rows, :] = value.astype(BF16)
    st.send("act", rows)
    grad = nt(st.rows("dy", c), wr[...]) * slope
    low = grad.astype(BF16)
    st["hg"][rows, :] = low
    back = nt(low, wh[...])
    st.out("dn2")[rows, :] = back + st.rows("dn2_in", c) if resume else back
    st.send("dn2", rows)
    return eight(grad)


def feed_grads(st, blocks, pieces, n2, bias_grad):
    width, hidden = n2.shape[1], bias_grad.shape[1] // blocks
    bias_grad = jnp.sum(bias_grad, axis=0, keepdims=True).astype(BF16)
    for b in range(blocks):
        part = slice(b * hidden, (b + 1) * hidden)
        down, up = st.out(f"down{b}"), st.out(f"up{b}")
        down[...] = tn(st.out("act")[:, part], st["dy"][...]).astype(BF16)
        st.send(f"down{b}")
        grad = tn(n2[...], st["hg"][:, part]).astype(BF16)
        rows, step = width // pieces, up.shape[0] // pieces
        for i in range(pieces):
            up[i * step : i * step + rows, :] = grad[i * rows : (i + 1) * rows, :]
            tail = jnp.broadcast_to(bias_grad[:, part], (step - rows, hidden))
            up[i * step + rows : (i + 1) * step, :] = tail
        st.send(f"up{b}")


def feed_parts(tokens, width, pieces, wh, wr):
    blocks, hidden = len(wr), wr[0].shape[0]
    everything = slice(None)
    ins = {}
    for b in range(blocks):
        part = slice(b * hidden, (b + 1) * hidden)
        ins[f"wh{b}"] = (wh[b], "wh", (everything, part))
        ins[f"wr{b}"] = (wr[b], "wr", (part, everything))
    outs = dict(act=((tokens, blocks * hidden), BF16), dn2=((tokens, width), F32))
    for b in range(blocks):
        outs[f"down{b}"] = ((hidden, width), BF16)
        outs[f"up{b}"] = ((width + 16 * pieces, hidden), BF16)
    scratch = dict(
        wh=((width + 16, blocks * hidden), BF16),
        wr=((blocks * hidden, width), BF16),
        hg=((tokens, blocks * hidden), BF16),
    )
    return ins, outs, scratch, 10 * tokens * width * hidden * blocks


def feed_start(st, blocks, width):
    for b in range(blocks):
        st[f"wh{b}"], st[f"wr{b}"]
    return st["wh"][width : width + 1, :].astype(F32)


def mix_feed(pieces, tok, dy, parts, come, wo, cols, gain, shift, wh, wr):
    tokens, width = tok.shape
    blocks, groups, chunks = len(wh), len(parts), tokens // CHUNK

    def body(st):
        for b in range(2 * groups):
            st[f"wo{b}"]
        for c in range(chunks):
            mix_chunk(st, groups, c)
        n2 = st.out("n2")
        bias = feed_start(st, blocks, width)
        bias_grad = 0.0
        for c in range(chunks):
            bias_grad = bias_grad + feed_chunk(st, c, n2[chunk_rows(c), :], bias, False)
        feed_grads(st, blocks, pieces, n2, bias_grad)

    ins = dict(cols=Rows(cols, 0), tok=Rows(tok, 0), gain=gain, shift=shift)
    for g, part in enumerate(parts):
        ins.update({f"{x}{g}": Rows(part[x], 0) for x in ("q", "num", "tot")})
        ins[f"come{g}"] = come[g]
    for b, x in enumerate(wo):
        ins[f"wo{b}"] = (x, "wo", (slice(b * PAIR, (b + 1) * PAIR),))
    more, outs, scratch, flops = feed_parts(tokens, width, pieces, wh, wr)
    ins.update(dy=dy, **more)
    outs.update(
        mixed=((tokens, width), BF16),
        inv=((tokens, width), BF16),
        residual=((tokens, width), F32),
        n2=((tokens, width), BF16),
    )
    scratch["wo"] = ((width, width), BF16)
    late = 1 + len(more)
    return staged("mix_feed", body, ins, outs, scratch, 0, 6 * chunks + 2 * blocks, late)


def feed(pieces, n2, dy, wh, wr, dn2):
    tokens, width = n2.shape
    blocks, chunks = len(wh), tokens // CHUNK

    def body(st):
        bias = feed_start(st, blocks, width)
        bias_grad = 0.0
        for c in range(chunks):
            bias_grad = bias_grad + feed_chunk(st, c, st.rows("n2", c), bias, True)
        feed_grads(st, blocks, pieces, st["n2"], bias_grad)

    ins = dict(n2=n2)
    more, outs, scratch, flops = feed_parts(tokens, width, pieces, wh, wr)
    ins.update(more)
    ins.update(dy=dy, dn2_in=dn2)
    return staged("feed", body, ins, outs, scratch, flops, 2 * chunks + 2 * blocks)


def unmix_chunk(st, blocks, c):
    cols, rows = st.rows("cols", c), chunk_rows(c)
    live, reads = column(cols, LIVE), column(cols, READ_HALF).astype(BF16)
    xhat, rstd = normalise(st.rows("residual", c))
    grad = st.rows("dn2", c)
    wide = st.rows("dy", c).astype(F32)
    rgrad = wide + norm_back(grad, xhat, rstd, line(st["gain"]))
    low = rgrad.astype(BF16)
    st.out("rgrad")[rows, :] = low
    mgrad = nt(low, st["wo"][...]) * live
    sums = pair_mask(PAIR).astype(BF16)
    sums = jnp.concatenate([sums, sums], axis=0)
    inv, mixed = st.rows("inv", c).astype(F32), st.rows("mixed", c).astype(F32)
    q = [st.rows(f"q{g}", c) for g in range(blocks // 2)]
    for b in range(blocks):
        lanes = slice(b * PAIR, (b + 1) * PAIR)
        one, scale = mgrad[:, lanes], inv[:, lanes]
        dw = (one * scale).astype(BF16)
        terms = one * mixed[:, lanes]
        high = terms.astype(BF16)
        rest = (terms - high.astype(F32)).astype(BF16)
        total = nn(jnp.concatenate([high, rest], axis=1), sums)
        tg = jnp.where(scale < 1.0, -total * scale, 0.0).astype(BF16)
        st.out("dw")[rows, b * WIDE : b * WIDE + PAIR] = dw
        st.out("dw")[rows, b * WIDE + PAIR : (b + 1) * WIDE] = tg
        st["reading"][rows, lanes] = q[b // 2][b % 2] * reads
    st.send("rgrad", rows)
    st.send("dw", rows)
    return eight(grad * xhat), eight(grad), eight(wide)


def unmix(dn2, residual, dy, mixed, inv, wo, q, cols, gain):
    tokens, width = dy.shape
    blocks, chunks = len(wo), tokens // CHUNK

    def body(st):
        for b in range(blocks):
            st[f"wo{b}"]
        small = [0.0, 0.0, 0.0]
        for c in range(chunks):
            small = [a + b for a, b in zip(small, unmix_chunk(st, blocks, c))]
        small = [jnp.sum(x, axis=0, keepdims=True) for x in small]
        st.out("small")[...] = jnp.concatenate(small + [jnp.zeros((5, width), F32)], axis=0)
        st.send("small")
        block_diagonal = pair_mask(WIDE)
        for b in range(blocks):
            lanes, wide = slice(b * PAIR, (b + 1) * PAIR), slice(b * WIDE, (b + 1) * WIDE)
            grown = tn(st["reading"][:, lanes], st.out("dw")[:, wide])
            st.out("gone")[b ^ 1] = jnp.where(block_diagonal, grown, 0.0).astype(BF16)
        st.send("gone")
        st.out("gwo")[...] = tn(st["mixed"][...], st.out("rgrad")[...]).astype(BF16)
        st.send("gwo")

    ins = dict(gain=gain, cols=Rows(cols, 0))
    ins.update(residual=Rows(residual, 0), dn2=Rows(dn2, 0), dy=Rows(dy, 0))
    for b, x in enumerate(wo):
        ins[f"wo{b}"] = (x, "wo", (slice(b * PAIR, (b + 1) * PAIR),))
    ins.update(inv=Rows(inv, 0), mixed=Rows(mixed, 0))
    ins.update({f"q{g}": Rows(x, 0) for g, x in enumerate(q)})
    outs = dict(
        rgrad=((tokens, width), BF16),
        dw=((tokens, 2 * width), BF16),
        gone=((blocks, PAIR, WIDE), BF16),
        gwo=((width, width), BF16),
        small=((8, width), F32),
    )
    scratch = dict(wo=((width, width), BF16), reading=((tokens, width), BF16))
    return staged(
        "unmix", body, ins, outs, scratch, 6 * tokens * width * width, 2 * chunks + 3
    )


def finish(residual, act, wr, bias):
    tokens, width = residual.shape

    def body(st):
        total = 0.0
        for i in range(len(wr)):
            total = total + nn(st[f"act{i}"][...], st[f"wr{i}"][...])
        total = total + st["residual"][...] + line(st["bias"])
        st.out("out")[...] = total.astype(BF16)
        st.send("out")

    ins, own, scratch = {}, [], {}
    for x in act:
        own += [(x, slice(i, i + wr[0].shape[0])) for i in range(0, x.shape[1], wr[0].shape[0])]
    for i, (x, columns) in enumerate(own):
        scratch[f"part{i}"] = ((tokens, wr[i].shape[0]), BF16)
        ins[f"act{i}"] = (x, f"part{i}", (slice(None),), slice(None), columns)
        ins[f"wr{i}"] = wr[i]
    ins.update(residual=residual, bias=bias)
    outs = dict(out=((tokens, width), BF16))
    flops = 2 * tokens * width * width * len(wr)
    return staged("finish", body, ins, outs, scratch, flops, 1)["out"]


def attend_back_chunk(st, blocks, c):
    cols, rows = st.rows("cols", c), chunk_rows(c)
    reads, reads_far = column(cols, READ_CHUNK), column(cols, READ_HALF)
    in_last = column(cols, IN_LAST)
    carried = cols[0:1, CARRIED : CARRIED + 1]
    mask = allowed_mask(column(cols, DOC), st["doc_row"][:, rows])
    here = head_lanes((CHUNK, PAIR))
    block_diagonal = pair_mask(WIDE)
    share = jnp.full((CHUNK, PAIR), 1.0 / HEAD_DIM, BF16)
    once = lax.broadcasted_iota(jnp.int32, (PAIR, WIDE), 1) < PAIR
    once = jnp.where(once, 1.0, 1.0 / HEAD_DIM).astype(BF16)
    out, state = st.out("pgrads"), st["state"]
    every = range(blocks)
    own = [here, jnp.logical_not(here)]
    mask2 = jnp.concatenate([mask, mask], axis=0)
    own_wide = [jnp.concatenate([o, o], axis=1) for o in own]
    pick = lambda x: jnp.where(here, x[:CHUNK], x[CHUNK:])
    q, k, v = ([st.rows(x, c)[b] for b in every] for x in ("q", "k", "v"))
    dw = st.rows("dw", c)
    dw = [dw[:, b * WIDE : (b + 1) * WIDE] for b in every]
    value_share = [jnp.concatenate([v[b], share], axis=1) for b in every]
    scores = [nt(stack(q[b], own), k[b]) for b in every]
    sgrad = [nt(stack(dw[b], own_wide), value_share[b]) for b in every]
    q_t = [q[b].T for b in every]
    dw_t = [dw[b][:, :PAIR].T for b in every]
    scores = [jnp.where(mask2, scores[b], 0.0).astype(BF16) for b in every]
    sgrad = [jnp.where(mask2, sgrad[b], 0.0).astype(BF16) for b in every]
    low = [state[b].astype(BF16) for b in every]
    if c > 0:
        states = [
            jnp.concatenate([st["come"][b] * once, st["held"][c, b] * once], axis=0) for b in every
        ]
        both = [nt(dw[b], states[b]) for b in every]
        dq = [reads_far * both[b][:, :PAIR] + reads * both[b][:, PAIR:] for b in every]
    else:
        dq = [reads_far * nt(dw[b], st["come"][b] * once) for b in every]
    dq = [dq[b] + pick(nn(sgrad[b], k[b])) for b in every]
    dk, dv = [], []
    for b in every:
        for out_t, left, right in ((dk, q_t[b], sgrad[b]), (dv, dw_t[b], scores[b])):
            both = []
            for h in range(2):
                feats = slice(h * HEAD_DIM, (h + 1) * HEAD_DIM)
                both.append(nn(left[feats], right[h * CHUNK : (h + 1) * CHUNK]))
            out_t.append(jnp.concatenate(both, axis=0).T)
    for b in every:
        dk_b = dk[b] + in_last * nt(value_share[b], low[b])
        dv_b = dv[b] + in_last * nn(k[b], low[b][:, :PAIR])
        at = 3 * b * PAIR
        dq_b = dq[b] * jnp.minimum(q[b].astype(F32), 1.0)
        dk_b = dk_b * jnp.minimum(k[b].astype(F32), 1.0)
        out[rows, at : at + PAIR] = dq_b.astype(BF16)
        out[rows, at + PAIR : at + 2 * PAIR] = dk_b.astype(BF16)
        out[rows, at + 2 * PAIR : at + 3 * PAIR] = dv_b.astype(BF16)
        if c > 0:
            grown = tn(q[b] * reads.astype(BF16), dw[b])
            state[b] = carried * state[b] + jnp.where(block_diagonal, grown, 0.0)
    st.send("pgrads", rows)


class PieceRows:
    def __init__(self, out, rows_one, rows_two, pieces):
        self.out, self.one, self.two = out, rows_one // pieces, rows_two // pieces

    def write(self, at, rows, share, offset):
        done, total = 0, rows.shape[0]
        while done < total:
            piece, inside = divmod(at + done, share)
            take = min(total - done, share - inside)
            start = piece * (self.one + self.two) + offset + inside
            self.out[start : start + take, :] = rows[done : done + take, :]
            done += take

    def first(self, at, rows):
        self.write(at, rows, self.one, 0)

    def second(self, at, rows):
        self.write(at, rows, self.two, self.one)


def attend_back(pieces, first, dw, gone, part, come, cols, doc_row, n1, gwo):
    tokens, width = n1.shape
    blocks, chunks = part["q"].shape[0], tokens // CHUNK

    def body(st):
        flag = st.rows("cols", chunks - 1)[0:1, FIRST_HALF : FIRST_HALF + 1]
        for b in range(blocks):
            st["state"][b] = st["gone"][first + b].astype(F32) * flag
        for c in reversed(range(chunks)):
            attend_back_chunk(st, blocks, c)
        for b in range(blocks):
            grad = tn(st["n1"][...], st.out("pgrads")[:, 3 * b * PAIR : 3 * (b + 1) * PAIR])
            grad = grad.astype(BF16)
            block = st["gwo"][b * PAIR : (b + 1) * PAIR, :]
            fill = PieceRows(st.out(f"grad{b}"), 3 * width, width, pieces)
            for p in range(3):
                fill.first(p * width, grad[:, p * PAIR : (p + 1) * PAIR])
            for j in range(width // PAIR):
                fill.second(j * PAIR, block[:, j * PAIR : (j + 1) * PAIR])
            st.send(f"grad{b}")

    ins = dict(doc_row=doc_row, gone=gone, come=come, held=part["held"])
    ins.update({x: Rows(part[x], chunks - 1) for x in ("q", "k", "v")})
    ins.update(cols=Rows(cols, chunks - 1))
    ins.update(dw=Rows(dw, chunks - 1, slice(first * WIDE, (first + blocks) * WIDE)), n1=n1)
    own = slice(first * PAIR, (first + blocks) * PAIR)
    ins.update(gwo=(gwo, "gwo", (slice(None),), own))
    outs = dict(pgrads=((tokens, 3 * blocks * PAIR), BF16))
    for b in range(blocks):
        outs[f"grad{b}"] = ((4 * width, PAIR), BF16)
    scratch = dict(state=((blocks, PAIR, WIDE), F32), gwo=((blocks * PAIR, width), BF16))
    flops = 2 * tokens * blocks * PAIR * (3 * width + 12 * CHUNK)
    return staged("attend_back", body, ins, outs, scratch, flops, chunks + blocks, 2)


def input_back(tok, rgrad, pgrads, gain, w, small):
    tokens, width = tok.shape
    blocks, chunks = len(w), tokens // CHUNK

    def body(st):
        for key in w_keys:
            st[key]
        gain = line(st["gain"])
        one = two = 0.0
        for c in range(chunks):
            rows = chunk_rows(c)
            both = jnp.concatenate([st.rows(f"pgrads{g}", c) for g in range(len(pgrads))], axis=1)
            grad = nt(both, st["w"][...])
            xhat, rstd = normalise(st.rows("tok", c).astype(F32))
            st.out("out")[rows, :] = st.rows("rgrad", c).astype(F32) + norm_back(grad, xhat, rstd, gain)
            st.send("out", rows)
            one, two = one + eight(grad * xhat), two + eight(grad)
        small = [jnp.sum(x, axis=0, keepdims=True) for x in (one, two)]
        st.out("small")[...] = jnp.concatenate(small + [st["small_in"][:6, :]], axis=0)
        st.send("small")

    ins, w_keys = {}, []
    for b in range(blocks):
        for p in range(3):
            at = (3 * b + p) * PAIR
            w_keys.append(f"w{b}_{p}")
            ins[w_keys[-1]] = (w[b], "w", (slice(None), slice(at, at + PAIR)), p)
    ins.update({f"pgrads{g}": Rows(x, 0) for g, x in enumerate(pgrads)})
    ins.update(gain=gain, tok=Rows(tok, 0), rgrad=Rows(rgrad, 0), small_in=small)
    outs = dict(out=((tokens, width), F32), small=((8, width), F32))
    scratch = dict(w=((width, 3 * blocks * PAIR), BF16))
    return staged(
        "input_back", body, ins, outs, scratch, 6 * tokens * width * width, chunks + 1
    )


def swap(x, axis, size, bit):
    return lax.ppermute(x, axis, [(i, i ^ bit) for i in range(size)])


def tie(x, *others):
    return lax.optimization_barrier((x, *others))[0]


def gate(*xs):
    return lax.optimization_barrier(xs)


def add(a, b):
    return (a.astype(F32) + b.astype(F32)).astype(BF16)


def cut(x, like):
    at, out = 0, []
    for y in like:
        out.append(x[at : at + y.shape[0]])
        at += y.shape[0]
    return out


def part(x, parts, which):
    rows = x.shape[0] // parts
    return lax.dynamic_slice_in_dim(x, which * rows, rows, 0)


def half(x, which):
    return part(x, 2, which)


def join(x, other, side):
    return jnp.where(side == 0, jnp.concatenate([x, other]), jnp.concatenate([other, x]))


def lockstep(*chains):
    results, sent = [None] * len(chains), {}
    for i, chain in enumerate(chains):
        sent[i] = next(chain)
    while sent:
        flat, tree = jax.tree.flatten(sent)
        sent = jax.tree.unflatten(tree, gate(*flat))
        for i in list(sent):
            try:
                sent[i] = chains[i].send(sent[i])
            except StopIteration as stop:
                results[i] = stop.value
                del sent[i]
    return results


def body(
    dp,
    head,
    tokens,
    doc_ids,
    pad_mask,
    norm1_gain,
    norm1_shift,
    w_qkv,
    w_out,
    norm2_gain,
    norm2_shift,
    w_hidden,
    hidden_bias,
    w_return,
    return_bias,
    out_grad,
):
    count, width = tokens.shape
    pieces = dp // 2
    core = lambda x: swap(x, "head", head, 1)
    cross = lambda x: swap(x, "head", head, 2)
    bits = dp.bit_length() - 1
    spot = lax.axis_index("dp")
    side = [(spot >> b) & 1 for b in range(bits)]
    along = lambda x, b: swap(x, "dp", dp, 1 << b)

    def leave(xs, b):
        return along(jnp.concatenate([half(x, 1 - side[b]) for x in xs]), b)

    def meet(xs, b, got):
        halves = [half(x, side[b]) for x in xs]
        return [add(x, y) for x, y in zip(halves, cut(got, halves))]

    def leave_quad(x):
        spot = lambda one, two: 2 * (side[0] ^ one) + (side[1] ^ two)
        return [
            swap(part(x, 4, spot(one, two)), "dp", dp, one + 2 * two)
            for one, two in ((1, 0), (1, 1), (0, 1))
        ]

    def meet_quad(x, got):
        x = part(x, 4, 2 * side[0] + side[1]).astype(F32)
        for y in got:
            x = x + y.astype(F32)
        return x.astype(BF16)

    def rest_of(xs):
        for b in range(2, bits - 1):
            xs = meet(xs, b, leave(xs, b))
        return xs

    def unfold(x, other, *shares):
        shape = (pieces // 2, -1, x.shape[1])
        low = jnp.where(side[0] == 0, x, other).reshape(shape)
        high = jnp.where(side[0] == 0, other, x).reshape(shape)
        at, out = 0, []
        for share in shares:
            parts = [y[:, at : at + share].reshape(-1, x.shape[1]) for y in (low, high)]
            out.append(jnp.concatenate(parts).astype(F32))
            at += share
        return out

    def spread(xs, late, *shares):
        for b in reversed(range(1, bits - 1)):
            got = yield along(jnp.concatenate(xs), b)
            xs = [join(x, y, side[b]) for x, y in zip(xs, cut(got, xs))]
        wire = along(jnp.concatenate(xs), 0)
        for _ in range(late):
            yield []
        got = yield wire
        return [unfold(x, y, *s) for x, y, s in zip(xs, cut(got, xs), shares)]

    wq, wo, wr = ([x, core(x), cross(x)] for x in (w_qkv, w_out, w_return))

    near = open_layer(
        doc_ids, pad_mask, tokens, norm1_gain, norm1_shift, wq[:2], w_hidden, hidden_bias
    )
    n1, cols, doc_row = near["n1"], near["cols"], near["doc_row"]
    wh = [near["wh"], core(near["wh"]), cross(near["wh"])]
    wq.append(core(tie(wq[2], n1)))
    come_near = core(near["last"])
    far = attend(n1, wq[2:], cols, tie(doc_row, wo[2]))
    come_far, across = gate(far["last"], wo[2])
    come = [come_near, core(come_far)]
    wo.append(core(across))
    mid = mix_feed(
        pieces,
        tokens,
        out_grad,
        [near, far],
        come,
        wo,
        cols,
        norm2_gain,
        norm2_shift,
        wh[:2],
        wr[:2],
    )
    wh.append(core(tie(wh[2], mid["n2"])))
    wr.append(core(tie(wr[2], mid["n2"])))
    down1, up1 = tie((mid["down1"], mid["up1"]), wh[3], wr[3])
    down1, up1 = core(down1), core(up1)
    end = feed(pieces, mid["n2"], out_grad, wh[2:], wr[2:], mid["dn2"])

    down3, up3, down1, up1 = gate(end["down1"], end["up1"], down1, up1)
    down3, up3 = core(down3), core(up3)
    down0, up0 = add(mid["down0"], down1), add(mid["up0"], up1)
    down2, up2 = add(end["down0"], down3), add(end["up0"], up3)

    ups, down_wire = [up0, up2], cross(down2)
    ups_wire = leave(ups, 0)
    back = unmix(
        end["dn2"],
        mid["residual"],
        out_grad,
        mid["mixed"],
        mid["inv"],
        wo,
        [near["q"], far["q"]],
        cols,
        tie(norm2_gain, down3, up3),
    )
    gone = core(back["gone"])
    acts = [mid["act"], end["act"]]
    output = finish(mid["residual"], acts, wr, tie(return_bias, back["small"]))
    gone, down_wire, ups_wire, output = gate(gone, down_wire, ups_wire, output)
    down, ups = add(down0, down_wire), meet(ups, 0, ups_wire)
    down_wires, up_wire = leave_quad(down), cross(ups[1])
    args = cols, tie(doc_row, output), n1, back["gwo"]
    side_b = attend_back(pieces, 2, back["dw"], gone, far, come[1], *args)
    grad3, up_wire, *down_wires = gate(side_b["grad1"], up_wire, *down_wires)
    grad3 = core(grad3)
    (down,) = rest_of([meet_quad(down, down_wires)])
    up = [add(ups[0], up_wire)]
    down_wire, up_wire = along(down, bits - 1), leave(up, 1)
    grad2 = add(side_b["grad0"], grad3)
    grad_wire = cross(grad2)
    args = cols, tie(doc_row, grad3), n1, back["gwo"]
    side_a = attend_back(pieces, 0, back["dw"], gone, near, come[0], *args)
    grad1, down_wire, up_wire, grad_wire = gate(
        side_a["grad1"], down_wire, up_wire, grad_wire
    )
    grad1 = core(grad1)
    down, (up,) = add(down, down_wire), rest_of(meet(up, 1, up_wire))
    up_wire = along(up, bits - 1)
    spread_down = spread([down], 1, (width // pieces,))
    down_wire = next(spread_down)
    grad = [add(add(side_a["grad0"], grad1), grad_wire)]
    grad_wire = leave(grad, 0)
    last = input_back(
        tokens,
        back["rgrad"],
        [side_a["pgrads"], side_b["pgrads"]],
        tie(norm1_gain, grad1),
        wq,
        back["small"],
    )
    small, down_wire, up_wire, grad_wire = gate(last["small"], down_wire, up_wire, grad_wire)
    up, grad = add(up, up_wire), meet(grad, 0, grad_wire)

    def finish_grad(xs):
        for b in range(1, bits - 1):
            got = yield leave(xs, b)
            xs = meet(xs, b, got)
        got = yield along(xs[0], bits - 1)
        return (yield from spread([add(xs[0], got)], 0, (3 * width // pieces, width // pieces)))

    def finish_small(x):
        one, two, three = yield [swap(x, "head", head, i) for i in (1, 2, 3)]
        x = (x + one) + (two + three)
        for b in range(bits):
            got = yield along(x, b)
            x = x + got
        return x

    def go_on(chain, got):
        try:
            while True:
                got = yield chain.send(got)
        except StopIteration as stop:
            return stop.value

    (grads,), (downs,), (ups,), small = lockstep(
        finish_grad(grad),
        go_on(spread_down, down_wire),
        spread([up], 1, (width // pieces, 16)),
        finish_small(small),
    )
    g_qkv, g_out = grads
    (down,), (up, bias_grad) = downs, ups
    g_out = g_out.reshape(width // PAIR, PAIR, PAIR)
    g_out = jnp.concatenate([g_out[i] for i in range(width // PAIR)], axis=1)
    return (
        output,
        last["out"],
        small[0],
        small[1],
        g_qkv.reshape(3, width, PAIR),
        g_out,
        small[2],
        small[3],
        up,
        bias_grad[0],
        down,
        small[4],
    )


def solution(mesh):
    return jax.shard_map(
        functools.partial(body, mesh.shape["dp"], mesh.shape["head"]),
        mesh=mesh,
        in_specs=(
            P(("dp", "head"), None),
            P("dp", None),
            P("dp", None),
            P(),
            P(),
            P(None, None, "head"),
            P("head", None),
            P(),
            P(),
            P(None, "head"),
            P("head"),
            P("head", None),
            P(),
            P(("dp", "head"), None),
        ),
        out_specs=(
            P(("dp", "head"), None),
            P(("dp", "head"), None),
            P(),
            P(),
            P(None, None, "head"),
            P("head", None),
            P(),
            P(),
            P(None, "head"),
            P("head"),
            P("head", None),
            P(),
        ),
        check_vma=False,
    )
```
